32 devices in a mesh: seq: 8 (over z, y), head: 4 (over x, core).
Axes of the slice: x: 2, y: 2, z: 4, core: 2. Of those that a mesh axis runs over, the one named last changes fastest.
Arguments:
- tokens: bfloat16 [2, 16384, 768], P(None, 'seq'), may hold values from -6 to 6
- doc_starts: int32 [2, 8], replicated, may hold values from 0 to 16383, as said below
- norm_gain: float32 [768], replicated, may hold values from 0.5 to 1.5
- gate_x_weight: bfloat16 [768, 2, 1536], P(None, None, 'head'), may hold values from -0.21875 to 0.21875
- bc_weight: bfloat16 [768, 256], replicated, may hold values from -0.21875 to 0.21875
- dt_weight: bfloat16 [768, 24], P(None, 'head'), may hold values from -0.21875 to 0.21875
- conv_x_weight: float32 [4, 1536], P(None, 'head'), may hold values from -3 to 3
- conv_x_bias: float32 [1536], P('head'), may hold values from -0.5 to 0.5
- conv_bc_weight: float32 [4, 256], replicated, may hold values from -3 to 3
- conv_bc_bias: float32 [256], replicated, may hold values from -0.5 to 0.5
- dt_bias: float32 [24], P('head'), may hold values from -6 to -4.5
- a_log: float32 [24], P('head'), may hold values from -8 to 3
- d_skip: float32 [24], P('head'), may hold values from 0.5 to 2
- gate_gain: float32 [1536], P('head'), may hold values from 0.5 to 1.5
- out_weight: bfloat16 [1536, 768], P('head'), may hold values from -0.15625 to 0.15625
- cotangent: bfloat16 [2, 16384, 768], P(None, 'seq'), may hold values from -6 to 6
Outputs:
- mixed_out: bfloat16 [2, 16384, 768], P(None, 'seq')
- token_grad: bfloat16 [2, 16384, 768], P(None, 'seq')
- grad_norm_gain: float32 [768], replicated
- grad_gate_x: float32 [768, 2, 1536], P(None, None, 'head')
- grad_bc: float32 [768, 256], P(None, 'head')
- grad_dt: float32 [768, 24], P(None, 'head')
- grad_conv_x: float32 [4, 1536], P(None, 'head')
- grad_conv_x_bias: float32 [1536], P('head')
- grad_conv_bc: float32 [4, 256], replicated
- grad_conv_bc_bias: float32 [256], replicated
- grad_dt_bias: float32 [24], P('head')
- grad_a_log: float32 [24], P('head')
- grad_d_skip: float32 [24], P('head')
- grad_gate_gain: float32 [1536], P('head')
- grad_out: float32 [1536, 768], P('head')
The draws below stay inside these ranges and needn't reach their ends.
Inputs may be any that keep to these rules, and one draw needn't show every extreme that they name: `doc_starts`: document start positions of each micro-batch, in no order and possibly repeated; an entry 0 starts nothing. In one micro-batch, drawn from the seed, every entry is 0, so that one document covers the whole sequence; another micro-batch has a start at 16383.
All inputs are finite; a program needn't handle non-finite values.
Results may differ from the reference program's by a relative error of at most 0.012.
The reference program's roundings to bfloat16 on the way count: a program that leaves them out, or rounds other values in their place, can miss the bound.
Values may be sent and summed in bfloat16 or wider, within the bound.
No kernel may reach another device: no remote copies, remote signals or barrier semaphores. Data moves between devices by JAX's collectives and lax.ppermute only.
A program may use at most 384 MiB of HBM per device.

```python
import math
import jax
import jax.numpy as jnp
from jax import lax

D = 768
HEADS = 24
HEAD_DIM = 64
STATE = 128
CONV = 4
GROUP = 256
MICRO = 2
NSTARTS = 8
DI = 1536
LENGTH = 16384


def draw_doc_starts(key, part):
    first_key, second_key = jax.random.split(jax.random.fold_in(key, 7))
    whole_doc = jax.random.randint(first_key, (), 0, MICRO)
    spots = jax.random.randint(second_key, (MICRO, NSTARTS), 1, LENGTH)
    rows = jnp.arange(MICRO)[:, None]
    columns = jnp.arange(NSTARTS)[None, :]
    spots = jnp.where((rows == (whole_doc + 1) % MICRO) & (columns == NSTARTS - 1), LENGTH - 1, spots)
    return jnp.where(rows == whole_doc, 0, spots).astype(jnp.int32)


def draw_a_log(key, part):
    first_key, second_key, third_key = jax.random.split(jax.random.fold_in(key, 11), 3)
    share = 0.5
    quick = jax.random.uniform(first_key, (HEADS,), jnp.float32) < share
    slow_mag = jnp.exp(jax.random.uniform(second_key, (HEADS,), jnp.float32, jnp.log(0.3), jnp.log(1.5))) * 100.0 / LENGTH
    quick_mag = jnp.exp(jax.random.uniform(third_key, (HEADS,), jnp.float32, jnp.log(3.0), jnp.log(8.0)))
    return jnp.log(jnp.where(quick, quick_mag, slow_mag)).astype(jnp.float32)


def steps_of(key, extent, cuts, low, largest):
    def one(axis_at, parts):
        steps = jax.random.uniform(jax.random.fold_in(jax.random.fold_in(key, 6), axis_at), (parts,), jnp.float32, low / len(cuts), largest / len(cuts))
        return jnp.repeat(jnp.exp(steps), extent[axis_at] // parts).reshape((-1,) + (1,) * (len(extent) - axis_at - 1))

    factor_of = one(*cuts[0])
    for cut in cuts[1:]:
        factor_of = factor_of * one(*cut)
    return factor_of


def gaussian(key, extent, width, limit, cuts=(), kind=jnp.bfloat16):
    values = jax.random.normal(key, extent, jnp.float32) * width
    if len(cuts) > 0:
        values = steps_of(key, extent, cuts, -0.22, 0.18) * values
    return jnp.clip(values, min=-limit, max=limit).astype(kind)


def setup_inputs(seed: int = 0) -> dict:
    keys = jax.random.split(jax.random.key(seed), 17)
    tokens = gaussian(keys[0], (MICRO, LENGTH, D), 1.0, 6.0, ((1, 8),))
    doc_starts = draw_doc_starts(jax.random.fold_in(keys[16], 71), 0)
    norm_gain = jnp.clip(1.0 + 0.1 * jax.random.normal(keys[2], (D,), jnp.float32), 0.5, 1.5)
    gate_x_weight = gaussian(keys[3], (D, 2, DI), D ** -0.5, 0.21875, ((2, 4),))
    bc_weight = gaussian(keys[4], (D, 2 * STATE), D ** -0.5, 0.21875)
    dt_weight = gaussian(keys[5], (D, HEADS), D ** -0.5, 0.21875, ((1, 4),))
    conv_x_weight = gaussian(keys[6], (CONV, DI), CONV ** -0.5, 3.0, ((1, 4),), jnp.float32)
    conv_x_bias = jnp.clip(jax.random.uniform(keys[7], (DI,), jnp.float32, -0.5, 0.5) * steps_of(keys[7], (DI,), ((0, 4),), -0.4, 0.0), -0.5, 0.5)
    conv_bc_weight = gaussian(keys[8], (CONV, 2 * STATE), CONV ** -0.5, 3.0, (), jnp.float32)
    conv_bc_bias = jnp.clip(jax.random.uniform(keys[9], (2 * STATE,), jnp.float32, -0.5, 0.5), -0.5, 0.5)
    dt_bias = jnp.clip(-6.0 + 1.5 * jax.random.uniform(keys[10], (HEADS,), jnp.float32) ** steps_of(keys[10], (HEADS,), ((0, 4),), -0.2, 0.2), -6.0, -4.5)
    a_log = draw_a_log(jax.random.fold_in(keys[16], 71), 0)
    d_skip = jnp.clip(jnp.exp(math.log(2.0) - 1.3862944 * jax.random.uniform(keys[12], (HEADS,), jnp.float32) ** steps_of(keys[12], (HEADS,), ((0, 4),), -0.2, 0.2)), 0.5, 2.0)
    gate_gain = jnp.clip(1.0 + 0.1 * jax.random.normal(keys[13], (DI,), jnp.float32), 0.5, 1.5)
    out_weight = gaussian(keys[14], (DI, D), DI ** -0.5, 0.15625, ((0, 4),))
    cotangent = gaussian(keys[15], (MICRO, LENGTH, D), 1.0, 6.0, ((1, 8),))
    return {"tokens": tokens, "doc_starts": doc_starts, "norm_gain": norm_gain, "gate_x_weight": gate_x_weight, "bc_weight": bc_weight, "dt_weight": dt_weight, "conv_x_weight": conv_x_weight, "conv_x_bias": conv_x_bias, "conv_bc_weight": conv_bc_weight, "conv_bc_bias": conv_bc_bias, "dt_bias": dt_bias, "a_log": a_log, "d_skip": d_skip, "gate_gain": gate_gain, "out_weight": out_weight, "cotangent": cotangent}


@jax.custom_vjp
def low(v):
    return lax.optimization_barrier(v.astype(jnp.bfloat16)).astype(jnp.float32)

@jax.custom_vjp
def low_back(v):
    return v

def low_keep(v):
    return (low(v), None)

def low_pass(kept, grad):
    return (grad,)

def back_keep(v):
    return (v, None)

def back_low(kept, grad):
    return (low(grad),)
low.defvjp(low_keep, low_pass)
low_back.defvjp(back_keep, back_low)
HIGHEST = lax.Precision.HIGHEST
EPSILON = 1e-05

def start_counts(doc_starts, places):
    hits = (doc_starts[None, :] >= 1) & (doc_starts[None, :] <= places[:, None])
    return lax.optimization_barrier(jnp.sum(hits.astype(jnp.int32), axis=1)).astype(jnp.int32)

def group_step(states, inputs_x, writes, reads, deltas, decay_rate, counts, before):
    running = jnp.cumsum(deltas * decay_rate[None, :], axis=0)
    positions = jnp.arange(counts.shape[0])
    allowed = (counts[:, None] == counts[None, :]) & (positions[:, None] >= positions[None, :])
    allowed = allowed[:, :, None]
    spread = running[:, None, :] - running[None, :, :]
    weights = jnp.where(allowed, jnp.exp(jnp.where(allowed, spread, 0.0)), 0.0)
    scores = jnp.dot(reads, writes.T, precision=HIGHEST)
    scaled = inputs_x * deltas[:, :, None]
    within = jnp.einsum('tsh,shp->thp', weights * scores[:, :, None], scaled, precision=HIGHEST)
    entry_scale = jnp.exp(running) * (counts == before).astype(running.dtype)[:, None]
    carried = jnp.einsum('tn,hpn->thp', reads, states, precision=HIGHEST) * entry_scale[:, :, None]
    leaving = jnp.exp(running[-1][None, :] - running) * (counts == counts[-1]).astype(running.dtype)[:, None]
    newest = jnp.einsum('sh,shp,sn->hpn', leaving, scaled, writes, precision=HIGHEST)
    overall = jnp.exp(running[-1]) * (counts[-1] == before).astype(running.dtype)
    return (states * overall[:, None, None] + newest, within + carried)

def scan_groups(states, inputs_x, writes, reads, deltas, decay_rate, counts, before):
    blocks = inputs_x.shape[0] // GROUP
    befores = jnp.concatenate([jnp.reshape(before, (1,)), counts[GROUP - 1::GROUP][:-1]]).astype(jnp.int32)

    def block_step(carry_states, pieces):
        return jax.checkpoint(group_step)(carry_states, pieces[0], pieces[1], pieces[2], pieces[3], decay_rate, pieces[4], pieces[5])
    pieces = (inputs_x.reshape((blocks, GROUP) + inputs_x.shape[1:]), writes.reshape(blocks, GROUP, -1), reads.reshape(blocks, GROUP, -1), deltas.reshape(blocks, GROUP, -1), counts.reshape(blocks, GROUP), befores)
    last_states, outputs = lax.scan(block_step, states, pieces)
    return (last_states, outputs.reshape((blocks * GROUP,) + outputs.shape[2:]))

def causal_conv(values, weight, shift_term, counts):
    taps_count = weight.shape[0]
    length = values.shape[0]
    padded = jnp.pad(values, ((taps_count - 1, 0), (0, 0)))
    padded_counts = jnp.pad(counts, (taps_count - 1, 0))
    result = jnp.zeros_like(values) + shift_term[None, :]
    for offset in range(taps_count):
        inside = (padded_counts[offset:offset + length] == counts).astype(values.dtype)
        result = result + weight[offset][None, :] * padded[offset:offset + length] * inside[:, None]
    return result

def sequence(x_float, starts, params):
    norm_gain, gate_x_weight, bc_weight, dt_weight, conv_x_weight, conv_x_bias, conv_bc_weight, conv_bc_bias, dt_bias, a_log, d_skip, gate_gain, out_weight = params
    length = x_float.shape[0]
    places = jnp.arange(length).astype(jnp.int32)
    counts = start_counts(starts, places)
    scale = lax.rsqrt(lax.optimization_barrier(jnp.mean(x_float * x_float, axis=1, keepdims=True)) + EPSILON)
    normed = low(x_float * scale * norm_gain[None, :])
    gate_in = low_back(jnp.dot(normed, gate_x_weight[:, 0, :], precision=HIGHEST))
    x_in = low_back(low(jnp.dot(normed, gate_x_weight[:, 1, :], precision=HIGHEST)))
    bc_in = low_back(low(jnp.dot(normed, bc_weight, precision=HIGHEST)))
    dt_in = low_back(jnp.dot(normed, dt_weight, precision=HIGHEST))
    x_conv = low(jax.nn.silu(causal_conv(x_in, conv_x_weight, conv_x_bias, counts)))
    bc_conv = low(jax.nn.silu(causal_conv(bc_in, conv_bc_weight, conv_bc_bias, counts)))
    writes = bc_conv[:, :STATE]
    reads = bc_conv[:, STATE:]
    deltas = jax.nn.softplus(dt_in + dt_bias[None, :])
    decay_rate = -jnp.exp(a_log)
    inputs_x = x_conv.reshape(length, HEADS, HEAD_DIM)
    zero_states = jnp.zeros((HEADS, HEAD_DIM, STATE), jnp.float32)
    last_states, outputs = scan_groups(zero_states, inputs_x, writes, reads, deltas, decay_rate, counts, jnp.int32(0))
    ssd_out = low_back(outputs.reshape(length, HEADS * HEAD_DIM))
    mixed = ssd_out + (inputs_x * d_skip[None, :, None]).reshape(length, HEADS * HEAD_DIM)
    gated = mixed * jax.nn.silu(gate_in)
    gate_scale = lax.rsqrt(lax.optimization_barrier(jnp.mean(gated * gated, axis=1, keepdims=True)) + EPSILON)
    branch = low(gated * gate_scale * gate_gain[None, :])
    return x_float + jnp.dot(branch, out_weight, precision=HIGHEST)

def reference(tokens, doc_starts, norm_gain, gate_x_weight, bc_weight, dt_weight, conv_x_weight, conv_x_bias, conv_bc_weight, conv_bc_bias, dt_bias, a_log, d_skip, gate_gain, out_weight, cotangent):
    weights = tuple((member.astype(jnp.float32) for member in (norm_gain, gate_x_weight, bc_weight, dt_weight, conv_x_weight, conv_x_bias, conv_bc_weight, conv_bc_bias, dt_bias, a_log, d_skip, gate_gain, out_weight)))

    def forward(x_float, *params):

        def single(pieces):
            return sequence(pieces[0], pieces[1], params)
        return lax.map(jax.checkpoint(single), (x_float, doc_starts))
    result, pull = jax.vjp(forward, tokens.astype(jnp.float32), *weights)
    grads = pull(cotangent.astype(jnp.float32))
    return (result.astype(jnp.bfloat16), grads[0].astype(jnp.bfloat16), grads[1], grads[2], grads[3], grads[4], grads[5], grads[6], grads[7], grads[8], grads[9], grads[10], grads[11], grads[12], grads[13])
```

```python
from functools import partial

import jax
import jax.numpy as jnp
import numpy as np
from jax import lax
from jax.experimental import pallas as pl
from jax.experimental.pallas import tpu as pltpu
from jax.sharding import PartitionSpec as P

EPS = 1e-05
Q = 128
TILE = 256
RIM = 16
NEVER = -1e30
TINY = 1e-37
BF = jnp.bfloat16
F32 = jnp.float32
VMEM_BYTES = 56 * 2**20
GAIN, TAPS, SHIFT, GATE, SKIP, RATE, BIAS, TABLE = 0, 1, 5, 6, 7, 8, 9, 16


def dot(a, b):
    return jnp.dot(a, b, preferred_element_type=F32)


def dot_nt(a, b):
    return lax.dot_general(a, b, (((1,), (1,)), ((), ())), preferred_element_type=F32)


def dot_tn(a, b):
    return lax.dot_general(a, b, (((0,), (0,)), ((), ())), preferred_element_type=F32)


def halves(value):
    high = value.astype(BF)
    return high, (value - high.astype(F32)).astype(BF)


def twice(value, axis):
    return jnp.concatenate([value, value], axis=axis)


def stacked(value, axis):
    return jnp.concatenate(halves(value), axis=axis)


def spread_heads(value, spread):
    return dot(jnp.concatenate(halves(value), axis=1), spread)


def gather_heads(value, gather):
    return dot(jnp.concatenate(halves(value), axis=1), gather)


def add_up(value, wedge):
    return dot(wedge, jnp.concatenate(halves(value), axis=0))


def sigmoid(value):
    return jax.nn.sigmoid(value)


def softplus(value):
    return jnp.maximum(value, 0.0) + jnp.log1p(jnp.exp(-jnp.abs(value)))


def iota(shape, axis):
    return lax.broadcasted_iota(jnp.int32, shape, axis)


class Docs:
    def __init__(self, meta, m):
        self.count = meta.shape[1] - 1
        self.starts = [meta[m, j] for j in range(self.count)]
        self.anchor = meta[m, self.count]

    def counts(self, places):
        total = (places >= self.starts[0]).astype(jnp.int32)
        for start in self.starts[1:]:
            total = total + (places >= start).astype(jnp.int32)
        return total

    def starts_at(self, places):
        hit = places == self.starts[0]
        for start in self.starts[1:]:
            hit = hit | (places == start)
        return hit

    def tap_masks(self, first, rows):
        places = first + iota((rows, 128), 0)
        masks = []
        broken = None
        for back in range(3):
            hit = self.starts_at(places - back)
            broken = hit if broken is None else broken | hit
            masks.append(jnp.where(broken, 0.0, 1.0))
        return masks


class Chunk:
    def __init__(self, docs, first, deltas, rate, wedge):
        self.before = docs.counts(first - 1)
        self.last = docs.counts(first + Q - 1)
        column = docs.counts(first + iota((Q, 128), 0))
        self.docs, self.first, self.column = docs, first, column
        self.run = add_up(deltas * rate, wedge)
        self.total = self.run[Q - 1 : Q]
        self.entry_bias = jnp.where(column == self.before, 0.0, NEVER)
        self.leave_bias = jnp.where(column == self.last, 0.0, NEVER)
        self.through = jnp.where(self.last == self.before, 0.0, NEVER)
        self.deltas = deltas

    def same(self):
        return self.column == self.docs.counts(self.first + iota((8, 128), 1))[0:1]

    def entry(self):
        return jnp.exp(self.run + self.entry_bias)

    def leaving(self):
        return jnp.exp(self.total - self.run + self.leave_bias) * self.deltas

    def overall(self):
        return jnp.exp(self.total + self.through)


def wide_row(row):
    return jnp.broadcast_to(row, (8, row.shape[1]))


def pair_blocks(value, pair, lanes):
    both = value[:, 128 * pair : 128 * pair + 128]
    zero = jnp.zeros_like(both)
    return jnp.concatenate([jnp.where(lanes, both, zero), jnp.where(lanes, zero, both)], axis=0)


def first_kernel(
    tile, channels,
    meta, rim, tokens, weights, table, spread, wedge, *rest, m,
):
    normed_o, gate_o, xbc_o, pre_o, conv_o, deltas_o, held_o, sums_o, leaving_o, edge_o, ext, state, total = rest[-13:]
    step = pl.program_id(0)
    docs = Docs(meta, m)
    width = xbc_o.shape[1]
    taps = table[TAPS : TAPS + 4, :width]
    shift = table[SHIFT : SHIFT + 1, :width]
    gain = table[GAIN : GAIN + 1, : tokens.shape[1]]
    rate = table[RATE : RATE + 1, :128]
    dt_bias = table[BIAS : BIAS + 1, :128]

    def normalize(rows):
        x = rows.astype(F32)
        scale = lax.rsqrt(jnp.mean(x * x, axis=1, keepdims=True) + EPS)
        return (x * scale * gain).astype(BF)

    @pl.when(step == 0)
    def _():
        edge = dot(normalize(rim[...]), weights[:, channels : channels + width]).astype(BF)
        edge_o[...] = edge
        ext[0:8, :] = edge.astype(F32)[RIM - 8 :]
        state[...] = jnp.zeros_like(state)
        total[...] = jnp.zeros_like(total)

    @pl.when(step > 0)
    def _():
        ext[0:8, :] = ext[tile : tile + 8, :]

    normed = normalize(tokens[...])
    normed_o[...] = normed
    gate_o[...] = dot(normed, weights[:, :channels])
    xbc = dot(normed, weights[:, channels : channels + width]).astype(BF)
    xbc_o[...] = xbc
    ext[8:, :] = xbc.astype(F32)
    deltas = softplus(dot(normed, weights[:, channels + width + 256 :]) + dt_bias)
    deltas_o[...] = deltas
    first = docs.anchor + step * tile
    masks = docs.tap_masks(first, tile)
    for slab in range(width // 128):
        lanes = slice(128 * slab, 128 * slab + 128)
        pre = shift[:, lanes] + taps[3:4, lanes] * ext[8 : 8 + tile, lanes]
        for back in range(1, 4):
            pre = pre + taps[3 - back : 4 - back, lanes] * ext[8 - back : 8 - back + tile, lanes] * masks[back - 1]
        pre_o[:, lanes] = pre
        conv_o[:, lanes] = (pre * sigmoid(pre)).astype(BF)
    for part in range(tile // Q):
        rows = slice(Q * part, Q * part + Q)
        chunk = Chunk(docs, first + Q * part, deltas[rows], rate, wedge[...])
        held_o[part] = state[...]
        sums_o[part] = total[...]
        total[...] = total[...] + chunk.total
        writes = conv_o[rows, channels : channels + 128]
        scaled = conv_o[rows, :channels].astype(F32) * spread_heads(chunk.leaving(), spread[...])
        keep = spread_heads(wide_row(chunk.overall()), spread[...])[0:1]
        state[...] = state[...] * keep + dot_tn(twice(writes, 0), stacked(scaled, 0))

    @pl.when(step == pl.num_programs(0) - 1)
    def _():
        end = docs.anchor + (step + 1) * tile - 1
        through = jnp.where(docs.counts(end) == docs.counts(docs.anchor - 1), 0.0, NEVER)
        leaving_o[0:128, :] = state[...]
        leaving_o[128:136, :] = spread_heads(jnp.exp(total[...] + through), spread[...])


def inside_kernel(
    tile, channels,
    meta, conv, deltas, cotangent, out_weight, table, spread, wedge, *rest, m, parts,
):
    mixed_o, back_o, near_o = rest[-3:]
    step = pl.program_id(0)

    @pl.when(step == 0)
    def _():
        near_o[...] = joined([part[...] for part in rest[:parts]])

    docs = Docs(meta, m)
    first = docs.anchor + step * tile
    lanes_q = iota((Q, 128), 1)
    causal = iota((Q, Q), 0) >= iota((Q, Q), 1)
    low = lanes_q < 64
    skip = table[SKIP : SKIP + 1, :channels]
    rate = table[RATE : RATE + 1, :128]
    back_o[...] = dot_nt(cotangent[...], out_weight[...])
    for part in range(tile // Q):
        rows = slice(Q * part, Q * part + Q)
        chunk = Chunk(docs, first + Q * part, deltas[rows, :], rate, wedge[...])
        u = conv[rows, :channels]
        writes = conv[rows, channels : channels + 128]
        reads = conv[rows, channels + 128 :]
        scores = dot_nt(reads, writes)
        bias = jnp.where(chunk.same() & causal, 0.0, NEVER)
        behind = jnp.transpose(jnp.log(jnp.maximum(chunk.deltas, TINY)) - chunk.run)
        pieces = []
        for pair in range(channels // 128):
            both = []
            for head in (2 * pair, 2 * pair + 1):
                decay = jnp.exp(chunk.run[:, head : head + 1] + behind[head : head + 1] + bias)
                both.append((decay * scores).astype(BF))
            pieces.append(dot(jnp.concatenate(both, axis=1), pair_blocks(u, pair, low)))
        mixed_o[rows, :] = jnp.concatenate(pieces, axis=1) + skip * u.astype(F32)


def mix_kernel(
    tile, channels,
    meta, inside, back, conv, deltas, gate, held, sums, table, spread, wedge, *rest, m, parts,
):
    mixed_o, stats_o, carry = rest[-3:]
    step = pl.program_id(0)

    @pl.when(step == 0)
    def _():
        carry[...] = joined([part[...] for part in rest[:parts]])

    docs = Docs(meta, m)
    first = docs.anchor + step * tile
    lanes_q = iota((Q, 128), 1)
    gate_gain = table[GATE : GATE + 1, :channels]
    rate = table[RATE : RATE + 1, :128]
    for part in range(tile // Q):
        rows = slice(Q * part, Q * part + Q)
        chunk = Chunk(docs, first + Q * part, deltas[rows, :], rate, wedge[...])
        reads = conv[rows, channels + 128 :]
        since = jnp.where(chunk.before == docs.counts(docs.anchor - 1), 0.0, NEVER)
        arrived = spread_heads(jnp.exp(sums[part] + since), spread[...])[0:1]
        state = stacked(held[part] + arrived * carry[0:128, :], 0)
        mixed = inside[rows, :] + dot(twice(reads, 1), state) * spread_heads(chunk.entry(), spread[...])
        mixed_o[rows, :] = mixed
        gate_rows = gate[rows, :]
        gated = mixed * gate_rows * sigmoid(gate_rows)
        squares = jnp.sum(gated * gated, axis=1, keepdims=True)
        inner = jnp.sum(gated * back[rows, :] * gate_gain, axis=1, keepdims=True)
        columns = jnp.where(lanes_q == 0, squares, jnp.where(lanes_q == 1, inner, 0.0))
        stats_o[:, rows] = jnp.transpose(columns)[0:8]


def third_kernel(
    tile, channels, full, chained,
    meta, mixed, back, gate, conv, deltas, normed, cotangent, out_weight, table, spread, wedge,
    stats_a, stats_b, stats_c, stats_d, *rest, m,
):
    if chained:
        grad_out_i, grad_gate_i, rows_i, *rest = rest
    branch_o, gate_back_o, ssd_back_o, held_o, sums_o, leaving_o, grad_out, grad_gate, rows_o, state, total = rest[-11:]
    step = pl.program_id(0)
    gate_gain = table[GATE : GATE + 1, :channels]
    rate = table[RATE : RATE + 1, :128]
    docs = Docs(meta, m)
    place = pl.num_programs(0) - 1 - step
    first = docs.anchor + place * tile

    @pl.when(step == 0)
    def _():
        state[...] = jnp.zeros_like(state)
        total[...] = jnp.zeros_like(total)
        if chained:
            grad_out[...] = grad_out_i[...]
            grad_gate[...] = grad_gate_i[...]
            rows_o[...] = rows_i[...]
        else:
            grad_out[...] = jnp.zeros_like(grad_out)
            grad_gate[...] = jnp.zeros_like(grad_gate)
            rows_o[...] = jnp.zeros_like(rows_o)

    stats = stats_a[...] + stats_b[...] + stats_c[...] + stats_d[...]
    branches = []
    for part in reversed(range(tile // Q)):
        rows = slice(Q * part, Q * part + Q)
        sides = jnp.transpose(jnp.concatenate([stats[:, rows], jnp.zeros((120, Q), F32)], axis=0))
        scale = lax.rsqrt(sides[:, 0:1] / full + EPS)
        inner = sides[:, 1:2]
        mixed_rows = mixed[rows, :]
        gate_rows = gate[rows, :]
        sigma = sigmoid(gate_rows)
        act = gate_rows * sigma
        gated = mixed_rows * act
        unit = gated * scale
        branch = (unit * gate_gain).astype(BF)
        branches.append(branch)
        back_rows = back[rows, :]
        grad_gated = scale * (back_rows * gate_gain) - unit * (scale * scale * (inner / full))
        grad_mixed = grad_gated * act
        gate_back_o[rows, :] = (grad_gated * mixed_rows * (sigma * (1.0 + gate_rows * (1.0 - sigma)))).astype(BF)
        ssd_back = grad_mixed.astype(BF)
        ssd_back_o[rows, :] = ssd_back
        u = conv[rows, :channels].astype(F32)
        rows_o[0:8, :] += jnp.sum((back_rows * unit).reshape(Q // 8, 8, channels), axis=0)
        rows_o[8:16, :] += jnp.sum((grad_mixed * u).reshape(Q // 8, 8, channels), axis=0)
        chunk = Chunk(docs, first + Q * part, deltas[rows, :], rate, wedge[...])
        held_o[part] = state[...]
        sums_o[part] = total[...]
        total[...] = total[...] + chunk.total
        reads = conv[rows, channels + 128 :]
        entered = stacked(ssd_back.astype(F32) * spread_heads(chunk.entry(), spread[...]), 0)
        keep = spread_heads(wide_row(chunk.overall()), spread[...])[0:1]
        state[...] = state[...] * keep + dot_tn(twice(reads, 0), entered)
    branch = jnp.concatenate(branches[::-1], axis=0)
    branch_o[...] = dot(branch, out_weight[...]).astype(BF)
    grad_out[...] += dot_tn(branch, cotangent[...])
    grad_gate[...] += dot_tn(normed[...], gate_back_o[...])

    @pl.when(step == pl.num_programs(0) - 1)
    def _():
        end = docs.anchor + pl.num_programs(0) * tile - 1
        through = jnp.where(docs.counts(end) == docs.counts(docs.anchor - 1), 0.0, NEVER)
        leaving_o[0:128, :] = state[...]
        leaving_o[128:136, :] = spread_heads(jnp.exp(total[...] + through), spread[...])


def within_kernel(
    tile, channels,
    meta, conv, deltas, ssd_back, table, wedge, *rest, m, parts,
):
    grads_o, source_o, target_o, near_o = rest[-4:]
    step = pl.program_id(0)

    @pl.when(step == 0)
    def _():
        near_o[...] = joined([part[...] for part in rest[:parts]])

    docs = Docs(meta, m)
    first = docs.anchor + step * tile
    lanes_q = iota((Q, 128), 1)
    rows_8 = iota((8, 128), 0)
    causal = iota((Q, Q), 1) >= iota((Q, Q), 0)
    low = lanes_q < 64
    skip = table[SKIP : SKIP + 1, :channels]
    rate = table[RATE : RATE + 1, :128]
    for part in range(tile // Q):
        rows = slice(Q * part, Q * part + Q)
        chunk = Chunk(docs, first + Q * part, deltas[rows, :], rate, wedge[...])
        u = conv[rows, :channels]
        writes = conv[rows, channels : channels + 128]
        reads = conv[rows, channels + 128 :]
        grad = ssd_back[rows, :]
        scores = dot_nt(writes, reads)
        bias = jnp.where(chunk.same() & causal, 0.0, NEVER)
        ahead = jnp.transpose(chunk.run)
        behind = jnp.log(jnp.maximum(chunk.deltas, TINY)) - chunk.run
        grad_scores = jnp.zeros((Q, Q), F32)
        by_source = jnp.zeros((Q, 128), F32)
        by_target = jnp.zeros((8, 128), F32)
        pieces = []
        for pair in range(channels // 128):
            blocks = pair_blocks(grad, pair, low)
            meets = dot_nt(u[:, 128 * pair : 128 * pair + 128], blocks)
            both = []
            for side in range(2):
                head = 2 * pair + side
                decay = jnp.exp(behind[:, head : head + 1] + ahead[head : head + 1] + bias)
                both.append((decay * scores).astype(BF))
                weighed = decay * meets[:, Q * side : Q * side + Q]
                grad_scores = grad_scores + weighed
                pairs = weighed * scores
                by_source = jnp.where(lanes_q == head, jnp.sum(pairs, axis=1, keepdims=True), by_source)
                by_target = jnp.where(rows_8 == head, jnp.sum(pairs, axis=0, keepdims=True), by_target)
            pieces.append(dot(jnp.concatenate(both, axis=1), blocks))
        source_o[rows, :] = by_source
        target_o[rows, :] = jnp.transpose(jnp.concatenate([by_target, jnp.zeros((120, Q), F32)], axis=0))
        high, low_part = halves(grad_scores)
        grads_o[rows, :channels] = jnp.concatenate(pieces, axis=1) + skip * grad.astype(F32)
        grads_o[rows, channels : channels + 128] = dot(jnp.concatenate([high, low_part], axis=1), twice(reads, 0))
        grads_o[rows, channels + 128 :] = dot_tn(jnp.concatenate([high, low_part], axis=0), twice(writes, 0))


def across_kernel(
    tile, channels, chained,
    meta, conv, pre, xbc, edge, deltas, ssd_back, inside, by_source, by_target,
    held, sums, carry, held_b, sums_b,
    table, spread, gather, wedge, wedge_up, wedge_below, *rest, m, parts,
):
    far, rest = rest[:parts], rest[parts:]
    if chained:
        taps_i, heads_i, *rest = rest
    in_back_o, dt_back_o, rim_o, tail_o, taps_o, heads_o, ext, grads, carry_b = rest[-9:]
    step = pl.program_id(0)
    docs = Docs(meta, m)
    places = pl.num_programs(0)
    place = places - 1 - step
    first = docs.anchor + place * tile
    end = docs.anchor + places * tile - 1
    width = pre.shape[1]
    taps = table[TAPS : TAPS + 4, :width]
    rate = table[RATE : RATE + 1, :128]

    @pl.when(step == 0)
    def _():
        if chained:
            taps_o[...] = taps_i[...]
            heads_o[...] = heads_i[...]
        else:
            taps_o[...] = jnp.zeros_like(taps_o)
            heads_o[...] = jnp.zeros_like(heads_o)
        carry_b[...] = joined([part[...] for part in far])
        ext[:, 0:16, :] = jnp.zeros_like(ext[:, 0:16, :])
        ext[:, 16 + tile :, :] = jnp.zeros_like(ext[:, 16 + tile :, :])

    @pl.when(step > 0)
    def _():
        ext[:, 16 + tile :, :] = ext[:, 16:24, :]

    for part in range(tile // Q):
        rows = slice(Q * part, Q * part + Q)
        chunk = Chunk(docs, first + Q * part, deltas[rows, :], rate, wedge[...])
        u = conv[rows, :channels].astype(F32)
        writes = conv[rows, channels : channels + 128]
        reads = conv[rows, channels + 128 :]
        since = jnp.where(chunk.before == docs.counts(docs.anchor - 1), 0.0, NEVER)
        until = jnp.where(chunk.last == docs.counts(end), 0.0, NEVER)
        arrived = spread_heads(jnp.exp(sums[part] + since), spread[...])[0:1]
        state = held[part] + arrived * carry[0:128, :]
        arrived_b = spread_heads(jnp.exp(sums_b[part] + until), spread[...])[0:1]
        state_b = held_b[part] + arrived_b * carry_b[0:128, :]
        state_high, state_low = halves(state)
        state_b_high, state_b_low = halves(state_b)
        outward = spread_heads(chunk.leaving(), spread[...])
        sent_high, sent_low = halves(u * outward)
        grad_in = ssd_back[rows, :].astype(F32) * spread_heads(chunk.entry(), spread[...])
        grad_high, grad_low = halves(grad_in)
        crossing = dot(twice(writes, 1), jnp.concatenate([state_b_high, state_b_low], axis=0)) * outward
        out_part = gather_heads(u * crossing, gather[...])
        in_part = gather_heads(
            grad_in * dot(twice(reads, 1), jnp.concatenate([state_high, state_low], axis=0)), gather[...]
        )
        between = jnp.sum((state * state_b).reshape(16, 8, channels), axis=0)
        between = jnp.sum(gather_heads(between, gather[...]), axis=0, keepdims=True) * chunk.overall()
        source = by_source[rows, :]
        grad_run = (
            between
            + add_up(in_part + by_target[rows, :] - source, wedge_up[...])
            + add_up(out_part, wedge_below[...])
        )
        slope = 1.0 - jnp.exp(-chunk.deltas)
        ratio = jnp.where(chunk.deltas > 1e-6, slope / jnp.maximum(chunk.deltas, 1e-6), 1.0)
        dt_back = (source + out_part) * ratio + rate * grad_run * slope
        dt_back_o[rows, :] = dt_back.astype(BF)
        heads_o[0:8, :] += jnp.sum(dt_back.reshape(Q // 8, 8, 128), axis=0)
        heads_o[8:16, :] += jnp.sum((grad_run * chunk.deltas).reshape(Q // 8, 8, 128), axis=0)
        grads[rows, :channels] = inside[rows, :channels] + crossing
        grads[rows, channels : channels + 128] = inside[rows, channels : channels + 128] + dot_nt(
            jnp.concatenate([sent_high, sent_low, sent_high], axis=1),
            jnp.concatenate([state_b_high, state_b_high, state_b_low], axis=1),
        )
        grads[rows, channels + 128 :] = inside[rows, channels + 128 :] + dot_nt(
            jnp.concatenate([grad_high, grad_low, grad_high], axis=1),
            jnp.concatenate([state_high, state_high, state_low], axis=1),
        )

    masks = docs.tap_masks(first, tile)
    for slab in range(width // 128):
        lanes = slice(128 * slab, 128 * slab + 128)
        pre_rows = pre[:, lanes]
        sigma = sigmoid(pre_rows)
        grad_pre = grads[:, lanes] * (sigma * (1.0 + pre_rows * (1.0 - sigma)))
        source = xbc[:, lanes].astype(F32)
        result = taps[3:4, lanes] * grad_pre
        taps_o[24:32, lanes] += jnp.sum((grad_pre * source).reshape(tile // 8, 8, 128), axis=0)
        taps_o[32:40, lanes] += jnp.sum(grad_pre.reshape(tile // 8, 8, 128), axis=0)
        for back in range(1, 4):
            ext[back - 1, 16 : 16 + tile, lanes] = grad_pre * masks[back - 1]
            moved = ext[back - 1, 16 + back : 16 + back + tile, lanes]
            result = result + taps[3 - back : 4 - back, lanes] * moved
            taps_o[8 * (3 - back) : 8 * (4 - back), lanes] += jnp.sum((moved * source).reshape(tile // 8, 8, 128), axis=0)
        high = result.astype(BF)
        in_back_o[:, lanes] = high
        if 128 * slab >= channels:
            in_back_o[:, slice(256 + 128 * slab, 384 + 128 * slab)] = (result - high.astype(F32)).astype(BF)

        @pl.when(step == 0)
        def _():
            tail_o[:, lanes] = result[tile - RIM :]

    @pl.when(place == 0)
    def _():
        total = jnp.zeros((RIM, width), F32)
        source = edge[...].astype(F32)
        for back in range(1, 4):
            moved = ext[back - 1, back : back + RIM, :]
            total = total + taps[3 - back : 4 - back, :] * moved
            taps_o[8 * (3 - back) : 8 * (4 - back), :] += jnp.sum((moved * source).reshape(RIM // 8, 8, width), axis=0)
        rim_o[...] = total


def input_kernel(
    tile, channels, chained, last,
    tokens, normed, gate_back, in_back, dt_back, weights, *rest,
):
    if last:
        tail, rim, *rest = rest
    if chained:
        grads_i, rows_i, *rest = rest
    part_o, grads_o, rows_o, every = rest[-4:]
    step = pl.program_id(0)
    wide = in_back.shape[1]
    width = wide - 256

    @pl.when(step == 0)
    def _():
        if chained:
            grads_o[...] = grads_i[...]
            rows_o[...] = rows_i[...]
        else:
            grads_o[...] = jnp.zeros_like(grads_o)
            rows_o[...] = jnp.zeros_like(rows_o)

    every[:, :channels] = gate_back[...]
    every[:, channels : channels + wide] = in_back[...]
    every[:, channels + wide :] = dt_back[...]
    if last:
        high, low = halves(tail[...] + rim[...])
        every[tile - RIM :, channels : channels + width] = high
        every[tile - RIM :, channels + width : channels + wide] = low[:, channels:]
    x = tokens[...].astype(F32)
    scale = lax.rsqrt(jnp.mean(x * x, axis=1, keepdims=True) + EPS)
    part = dot_nt(every[...], weights[...])
    part_o[...] = part.astype(BF)
    rows_o[...] += jnp.sum((part * (x * scale)).reshape(tile // 8, 8, x.shape[1]), axis=0)
    grads_o[...] += dot_tn(normed[...], every[:, channels:])


class Call:
    def __init__(self, kernel, steps, name):
        self.kernel, self.steps, self.name = kernel, steps, name
        self.args, self.in_specs, self.outs, self.out_specs, self.scratch = [], [], [], [], []
        self.aliases = {}

    def whole(self, *arrays):
        for array in arrays:
            self.args.append(array)
            self.in_specs.append(pl.BlockSpec(array.shape, lambda i, rank=array.ndim: (0,) * rank))
        return self

    def scalars(self, array):
        self.args.append(array)
        self.in_specs.append(pl.BlockSpec(memory_space=pltpu.SMEM))
        return self

    def blocks(self, *arrays_specs):
        for array, spec in arrays_specs:
            self.args.append(array)
            self.in_specs.append(spec)
        return self

    def out(self, shape, dtype, spec=None):
        self.outs.append(jax.ShapeDtypeStruct(shape, dtype))
        self.out_specs.append(spec or pl.BlockSpec(shape, lambda i, rank=len(shape): (0,) * rank))
        return self

    def after(self, *arrays):
        for array in arrays:
            self.args.append(array)
            self.in_specs.append(pl.BlockSpec(memory_space=pl.ANY))
        return self

    def alias(self, array):
        self.aliases = {len(self.args): 0}
        return self.after(array)

    def temp(self, shape, dtype):
        self.scratch.append(pltpu.VMEM(shape, dtype))
        return self

    def run(self, micros):
        return pl.pallas_call(
            self.kernel,
            grid=(self.steps,),
            in_specs=self.in_specs,
            out_specs=tuple(self.out_specs),
            out_shape=tuple(self.outs),
            scratch_shapes=self.scratch,
            input_output_aliases=self.aliases,
            compiler_params=pltpu.CompilerParams(
                dimension_semantics=("arbitrary",), vmem_limit_bytes=VMEM_BYTES
            ),
            cost_estimate=pl.CostEstimate(flops=int(micros * 1.15e9), bytes_accessed=0, transcendentals=0),
            name=self.name,
        )(*self.args)


def swap(value, axis, bits):
    count = lax.axis_size(axis)
    return lax.ppermute(value, axis, [(i, i ^ bits) for i in range(count)])


def from_behind(value, axis, steps):
    count = lax.axis_size(axis)
    sources = range(max(0, -steps), min(count, count - steps))
    return lax.ppermute(value, axis, [(i, i + steps) for i in sources])


def joined(parts):
    rows = parts[0].shape[0] - 8
    state, decay = parts[0][:rows], parts[0][rows : rows + 1]
    for part in parts[1:]:
        state = state + decay * part[:rows]
        decay = decay * part[rows : rows + 1]
    return jnp.concatenate([state, jnp.broadcast_to(decay, (8, decay.shape[1]))], axis=0)


def near_parts(leaving, axis, sign):
    return [from_behind(leaving, axis, sign * k) for k in range(1, min(4, lax.axis_size(axis)))]


def far_parts(carry, axis, sign):
    count = lax.axis_size(axis)
    window = 3
    parts = [carry]
    while window < count - 1:
        carry = joined(parts) if len(parts) > 1 else carry
        parts = [carry] + [from_behind(carry, axis, sign * k) for k in (window, 2 * window) if k < count]
        window *= 3
    return parts


def sum_rows(parts):
    total = parts[0].astype(F32)
    for part in parts[1:]:
        total = total + part.astype(F32)
    return total


def head_pair(part):
    rows = part.shape[0] // 2
    side = lax.axis_index("head") % 2
    mine = lax.dynamic_slice_in_dim(part, side * rows, rows, 0)
    other = lax.dynamic_slice_in_dim(part, (1 - side) * rows, rows, 0)
    return (mine.astype(F32) + swap(other, "head", 1).astype(F32)).astype(BF)


def head_rest(low):
    total = low.astype(F32)
    bit = 2
    while bit < lax.axis_size("head"):
        low = total.astype(BF)
        total = low.astype(F32) + swap(low, "head", bit).astype(F32)
        bit *= 2
    return total


def scatter_sum(value, axis):
    count = lax.axis_size(axis)
    me = lax.axis_index(axis)
    rows = value.shape[0] // count
    total = lax.dynamic_slice_in_dim(value, me * rows, rows, 0).astype(F32)
    for bits in range(1, count):
        piece = lax.dynamic_slice_in_dim(value, jnp.bitwise_xor(me, bits) * rows, rows, 0)
        total = total + swap(piece, axis, bits).astype(F32)
    return total


def gather_rows(value, axis):
    count = lax.axis_size(axis)
    me = lax.axis_index(axis)
    rows = value.shape[0]
    result = jnp.zeros((count * rows, value.shape[1]), value.dtype)
    result = lax.dynamic_update_slice_in_dim(result, value, me * rows, 0)
    for bits in range(1, count):
        result = lax.dynamic_update_slice_in_dim(
            result, swap(value, axis, bits), jnp.bitwise_xor(me, bits) * rows, 0
        )
    return result


def all_sum(value, axis):
    bit = 1
    while bit < lax.axis_size(axis):
        value = value + swap(value, axis, bit)
        bit *= 2
    return value


def local(
    tokens,
    doc_starts,
    norm_gain,
    gate_x_weight,
    bc_weight,
    dt_weight,
    conv_x_weight,
    conv_x_bias,
    conv_bc_weight,
    conv_bc_bias,
    dt_bias,
    a_log,
    d_skip,
    gate_gain,
    out_weight,
    cotangent,
):
    micro, length, model = tokens.shape
    channels = gate_x_weight.shape[2]
    heads = dt_weight.shape[1]
    dim = channels // heads
    states = bc_weight.shape[1] // 2
    width = channels + 2 * states
    full = channels * lax.axis_size("head")
    tile = TILE
    steps = length // tile
    per = tile // Q
    blocks = length // Q

    rim_tokens = from_behind(tokens[:, length - RIM :], "seq", 1)
    weights = jnp.concatenate(
        [gate_x_weight[:, 0], gate_x_weight[:, 1], bc_weight, bc_weight,
         jnp.pad(dt_weight, ((0, 0), (0, 128 - heads)))], axis=1
    )
    decay_rate = -jnp.exp(a_log)

    def table_rows(*parts):
        row = jnp.concatenate(parts, axis=-1)
        row = row if row.ndim == 2 else row[None]
        return jnp.pad(row, ((0, 0), (0, model - row.shape[1])))

    table = jnp.concatenate(
        [
            table_rows(norm_gain),
            table_rows(conv_x_weight, conv_bc_weight),
            table_rows(conv_x_bias, conv_bc_bias),
            table_rows(gate_gain),
            table_rows(jnp.repeat(d_skip, dim)),
            table_rows(decay_rate),
            table_rows(dt_bias, jnp.full((128 - heads,), -200.0, F32)),
            jnp.zeros((TABLE - BIAS - 1, model), F32),
        ],
        axis=0,
    )
    owner = np.arange(channels)[None, :] // dim == np.arange(128)[:, None]
    spread = np.concatenate([owner, owner], axis=0).astype(BF)
    gather = np.concatenate([owner.T, owner.T], axis=0).astype(BF)
    order = np.arange(Q)
    until_here = order[:, None] >= order[None, :]
    below = order[:, None] > order[None, :]
    wedge = np.concatenate([until_here] * 2, axis=1).astype(BF)
    wedge_up = np.concatenate([until_here.T] * 2, axis=1).astype(BF)
    wedge_below = np.concatenate([below] * 2, axis=1).astype(BF)
    anchor = lax.axis_index("seq") * length
    meta = jnp.concatenate(
        [jnp.where(doc_starts >= 1, doc_starts, 2**30), jnp.full((micro, 1), anchor)], axis=1
    ).astype(jnp.int32)

    ahead = lambda i: i
    astern = lambda i: steps - 1 - i

    def rows_of(cols, turn):
        return pl.BlockSpec((tile, cols), lambda i: (turn(i), 0))

    def rows_in(m, cols, turn):
        return pl.BlockSpec((None, tile, cols), lambda i: (m, turn(i), 0))

    def chunks_of(turn, rows, cols):
        return pl.BlockSpec((per, rows, cols), lambda i: (turn(i), 0, 0))

    def stat_spec(turn):
        return pl.BlockSpec((8, tile), lambda i: (0, turn(i)))

    def project(m, *waits):
        call = Call(partial(first_kernel, tile, channels, m=m), steps, f"project_{m}")
        call.scalars(meta)
        call.blocks((rim_tokens, pl.BlockSpec((None, RIM, model), lambda i: (m, 0, 0))))
        call.blocks((tokens, rows_in(m, model, ahead)))
        call.whole(weights, table, spread, wedge).after(*waits)
        call.out((length, model), BF, rows_of(model, ahead))
        call.out((length, channels), F32, rows_of(channels, ahead))
        call.out((length, width), BF, rows_of(width, ahead))
        call.out((length, width), F32, rows_of(width, ahead))
        call.out((length, width), BF, rows_of(width, ahead))
        call.out((length, 128), F32, rows_of(128, ahead))
        call.out((blocks, 128, channels), F32, chunks_of(ahead, 128, channels))
        call.out((blocks, 8, 128), F32, chunks_of(ahead, 8, 128))
        call.out((136, channels), F32)
        call.out((RIM, width), BF)
        call.temp((tile + 8, width), F32).temp((128, channels), F32).temp((8, 128), F32)
        return call.run(22)

    def inside(m, kept, parts, *waits):
        normed, gate, xbc, pre, conv, deltas = kept[:6]
        call = Call(partial(inside_kernel, tile, channels, m=m, parts=len(parts)), steps, f"inside_{m}")
        call.scalars(meta)
        call.blocks((conv, rows_of(width, ahead)), (deltas, rows_of(128, ahead)), (cotangent, rows_in(m, model, ahead)))
        call.whole(out_weight, table, spread, wedge, *parts).after(*waits)
        call.out((length, channels), F32, rows_of(channels, ahead))
        call.out((length, channels), F32, rows_of(channels, ahead))
        call.out((136, channels), F32)
        return call.run(12)

    def mix(m, kept, inner, back, parts, *waits):
        normed, gate, xbc, pre, conv, deltas, held, sums = kept[:8]
        call = Call(partial(mix_kernel, tile, channels, m=m, parts=len(parts)), steps, f"mix_{m}")
        call.scalars(meta)
        call.blocks(
            (inner, rows_of(channels, ahead)),
            (back, rows_of(channels, ahead)),
            (conv, rows_of(width, ahead)),
            (deltas, rows_of(128, ahead)),
            (gate, rows_of(channels, ahead)),
            (held, chunks_of(ahead, 128, channels)),
            (sums, chunks_of(ahead, 8, 128)),
        )
        call.whole(table, spread, wedge, *parts).after(*waits)
        call.out((length, channels), F32, rows_of(channels, ahead))
        call.out((8, length), F32, stat_spec(ahead))
        call.out((136, channels), F32)
        return call.run(12)

    def norm(m, kept, mixed, back, stats, chain, *waits):
        normed, gate, xbc, pre, conv, deltas = kept[:6]
        call = Call(partial(third_kernel, tile, channels, float(full), bool(chain), m=m), steps, f"gate_{m}")
        call.scalars(meta)
        call.blocks(
            (mixed, rows_of(channels, astern)),
            (back, rows_of(channels, astern)),
            (gate, rows_of(channels, astern)),
            (conv, rows_of(width, astern)),
            (deltas, rows_of(128, astern)),
            (normed, rows_of(model, astern)),
            (cotangent, rows_in(m, model, astern)),
        )
        call.whole(out_weight, table, spread, wedge)
        call.blocks(*[(part, stat_spec(astern)) for part in stats])
        call.whole(*chain).after(*waits)
        call.out((length, model), BF, rows_of(model, astern))
        call.out((length, channels), BF, rows_of(channels, astern))
        call.out((length, channels), BF, rows_of(channels, astern))
        call.out((blocks, 128, channels), F32, chunks_of(astern, 128, channels))
        call.out((blocks, 8, 128), F32, chunks_of(astern, 8, 128))
        call.out((136, channels), F32)
        call.out((channels, model), F32)
        call.out((model, channels), F32)
        call.out((16, channels), F32)
        call.temp((128, channels), F32).temp((8, 128), F32)
        return call.run(19)

    def within(m, kept, ssd_back, parts, *waits):
        conv, deltas = kept[4:6]
        call = Call(partial(within_kernel, tile, channels, m=m, parts=len(parts)), steps, f"within_{m}")
        call.scalars(meta)
        call.blocks((conv, rows_of(width, ahead)), (deltas, rows_of(128, ahead)), (ssd_back, rows_of(channels, ahead)))
        call.whole(table, wedge, *parts).after(*waits)
        call.out((length, width), F32, rows_of(width, ahead))
        call.out((length, 128), F32, rows_of(128, ahead))
        call.out((length, 128), F32, rows_of(128, ahead))
        call.out((136, channels), F32)
        return call.run(14)

    def across(m, kept, carry, third, inner, parts, chain, *waits):
        normed, gate, xbc, pre, conv, deltas, held, sums, leaving, edge = kept
        call = Call(partial(across_kernel, tile, channels, bool(chain), m=m, parts=len(parts)), steps, f"across_{m}")
        call.scalars(meta)
        call.blocks((conv, rows_of(width, astern)), (pre, rows_of(width, astern)), (xbc, rows_of(width, astern)))
        call.whole(edge)
        call.blocks(
            (deltas, rows_of(128, astern)),
            (third[2], rows_of(channels, astern)),
            (inner[0], rows_of(width, astern)),
            (inner[1], rows_of(128, astern)),
            (inner[2], rows_of(128, astern)),
            (held, chunks_of(astern, 128, channels)),
            (sums, chunks_of(astern, 8, 128)),
        )
        call.whole(carry)
        call.blocks((third[3], chunks_of(astern, 128, channels)), (third[4], chunks_of(astern, 8, 128)))
        call.whole(table, spread, gather, wedge, wedge_up, wedge_below, *parts, *chain).after(*waits)
        call.out((length, width + 256), BF, rows_of(width + 256, astern))
        call.out((length, 128), BF, rows_of(128, astern))
        call.out((RIM, width), F32)
        call.out((RIM, width), F32)
        call.out((40, width), F32)
        call.out((16, 128), F32)
        call.temp((3, tile + 24, width), F32).temp((tile, width), F32).temp((136, channels), F32)
        return call.run(32)

    def input_back(m, kept, gate_back, fourth, span, rows, rim, chain, earlier, *waits):
        count = span[1] - span[0]
        turn = lambda i: i + span[0]
        put = lambda i: i + span[0] - rows[0]
        name = f"input_{m}_{span[0]}"
        call = Call(partial(input_kernel, tile, channels, bool(chain), rim is not None), count, name)
        call.blocks(
            (tokens, rows_in(m, model, turn)),
            (kept[0], rows_of(model, turn)),
            (gate_back, rows_of(channels, turn)),
            (fourth[0], rows_of(width + 256, turn)),
            (fourth[1], rows_of(128, turn)),
        )
        call.whole(weights)
        if rim is not None:
            call.whole(fourth[3], rim)
        call.whole(*chain)
        if earlier is not None:
            call.alias(earlier)
        call.after(*waits)
        call.out((rows[1] * tile, model), BF, rows_of(model, put))
        call.out((model, width + 256 + 128), F32)
        call.out((8, model), F32)
        call.temp((tile, channels + width + 256 + 128), BF)
        return call.run(3 + 1.5 * count)

    def input_all(m, kept, gate_back, fourth, rim, chain, pieces, waits, last_waits):
        outs = []
        size = steps // pieces
        for piece in range(pieces):
            rows = (piece * size, size)
            last = piece == pieces - 1
            most = input_back(
                m, kept, gate_back, fourth, (rows[0], rows[0] + size - last), rows, None, chain, None, *waits
            )
            waits, chain = [], most[1:3]
            if last:
                most = input_back(
                    m, kept, gate_back, fourth, (steps - 1, steps), rows, rim, chain, most[0], *last_waits
                )
                chain = most[1:3]
            outs.append(most[0])
        return outs, chain

    every = range(micro)
    kept, inner, mixes, thirds, order_by, chain = [], [], [], [], [], ()
    for m in every:
        kept.append(project(m, *order_by))
        order_by = [kept[m][8]]
    for m in every:
        inner.append(inside(m, kept[m], near_parts(kept[m][8], "seq", 1), *order_by))
        order_by = [inner[m][2]]
    for m in every:
        mixes.append(mix(m, kept[m], inner[m][0], inner[m][1], far_parts(inner[m][2], "seq", 1), *order_by))
        order_by = [mixes[m][1]]
    for m in every:
        stats = [mixes[m][1]] + [swap(mixes[m][1], "head", bits) for bits in range(1, lax.axis_size("head"))]
        thirds.append(norm(m, kept[m], mixes[m][0], inner[m][1], stats, chain, *order_by))
        chain = thirds[m][6:9]
        order_by = [thirds[m][5]]
    grad_out, grad_gate, gate_rows = chain
    early = lax.psum((grad_out, grad_gate), "seq")
    mixed_pair = [head_pair(thirds[m][0]) for m in every]
    mixed_all = [head_rest(mixed_pair[m]) for m in every]
    inner_b, fourths, token_pair, token_all, chain, chain_b = [], [], [], [], (), ()
    for m in every:
        inner_b.append(within(m, kept[m], thirds[m][2], near_parts(thirds[m][5], "seq", -1), *order_by))
        order_by = [inner_b[m][3], mixed_pair[m]]
    far_next = far_parts(inner_b[0][3], "seq", -1)
    for m in every:
        far = far_next
        if m + 1 < micro:
            far_next = far_parts(inner_b[m + 1][3], "seq", -1)
        fourths.append(across(m, kept[m], mixes[m][2], thirds[m], inner_b[m], far, chain, *order_by))
        chain = fourths[m][4:6]
        rim = from_behind(fourths[m][2], "seq", -1)
        waits = [mixed_all[m]] + (far_next if m + 1 < micro else [])
        pieces = 2 if m + 1 == micro and steps % 2 == 0 else 1
        outs, chain_b = input_all(
            m, kept[m], thirds[m][1], fourths[m], rim, chain_b, pieces, waits, [x for xs in token_all for x in xs]
        )
        token_pair.append([head_pair(out) for out in outs])
        token_all.append([head_rest(low) for low in token_pair[m]])
        order_by = [*token_pair[m]]
    tap_rows, head_rows = chain
    grads, gain_rows = chain_b

    grads, *token_pair[-1] = lax.optimization_barrier((grads, *token_pair[-1]))
    token_all[-1] = [head_rest(low) for low in token_pair[-1]]
    bc_high, bc_low = halves(grads[:, channels:width] + grads[:, width : width + 256])
    part = scatter_sum(
        jnp.concatenate([grads[:, :channels].astype(BF), bc_high, bc_low, grads[:, width + 256 :].astype(BF)], axis=1),
        "seq",
    )
    share = 2 * states // lax.axis_size("head")
    part, token_all[-1][0] = lax.optimization_barrier((part, token_all[-1][0]))
    bc_part = part[:, channels:width] + part[:, width : width + 256]
    bc_part = sum_rows([bc_part] + [swap(bc_part, "head", bits) for bits in range(1, lax.axis_size("head"))])
    bc_mine = lax.dynamic_slice_in_dim(bc_part, lax.axis_index("head") * share, share, 1)
    bc_mine, early = lax.optimization_barrier((bc_mine, early))
    gathered_low = gather_rows(
        jnp.concatenate(
            [part[:, :channels], bc_mine, part[:, width + 256 : width + 256 + heads],
             jnp.zeros((part.shape[0], 128 - share - heads), F32)], axis=1
        ).astype(BF),
        "seq",
    )
    gathered = gathered_low.astype(F32)
    grad_x = gathered[:, :channels]
    grad_bc = gathered[:, channels : channels + share]
    grad_dt = gathered[:, channels + share : channels + share + heads]

    side = lax.axis_index("head") % 2

    def half_of(value, m, begin, rows):
        return lax.dynamic_slice(value, (m, begin + side * rows, 0), (1, rows, model))[0].astype(F32)

    def place(result, m, begin, half):
        rows = half.shape[0]
        other = swap(half, "head", 1)
        result = lax.dynamic_update_slice(result, half[None], (m, begin + side * rows, 0))
        return lax.dynamic_update_slice(result, other[None], (m, begin + (1 - side) * rows, 0))

    mixed_out = jnp.zeros((micro, length, model), BF)
    for m in every:
        mixed_out = place(mixed_out, m, 0, (half_of(tokens, m, 0, length // 2) + mixed_all[m]).astype(BF))

    def finish_token(m, begin, grad_normed):
        rows = grad_normed.shape[0]
        x = half_of(tokens, m, begin, rows)
        scale = lax.rsqrt(jnp.mean(x * x, axis=1, keepdims=True) + EPS)
        grad_hat = grad_normed * norm_gain
        return (
            half_of(cotangent, m, begin, rows)
            + scale * grad_hat
            - x * scale**3 * jnp.mean(grad_hat * x, axis=1, keepdims=True)
        ).astype(BF)

    token_grad = jnp.zeros((micro, length, model), BF)
    for m in every:
        begin = 0
        for piece, grad_normed in enumerate(token_all[m]):
            if m + 1 == micro and piece + 1 == len(token_all[m]):
                grad_normed = lax.optimization_barrier((grad_normed, gathered_low))[0]
            token_grad = place(token_grad, m, begin, finish_token(m, begin, grad_normed))
            begin += 2 * grad_normed.shape[0]

    def folded(rows):
        return jnp.sum(rows.reshape(-1, 8, rows.shape[1]), axis=1)

    by_tap = folded(tap_rows)
    by_row = folded(gate_rows)
    by_head = folded(head_rows)[:, :heads]
    skip_sum = jnp.sum(by_row[1].reshape(heads, dim), axis=1)
    gain_sum = jnp.sum(gain_rows, axis=0)
    small = jnp.concatenate(
        [by_tap[:, channels:].reshape(-1), gain_sum,
         by_tap[:, :channels].reshape(-1), by_row[0], by_head.reshape(-1), skip_sum]
    )
    shared_size = by_tap[:, channels:].size + model
    small = jnp.pad(small, (0, -small.size % 1024)).reshape(-1, 128)
    small = all_sum(small, "seq")
    shared_rows = shared_size // 128
    shared = all_sum(small[:shared_rows], "head").reshape(-1)
    rest = small[shared_rows:].reshape(-1)
    tap_count = conv_x_weight.shape[0]
    bc_taps = shared[: (tap_count + 1) * 2 * states].reshape(tap_count + 1, 2 * states)
    grad_norm_gain = shared[(tap_count + 1) * 2 * states : shared_size]
    cut = (tap_count + 1) * channels
    x_taps = rest[:cut].reshape(tap_count + 1, channels)
    grad_gate_gain = rest[cut : cut + channels]
    tails = rest[cut + channels : cut + channels + 3 * heads].reshape(3, heads)
    return (
        mixed_out,
        token_grad,
        grad_norm_gain,
        jnp.stack([early[1], grad_x], axis=1),
        grad_bc,
        grad_dt,
        x_taps[:tap_count],
        x_taps[tap_count],
        bc_taps[:tap_count],
        bc_taps[tap_count],
        tails[0],
        tails[1] * decay_rate,
        tails[2],
        grad_gate_gain,
        early[0],
    )


def solution(mesh):
    in_specs = (
        P(None, "seq", None),
        P(),
        P(),
        P(None, None, "head"),
        P(),
        P(None, "head"),
        P(None, "head"),
        P("head"),
        P(),
        P(),
        P("head"),
        P("head"),
        P("head"),
        P("head"),
        P("head", None),
        P(None, "seq", None),
    )
    out_specs = (
        P(None, "seq", None),
        P(None, "seq", None),
        P(),
        P(None, None, "head"),
        P(None, "head"),
        P(None, "head"),
        P(None, "head"),
        P("head"),
        P(),
        P(),
        P("head"),
        P("head"),
        P("head"),
        P("head"),
        P("head", None),
    )
    return jax.shard_map(local, mesh=mesh, in_specs=in_specs, out_specs=out_specs, check_vma=False)
```

```python
from functools import partial

import jax
import jax.numpy as jnp
import numpy as np
from jax import lax
from jax.experimental import pallas as pl
from jax.experimental.pallas import tpu as pltpu
from jax.sharding import PartitionSpec as P

EPS = 1e-05
Q = 128
STATES = 128
TILE = 512
SMALL = 256
RIM = 16
NEVER = -1e30
TINY = 1e-37
BF = jnp.bfloat16
F32 = jnp.float32
VMEM_BYTES = 48 * 2**20
SCALE = 1.0
GAIN, TAPS, SHIFT, GATE, SKIP, RATE, BIAS, TABLE = 0, 1, 5, 6, 7, 8, 9, 16


def dot(a, b):
    return jnp.dot(a, b, preferred_element_type=F32)


def dot_nt(a, b):
    return lax.dot_general(a, b, (((1,), (1,)), ((), ())), preferred_element_type=F32)


def dot_tn(a, b):
    return lax.dot_general(a, b, (((0,), (0,)), ((), ())), preferred_element_type=F32)


def halves(value):
    high = value.astype(BF)
    return high, (value - high.astype(F32)).astype(BF)


def twice(value, axis):
    return jnp.concatenate([value, value], axis=axis)


def stacked(value, axis):
    return jnp.concatenate(halves(value), axis=axis)


def cut_rows(value, likes):
    pieces, at = [], 0
    for like in likes:
        pieces.append(value[at : at + like.shape[0]])
        at += like.shape[0]
    return pieces


def spread_heads(values, spread):
    both = stacked(jnp.concatenate(values, axis=0), 1)
    return cut_rows(dot(both, spread), values)


def gather_heads(values, gather):
    both = stacked(jnp.concatenate(values, axis=0), 1)
    return cut_rows(dot(both, gather), values)


def add_up(values, wedge):
    result = dot(wedge, jnp.concatenate([stacked(value, 0) for value in values], axis=1))
    return [result[:, 128 * c : 128 * c + 128] for c in range(len(values))]


def near_f32(left, right):
    rows, columns = left.shape[0], right.shape[0]
    product = dot_nt(stacked(left, 0), stacked(right, 0))
    return product[:rows, :columns] + product[:rows, columns:] + product[rows:, :columns]


def sigmoid(value):
    return jax.nn.sigmoid(value)


def softplus(value):
    return jnp.maximum(value, 0.0) + jnp.log1p(jnp.exp(-jnp.abs(value)))


def iota(shape, axis):
    return lax.broadcasted_iota(jnp.int32, shape, axis)


class Docs:
    def __init__(self, meta, m):
        self.count = meta.shape[1] - 1
        self.starts = [meta[m, j] for j in range(self.count)]
        self.anchor = meta[m, self.count]

    def counts(self, places):
        total = (places >= self.starts[0]).astype(jnp.int32)
        for start in self.starts[1:]:
            total = total + (places >= start).astype(jnp.int32)
        return total

    def starts_at(self, places):
        hit = places == self.starts[0]
        for start in self.starts[1:]:
            hit = hit | (places == start)
        return hit

    def tap_masks(self, first, rows):
        places = first + iota((rows, 128), 0)
        masks = []
        broken = None
        for back in range(3):
            hit = self.starts_at(places - back)
            broken = hit if broken is None else broken | hit
            masks.append(jnp.where(broken, 0.0, 1.0))
        return masks


class Tile:
    def __init__(self, docs, first, deltas, rate, wedge):
        count = deltas.shape[0] // Q
        self.docs, self.first = docs, first
        self.parts = [slice(Q * c, Q * c + Q) for c in range(count)]
        self.deltas = [deltas[rows] for rows in self.parts]
        runs = add_up([part * rate for part in self.deltas], wedge)
        self.run = runs
        self.total = [run[Q - 1 : Q] for run in runs]
        self.before = [docs.counts(first + Q * c - 1) for c in range(count)]
        self.last = [docs.counts(first + Q * c + Q - 1) for c in range(count)]
        self.column = [docs.counts(first + Q * c + iota((Q, 128), 0)) for c in range(count)]

    def same(self, c):
        return self.column[c] == self.docs.counts(self.first + Q * c + iota((8, 128), 1))[0:1]

    def entry(self, c):
        return jnp.exp(self.run[c] + jnp.where(self.column[c] == self.before[c], 0.0, NEVER))

    def leaving(self, c):
        bias = jnp.where(self.column[c] == self.last[c], 0.0, NEVER)
        return jnp.exp(self.total[c] - self.run[c] + bias) * self.deltas[c]

    def overall(self, c):
        return jnp.exp(self.total[c] + jnp.where(self.last[c] == self.before[c], 0.0, NEVER))


def wide_row(row):
    return jnp.broadcast_to(row, (8, row.shape[1]))


def pair_blocks(value, pair, lanes):
    both = value[:, 128 * pair : 128 * pair + 128]
    zero = jnp.zeros_like(both)
    return jnp.concatenate([jnp.where(lanes, both, zero), jnp.where(lanes, zero, both)], axis=0)


def first_kernel(
    tile, channels,
    meta, rim, tokens, weights, table, spread, wedge, *rest, m,
):
    normed_o, gate_o, xbc_o, pre_o, conv_o, deltas_o, held_o, sums_o, leaving_o, edge_o, ext, state, total = rest[-13:]
    step = pl.program_id(0)
    docs = Docs(meta, m)
    width = xbc_o.shape[1]
    taps = table[TAPS : TAPS + 4, :width]
    shift = table[SHIFT : SHIFT + 1, :width]
    gain = table[GAIN : GAIN + 1, : tokens.shape[1]]
    rate = table[RATE : RATE + 1, :128]
    dt_bias = table[BIAS : BIAS + 1, :128]

    def normalize(rows):
        x = rows.astype(F32)
        scale = lax.rsqrt(jnp.mean(x * x, axis=1, keepdims=True) + EPS)
        return (x * scale * gain).astype(BF)

    @pl.when(step == 0)
    def _():
        edge = dot(normalize(rim[...]), weights[:, channels : channels + width]).astype(BF)
        edge_o[...] = edge
        ext[0:8, :] = edge.astype(F32)[RIM - 8 :]
        state[...] = jnp.zeros_like(state)
        total[...] = jnp.zeros_like(total)

    @pl.when(step > 0)
    def _():
        ext[0:8, :] = ext[tile : tile + 8, :]

    normed = normalize(tokens[...])
    normed_o[...] = normed
    gate_o[...] = dot(normed, weights[:, :channels])
    xbc = dot(normed, weights[:, channels : channels + width]).astype(BF)
    xbc_o[...] = xbc
    ext[8:, :] = xbc.astype(F32)
    deltas = softplus(dot(normed, weights[:, channels + width + 256 :]) + dt_bias)
    deltas_o[...] = deltas
    first = docs.anchor + step * tile
    masks = docs.tap_masks(first, tile)
    for slab in range(width // 128):
        lanes = slice(128 * slab, 128 * slab + 128)
        pre = shift[:, lanes] + taps[3:4, lanes] * ext[8 : 8 + tile, lanes]
        for back in range(1, 4):
            pre = pre + taps[3 - back : 4 - back, lanes] * ext[8 - back : 8 - back + tile, lanes] * masks[back - 1]
        pre_o[:, lanes] = pre.astype(BF)
        conv_o[:, lanes] = (pre * sigmoid(pre)).astype(BF)
    parts = Tile(docs, first, deltas, rate, wedge[...])
    count = len(parts.parts)
    wide = spread_heads(
        [parts.leaving(c) for c in range(count)] + [wide_row(parts.overall(c)) for c in range(count)], spread[...]
    )
    for c, rows in enumerate(parts.parts):
        held_o[c] = state[...]
        sums_o[c] = total[...]
        total[...] = total[...] + parts.total[c]
        writes = conv_o[rows, channels : channels + 128]
        scaled = conv_o[rows, :channels].astype(F32) * wide[c]
        state[...] = state[...] * wide[count + c][0:1] + dot_tn(twice(writes, 0), stacked(scaled, 0))

    @pl.when(step == pl.num_programs(0) - 1)
    def _():
        end = docs.anchor + (step + 1) * tile - 1
        through = jnp.where(docs.counts(end) == docs.counts(docs.anchor - 1), 0.0, NEVER)
        leaving_o[...] = packed(state[...], spread_heads([jnp.exp(total[...] + through)], spread[...])[0][0:1])


def inside_kernel(
    tile, channels,
    meta, conv, deltas, table, wedge, *rest, m, sources,
):
    mixed_o, near_o, send_o = rest[-3:]
    step = pl.program_id(0)

    @pl.when(step == 0)
    def _():
        state, decay = joined([part[...] for part in rest[:sources]])
        near_o[:STATES, :] = state
        near_o[STATES:, :] = jnp.broadcast_to(decay, (8, channels))
        send_o[...] = packed(state, decay)

    docs = Docs(meta, m)
    first = docs.anchor + step * tile
    lanes_q = iota((Q, 128), 1)
    causal = iota((Q, Q), 0) >= iota((Q, Q), 1)
    low = lanes_q < 64
    skip = table[SKIP : SKIP + 1, :channels]
    rate = table[RATE : RATE + 1, :128]
    parts = Tile(docs, first, deltas[...], rate, wedge[...])
    for c, rows in enumerate(parts.parts):
        u = conv[rows, :channels]
        writes = conv[rows, channels : channels + 128]
        reads = conv[rows, channels + 128 :]
        scores = dot_nt(reads, writes)
        run = parts.run[c]
        bias = jnp.where(parts.same(c) & causal, 0.0, NEVER)
        behind = jnp.transpose(jnp.log(jnp.maximum(parts.deltas[c], TINY)) - run)
        pieces = []
        for pair in range(channels // 128):
            both = []
            for head in (2 * pair, 2 * pair + 1):
                decay = jnp.exp(run[:, head : head + 1] + behind[head : head + 1] + bias)
                both.append((decay * scores).astype(BF))
            pieces.append(dot(jnp.concatenate(both, axis=1), pair_blocks(u, pair, low)))
        mixed_o[rows, :] = jnp.concatenate(pieces, axis=1) + skip * u.astype(F32)


def mix_kernel(
    tile, channels,
    meta, inside, conv, deltas, gate, held, sums, cotangent, out_weight, table, spread, wedge, *rest, m, sources,
):
    mixed_o, stats_o, carry = rest[-3:]
    step = pl.program_id(0)

    @pl.when(step == 0)
    def _():
        carry[...] = joined([part[...] for part in rest[:sources]])[0]

    back = dot_nt(cotangent[...], out_weight[...]) * table[GATE : GATE + 1, :channels]
    docs = Docs(meta, m)
    first = docs.anchor + step * tile
    lanes_q = iota((Q, 128), 1)
    rate = table[RATE : RATE + 1, :128]
    parts = Tile(docs, first, deltas[...], rate, wedge[...])
    count = len(parts.parts)
    start = docs.counts(docs.anchor - 1)
    arrived = [jnp.exp(sums[c] + jnp.where(parts.before[c] == start, 0.0, NEVER)) for c in range(count)]
    wide = spread_heads([parts.entry(c) for c in range(count)] + arrived, spread[...])
    for c, rows in enumerate(parts.parts):
        reads = conv[rows, channels + 128 :]
        state = stacked(held[c] + wide[count + c][0:1] * carry[...], 0)
        mixed = inside[rows, :] + dot(twice(reads, 1), state) * wide[c]
        mixed_o[rows, :] = mixed
        gate_rows = gate[rows, :]
        gated = mixed * gate_rows * sigmoid(gate_rows)
        squares = jnp.sum(gated * gated, axis=1, keepdims=True)
        inner = jnp.sum(gated * back[rows], axis=1, keepdims=True)
        columns = jnp.where(lanes_q == 0, squares, jnp.where(lanes_q == 1, inner, 0.0))
        stats_o[:, rows] = jnp.transpose(columns)[0:8]


def third_kernel(
    tile, channels, full, chained,
    meta, mixed, gate, conv, deltas, normed, cotangent, out_weight, table, spread, wedge,
    stats_a, stats_b, stats_c, stats_d, *rest, m,
):
    if chained:
        grad_out_i, grad_gate_i, rows_i, *rest = rest
    branch_o, gate_back_o, ssd_back_o, held_o, sums_o, leaving_o, grad_out, grad_gate, rows_o, state, total = rest[-11:]
    step = pl.program_id(0)
    gate_gain = table[GATE : GATE + 1, :channels]
    rate = table[RATE : RATE + 1, :128]
    docs = Docs(meta, m)
    place = pl.num_programs(0) - 1 - step
    first = docs.anchor + place * tile

    @pl.when(step == 0)
    def _():
        state[...] = jnp.zeros_like(state)
        total[...] = jnp.zeros_like(total)
        if chained:
            grad_out[...] = grad_out_i[...]
            grad_gate[...] = grad_gate_i[...]
            rows_o[...] = rows_i[...]
        else:
            grad_out[...] = jnp.zeros_like(grad_out)
            grad_gate[...] = jnp.zeros_like(grad_gate)
            rows_o[...] = jnp.zeros_like(rows_o)

    stats = stats_a[...] + stats_b[...] + stats_c[...] + stats_d[...]
    branches = []
    back = dot_nt(cotangent[...], out_weight[...])
    parts = Tile(docs, first, deltas[...], rate, wedge[...])
    count = len(parts.parts)
    wide = spread_heads(
        [parts.entry(c) for c in range(count)] + [wide_row(parts.overall(c)) for c in range(count)], spread[...]
    )
    for c in reversed(range(count)):
        rows = parts.parts[c]
        sides = jnp.transpose(jnp.concatenate([stats[:, rows], jnp.zeros((120, Q), F32)], axis=0))
        scale = lax.rsqrt(sides[:, 0:1] / full + EPS)
        inner = sides[:, 1:2]
        mixed_rows = mixed[rows, :]
        gate_rows = gate[rows, :]
        sigma = sigmoid(gate_rows)
        act = gate_rows * sigma
        gated = mixed_rows * act
        unit = gated * scale
        branch = (unit * gate_gain).astype(BF)
        branches.append(branch)
        back_rows = back[rows]
        grad_gated = scale * (back_rows * gate_gain) - unit * (scale * scale * (inner / full))
        grad_mixed = grad_gated * act
        gate_back_o[rows, :] = (grad_gated * mixed_rows * (sigma * (1.0 + gate_rows * (1.0 - sigma)))).astype(BF)
        ssd_back = grad_mixed.astype(BF)
        ssd_back_o[rows, :] = ssd_back
        u = conv[rows, :channels].astype(F32)
        rows_o[0:8, :] += jnp.sum((back_rows * unit).reshape(Q // 8, 8, channels), axis=0)
        rows_o[8:16, :] += jnp.sum((grad_mixed * u).reshape(Q // 8, 8, channels), axis=0)
        held_o[c] = state[...]
        sums_o[c] = total[...]
        total[...] = total[...] + parts.total[c]
        reads = conv[rows, channels + 128 :]
        entered = stacked(ssd_back.astype(F32) * wide[c], 0)
        state[...] = state[...] * wide[count + c][0:1] + dot_tn(twice(reads, 0), entered)
    branch = jnp.concatenate(branches[::-1], axis=0)
    branch_o[...] = dot(branch, out_weight[...]).astype(BF)
    grad_out[...] += dot_tn(branch, cotangent[...])
    grad_gate[...] += dot_tn(normed[...], gate_back_o[...])

    @pl.when(step == pl.num_programs(0) - 1)
    def _():
        end = docs.anchor + pl.num_programs(0) * tile - 1
        through = jnp.where(docs.counts(end) == docs.counts(docs.anchor - 1), 0.0, NEVER)
        leaving_o[...] = packed(state[...], spread_heads([jnp.exp(total[...] + through)], spread[...])[0][0:1])


def within_kernel(
    tile, channels,
    meta, conv, deltas, ssd_back, table, wedge, *rest, m, sources,
):
    grads_o, ends_o, near_o, send_o = rest[-4:]
    step = pl.program_id(0)

    @pl.when(step == 0)
    def _():
        state, decay = joined([part[...] for part in rest[:sources]])
        near_o[:STATES, :] = state
        near_o[STATES:, :] = jnp.broadcast_to(decay, (8, channels))
        send_o[...] = packed(state, decay)

    docs = Docs(meta, m)
    first = docs.anchor + step * tile
    lanes_q = iota((Q, 128), 1)
    rows_16 = iota((16, 128), 0)
    causal = iota((Q, Q), 1) >= iota((Q, Q), 0)
    low = lanes_q < 64
    skip = table[SKIP : SKIP + 1, :channels]
    rate = table[RATE : RATE + 1, :128]
    parts = Tile(docs, first, deltas[...], rate, wedge[...])
    for c, rows in enumerate(parts.parts):
        u = conv[rows, :channels]
        writes = conv[rows, channels : channels + 128]
        reads = conv[rows, channels + 128 :]
        grad = ssd_back[rows, :]
        scores = dot_nt(writes, reads)
        bias = jnp.where(parts.same(c) & causal, 0.0, NEVER)
        ahead = jnp.transpose(parts.run[c])
        behind = jnp.log(jnp.maximum(parts.deltas[c], TINY)) - parts.run[c]
        grad_scores = jnp.zeros((Q, Q), F32)
        by_source = jnp.zeros((Q, 128), F32)
        by_target = jnp.zeros((16, 128), F32)
        pieces = []
        for pair in range(channels // 128):
            blocks = pair_blocks(grad, pair, low)
            meets = dot_nt(u[:, 128 * pair : 128 * pair + 128], blocks)
            both = []
            for side in range(2):
                head = 2 * pair + side
                decay = jnp.exp(behind[:, head : head + 1] + ahead[head : head + 1] + bias)
                both.append((decay * scores).astype(BF))
                weighed = decay * meets[:, Q * side : Q * side + Q]
                grad_scores = grad_scores + weighed
                pairs = weighed * scores
                by_source = jnp.where(lanes_q == head, jnp.sum(pairs, axis=1, keepdims=True), by_source)
                by_target = jnp.where(rows_16 == head + 8, jnp.sum(pairs, axis=0, keepdims=True), by_target)
            pieces.append(dot(jnp.concatenate(both, axis=1), blocks))
        ends_o[rows, :] = by_source + jnp.transpose(jnp.concatenate([by_target, jnp.zeros((112, Q), F32)], axis=0))
        high, low_part = halves(grad_scores)
        grads_o[rows, :channels] = jnp.concatenate(pieces, axis=1) + skip * grad.astype(F32)
        grads_o[rows, channels : channels + 128] = dot(jnp.concatenate([high, low_part], axis=1), twice(reads, 0))
        grads_o[rows, channels + 128 :] = dot_tn(jnp.concatenate([high, low_part], axis=0), twice(writes, 0))


def across_kernel(
    tile, channels, chained,
    meta, conv, pre, xbc, edge, deltas, ssd_back, inside, ends,
    held, sums, carry, held_b, sums_b,
    table, spread, gather, wedge, wedge_up, wedge_below, *rest, m, sources,
):
    far, rest = rest[:sources], rest[sources:]
    if chained:
        taps_i, heads_i, *rest = rest
    in_back_o, dt_back_o, rim_o, tail_o, taps_o, heads_o, ext, grads, carry_b = rest[-9:]
    step = pl.program_id(0)
    docs = Docs(meta, m)
    places = pl.num_programs(0)
    place = places - 1 - step
    first = docs.anchor + place * tile
    end = docs.anchor + places * tile - 1
    width = pre.shape[1]
    taps = table[TAPS : TAPS + 4, :width]
    rate = table[RATE : RATE + 1, :128]
    lanes_q = iota((Q, 128), 1)

    @pl.when(step == 0)
    def _():
        if chained:
            taps_o[...] = taps_i[...]
            heads_o[...] = heads_i[...]
        else:
            taps_o[...] = jnp.zeros_like(taps_o)
            heads_o[...] = jnp.zeros_like(heads_o)
        carry_b[...] = joined([part[...] for part in far])[0]
        ext[:, 0:16, :] = jnp.zeros_like(ext[:, 0:16, :])
        ext[:, 16 + tile :, :] = jnp.zeros_like(ext[:, 16 + tile :, :])

    @pl.when(step > 0)
    def _():
        ext[:, 16 + tile :, :] = ext[:, 16:24, :]

    parts = Tile(docs, first, deltas[...], rate, wedge[...])
    count = len(parts.parts)
    start, stop = docs.counts(docs.anchor - 1), docs.counts(end)
    each = range(count)
    arrived = [jnp.exp(sums[c] + jnp.where(parts.before[c] == start, 0.0, NEVER)) for c in each]
    arrived_b = [jnp.exp(sums_b[c] + jnp.where(parts.last[c] == stop, 0.0, NEVER)) for c in each]
    wide = spread_heads(
        [parts.entry(c) for c in each] + [parts.leaving(c) for c in each] + arrived + arrived_b, spread[...]
    )
    crossings, products = [], []
    for c, rows in enumerate(parts.parts):
        u = conv[rows, :channels].astype(F32)
        writes = conv[rows, channels : channels + 128]
        reads = conv[rows, channels + 128 :]
        outward = wide[count + c]
        state = held[c] + wide[2 * count + c][0:1] * carry[...]
        state_b = held_b[c] + wide[3 * count + c][0:1] * carry_b[...]
        grad_in = ssd_back[rows, :].astype(F32) * wide[c]
        crossing = dot(twice(writes, 1), stacked(state_b, 0)) * outward
        products.append(u * crossing)
        crossings.append(grad_in * dot(twice(reads, 1), stacked(state, 0)))
        products.append(jnp.sum((state * state_b).reshape(16, 8, channels), axis=0))
        grads[rows, :channels] = inside[rows, :channels] + crossing
        grads[rows, channels : channels + 128] = inside[rows, channels : channels + 128] + near_f32(u * outward, state_b)
        grads[rows, channels + 128 :] = inside[rows, channels + 128 :] + near_f32(grad_in, state)
    gathered = gather_heads(crossings + products, gather[...])
    in_parts, out_parts = gathered[:count], gathered[count : count + 2 * count : 2]
    ups, sources = [], []
    for c, rows in enumerate(parts.parts):
        both_ends = ends[rows, :]
        sources.append(jnp.where(lanes_q < 8, both_ends, 0.0))
        target = jnp.where(lanes_q < 8, pltpu.roll(both_ends, 120, 1), 0.0)
        ups.append(in_parts[c] + target - sources[c])
    ups = add_up(ups, wedge_up[...])
    belows = add_up(out_parts, wedge_below[...])
    for c, rows in enumerate(parts.parts):
        between = jnp.sum(gathered[count + 2 * c + 1], axis=0, keepdims=True) * parts.overall(c)
        grad_run = between + ups[c] + belows[c]
        part_deltas = parts.deltas[c]
        slope = 1.0 - jnp.exp(-part_deltas)
        ratio = jnp.where(part_deltas > 1e-6, slope / jnp.maximum(part_deltas, 1e-6), 1.0)
        dt_back = (sources[c] + out_parts[c]) * ratio + rate * grad_run * slope
        dt_back_o[rows, :] = dt_back.astype(BF)
        heads_o[0:8, :] += jnp.sum(dt_back.reshape(Q // 8, 8, 128), axis=0)
        heads_o[8:16, :] += jnp.sum((grad_run * part_deltas).reshape(Q // 8, 8, 128), axis=0)

    masks = docs.tap_masks(first, tile)
    for slab in range(width // 128):
        lanes = slice(128 * slab, 128 * slab + 128)
        pre_rows = pre[:, lanes].astype(F32)
        sigma = sigmoid(pre_rows)
        grad_pre = grads[:, lanes] * (sigma * (1.0 + pre_rows * (1.0 - sigma)))
        source = xbc[:, lanes].astype(F32)
        result = taps[3:4, lanes] * grad_pre
        taps_o[24:32, lanes] += jnp.sum((grad_pre * source).reshape(tile // 8, 8, 128), axis=0)
        taps_o[32:40, lanes] += jnp.sum(grad_pre.reshape(tile // 8, 8, 128), axis=0)
        for back in range(1, 4):
            ext[back - 1, 16 : 16 + tile, lanes] = grad_pre * masks[back - 1]
            moved = ext[back - 1, 16 + back : 16 + back + tile, lanes]
            result = result + taps[3 - back : 4 - back, lanes] * moved
            taps_o[8 * (3 - back) : 8 * (4 - back), lanes] += jnp.sum((moved * source).reshape(tile // 8, 8, 128), axis=0)
        high = result.astype(BF)
        in_back_o[:, lanes] = high
        if 128 * slab >= channels:
            in_back_o[:, slice(256 + 128 * slab, 384 + 128 * slab)] = (result - high.astype(F32)).astype(BF)

        @pl.when(step == 0)
        def _():
            tail_o[:, lanes] = result[tile - RIM :]

    @pl.when(place == 0)
    def _():
        total = jnp.zeros((RIM, width), F32)
        source = edge[...].astype(F32)
        for back in range(1, 4):
            moved = ext[back - 1, back : back + RIM, :]
            total = total + taps[3 - back : 4 - back, :] * moved
            taps_o[8 * (3 - back) : 8 * (4 - back), :] += jnp.sum((moved * source).reshape(RIM // 8, 8, width), axis=0)
        rim_o[...] = total


def part_kernel(
    tile, channels, chained, last, tiles,
    tokens, gate_back, in_back, dt_back, weights, *rest,
):
    if last:
        tail, rim, *rest = rest
    if chained:
        rows_i, *rest = rest
    part_o, rows_o, every = rest[-3:]
    step = pl.program_id(0)
    wide = in_back.shape[1]
    width = wide - 256

    @pl.when(step == 0)
    def _():
        rows_o[...] = rows_i[...] if chained else jnp.zeros_like(rows_o)

    every[:, :channels] = gate_back[...]
    every[:, channels : channels + wide] = in_back[...]
    every[:, channels + wide :] = dt_back[...]
    if last:

        @pl.when(step == tiles - 1)
        def _():
            high, low = halves(tail[...] + rim[...])
            every[tile - RIM :, channels : channels + width] = high
            every[tile - RIM :, channels + width : channels + wide] = low[:, channels:]

    x = tokens[...].astype(F32)
    scale = lax.rsqrt(jnp.mean(x * x, axis=1, keepdims=True) + EPS)
    part = dot_nt(every[...], weights[...])
    part_o[...] = part.astype(BF)
    rows_o[...] += jnp.sum((part * (x * scale)).reshape(tile // 8, 8, x.shape[1]), axis=0)


def weight_kernel(
    tile, channels, chained, tiles,
    normed, in_back, dt_back, tail, rim, *rest,
):
    if chained:
        grads_i, dt_i, *rest = rest
    grads_o, dt_o, every, total, dt_total = rest[-5:]
    step = pl.program_id(0)
    wide = in_back.shape[1]
    width = wide - 256

    @pl.when(step == 0)
    def _():
        total[...] = grads_i[...] if chained else jnp.zeros_like(total)
        dt_total[...] = jnp.zeros_like(dt_total)

    every[...] = in_back[...]

    @pl.when(step == tiles - 1)
    def _():
        high, low = halves(tail[...] + rim[...])
        every[tile - RIM :, :width] = high
        every[tile - RIM :, width:] = low[:, channels:]

    turned = jnp.transpose(normed[...])
    total[:, :channels] += dot(turned, every[:, :channels])
    total[:, channels:] += dot(
        twice(turned, 1), jnp.concatenate([every[:, channels:width], every[:, width:]], axis=0)
    )
    dt_total[...] += dot_nt(jnp.transpose(dt_back[...]), turned)

    @pl.when(step == tiles - 1)
    def _():
        grads_o[...] = total[...].astype(grads_o.dtype)
        dt_o[...] = dt_total[0:8] + dt_i[...] if chained else dt_total[0:8]


def place_kernel(
    token,
    side, mine, other, tokens, *rest,
):
    if token:
        cotangent, table, *rest = rest
    out = rest[-1]
    step = pl.program_id(0)

    def finish(total):
        x = tokens[...].astype(F32)
        total = total.astype(F32)
        if not token:
            return (x + total).astype(BF)
        scale = lax.rsqrt(jnp.mean(x * x, axis=1, keepdims=True) + EPS)
        grad_hat = total * table[GAIN : GAIN + 1, :]
        inner = jnp.mean(grad_hat * x, axis=1, keepdims=True)
        return (cotangent[...].astype(F32) + scale * grad_hat - x * (scale * scale * scale * inner)).astype(BF)

    here = step // (pl.num_programs(0) // 2) == side[0]

    @pl.when(here)
    def _():
        out[...] = finish(mine[...])

    @pl.when(jnp.logical_not(here))
    def _():
        out[...] = finish(other[...])


class Call:
    def __init__(self, kernel, steps, name):
        self.kernel, self.steps, self.name = kernel, steps, name
        self.args, self.in_specs, self.outs, self.out_specs, self.scratch = [], [], [], [], []
        self.aliases = {}

    def whole(self, *arrays):
        for array in arrays:
            self.args.append(array)
            self.in_specs.append(pl.BlockSpec(array.shape, lambda i, rank=array.ndim: (0,) * rank))
        return self

    def scalars(self, array):
        self.args.append(array)
        self.in_specs.append(pl.BlockSpec(memory_space=pltpu.SMEM))
        return self

    def blocks(self, *arrays_specs):
        for array, spec in arrays_specs:
            self.args.append(array)
            self.in_specs.append(spec)
        return self

    def out(self, shape, dtype, spec=None):
        self.outs.append(jax.ShapeDtypeStruct(shape, dtype))
        self.out_specs.append(spec or pl.BlockSpec(shape, lambda i, rank=len(shape): (0,) * rank))
        return self

    def after(self, *arrays):
        for array in arrays:
            self.args.append(array)
            self.in_specs.append(pl.BlockSpec(memory_space=pl.ANY))
        return self

    def alias(self, array):
        self.aliases = {len(self.args): 0}
        return self.after(array)

    def temp(self, shape, dtype):
        self.scratch.append(pltpu.VMEM(shape, dtype))
        return self

    def run(self, micros, scalars=None):
        ahead = () if scalars is None else (scalars,)
        return pl.pallas_call(
            self.kernel,
            grid_spec=pltpu.PrefetchScalarGridSpec(
                num_scalar_prefetch=len(ahead),
                grid=(self.steps,),
                in_specs=self.in_specs,
                out_specs=tuple(self.out_specs),
                scratch_shapes=self.scratch,
            ),
            out_shape=tuple(self.outs),
            input_output_aliases={at + len(ahead): to for at, to in self.aliases.items()},
            compiler_params=pltpu.CompilerParams(
                dimension_semantics=("arbitrary",), vmem_limit_bytes=VMEM_BYTES
            ),
            cost_estimate=pl.CostEstimate(flops=int(micros * SCALE * 1.15e9), bytes_accessed=0, transcendentals=0),
            name=self.name,
        )(*ahead, *self.args)


def swap(value, axis, bits):
    count = lax.axis_size(axis)
    return lax.ppermute(value, axis, [(i, i ^ bits) for i in range(count)])


def from_behind(value, axis, steps):
    count = lax.axis_size(axis)
    sources = range(max(0, -steps), min(count, count - steps))
    return lax.ppermute(value, axis, [(i, i + steps) for i in sources])


def packed(state, decay):
    high, low = halves(jnp.broadcast_to(decay, (8, decay.shape[1])))
    return jnp.concatenate([state.astype(BF), high, low], axis=0)


def unpacked(part):
    if part.dtype == F32:
        return part[:STATES], part[STATES : STATES + 1]
    part = part.astype(F32)
    return part[:STATES], part[STATES : STATES + 1] + part[STATES + 8 : STATES + 9]


def joined(parts):
    state, decay = unpacked(parts[0])
    for part in parts[1:]:
        more, keep = unpacked(part)
        state = state + decay * more
        decay = decay * keep
    return state, decay


def near_parts(leaving, axis, sign):
    return [from_behind(leaving, axis, sign * k) for k in range(1, min(4, lax.axis_size(axis)))]


def far_parts(carry, sent, axis, sign):
    count = lax.axis_size(axis)
    window = 3
    parts = [carry]
    while window < count - 1:
        if len(parts) > 1:
            state, decay = joined(parts)
            sent = packed(state, decay)
            carry = jnp.concatenate([state, jnp.broadcast_to(decay, (8, decay.shape[1]))], axis=0)
        parts = [carry] + [from_behind(sent, axis, sign * k) for k in (window, 2 * window) if k < count]
        window *= 3
    return parts


def sum_rows(parts):
    total = parts[0].astype(F32)
    for part in parts[1:]:
        total = total + part.astype(F32)
    return total


def head_pair(part):
    rows = part.shape[0] // 2
    side = lax.axis_index("head") % 2
    mine = lax.dynamic_slice_in_dim(part, side * rows, rows, 0)
    other = lax.dynamic_slice_in_dim(part, (1 - side) * rows, rows, 0)
    return (mine.astype(F32) + swap(other, "head", 1).astype(F32)).astype(BF)


def head_rest(low):
    total = low.astype(F32)
    bit = 2
    while bit < lax.axis_size("head"):
        low = total.astype(BF)
        total = low.astype(F32) + swap(low, "head", bit).astype(F32)
        bit *= 2
    return total


def pair_parts(value, axis):
    rows = value.shape[0] // 2
    half = lax.axis_index(axis) % 2
    mine = lax.dynamic_slice_in_dim(value, half * rows, rows, 0)
    return mine, swap(lax.dynamic_slice_in_dim(value, (1 - half) * rows, rows, 0), axis, 1)


def scatter_parts(value, axis):
    count = lax.axis_size(axis) // 2
    me = lax.axis_index(axis) // 2
    rows = value.shape[0] // count
    parts = [lax.dynamic_slice_in_dim(value, me * rows, rows, 0)]
    for bits in range(1, count):
        piece = lax.dynamic_slice_in_dim(value, jnp.bitwise_xor(me, bits) * rows, rows, 0)
        parts.append(swap(piece, axis, 2 * bits))
    return parts


def gather_half(value, axis):
    count = lax.axis_size(axis) // 2
    me = lax.axis_index(axis) // 2
    rows = value.shape[0]
    result = jnp.zeros((count * rows, value.shape[1]), value.dtype)
    result = lax.dynamic_update_slice_in_dim(result, value, me * rows, 0)
    for bits in range(1, count):
        result = lax.dynamic_update_slice_in_dim(
            result, swap(value, axis, 2 * bits), jnp.bitwise_xor(me, bits) * rows, 0
        )
    return result


def gather_pair(half, axis):
    other = swap(half, axis, 1)
    first = lax.axis_index(axis) % 2 == 0
    return jnp.concatenate([jnp.where(first, half, other), jnp.where(first, other, half)], axis=0)


def all_sum(value, axis):
    bit = 1
    while bit < lax.axis_size(axis):
        value = value + swap(value, axis, bit)
        bit *= 2
    return value


def local(
    tokens,
    doc_starts,
    norm_gain,
    gate_x_weight,
    bc_weight,
    dt_weight,
    conv_x_weight,
    conv_x_bias,
    conv_bc_weight,
    conv_bc_bias,
    dt_bias,
    a_log,
    d_skip,
    gate_gain,
    out_weight,
    cotangent,
):
    micro, length, model = tokens.shape
    channels = gate_x_weight.shape[2]
    heads = dt_weight.shape[1]
    dim = channels // heads
    states = bc_weight.shape[1] // 2
    width = channels + 2 * states
    full = channels * lax.axis_size("head")
    tile, small = min(TILE, length), min(SMALL, length)
    steps = length // tile
    per = tile // Q
    blocks = length // Q

    rim_tokens = from_behind(tokens[:, length - RIM :], "seq", 1)
    weights = jnp.concatenate(
        [gate_x_weight[:, 0], gate_x_weight[:, 1], bc_weight, bc_weight,
         jnp.pad(dt_weight, ((0, 0), (0, 128 - heads)))], axis=1
    )
    decay_rate = -jnp.exp(a_log)

    def table_rows(*parts):
        row = jnp.concatenate(parts, axis=-1)
        row = row if row.ndim == 2 else row[None]
        return jnp.pad(row, ((0, 0), (0, model - row.shape[1])))

    table = jnp.concatenate(
        [
            table_rows(norm_gain),
            table_rows(conv_x_weight, conv_bc_weight),
            table_rows(conv_x_bias, conv_bc_bias),
            table_rows(gate_gain),
            table_rows(jnp.repeat(d_skip, dim)),
            table_rows(decay_rate),
            table_rows(dt_bias, jnp.full((128 - heads,), -200.0, F32)),
            jnp.zeros((TABLE - BIAS - 1, model), F32),
        ],
        axis=0,
    )
    owner = np.arange(channels)[None, :] // dim == np.arange(128)[:, None]
    spread = np.concatenate([owner, owner], axis=0).astype(BF)
    gather = np.concatenate([owner.T, owner.T], axis=0).astype(BF)
    order = np.arange(Q)
    until_here = order[:, None] >= order[None, :]
    below = order[:, None] > order[None, :]
    wedge = np.concatenate([until_here] * 2, axis=1).astype(BF)
    wedge_up = np.concatenate([until_here.T] * 2, axis=1).astype(BF)
    wedge_below = np.concatenate([below] * 2, axis=1).astype(BF)
    anchor = lax.axis_index("seq") * length
    meta = jnp.concatenate(
        [jnp.where(doc_starts >= 1, doc_starts, 2**30), jnp.full((micro, 1), anchor)], axis=1
    ).astype(jnp.int32)

    ahead = lambda i: i
    astern = lambda i: steps - 1 - i

    def rows_of(cols, turn, rows=tile):
        return pl.BlockSpec((rows, cols), lambda i: (turn(i), 0))

    def rows_in(m, cols, turn):
        return pl.BlockSpec((None, tile, cols), lambda i: (m, turn(i), 0))

    def chunks_of(turn, rows, cols):
        return pl.BlockSpec((per, rows, cols), lambda i: (turn(i), 0, 0))

    def stat_spec(turn):
        return pl.BlockSpec((8, tile), lambda i: (0, turn(i)))

    def project(m, *waits):
        call = Call(partial(first_kernel, tile, channels, m=m), steps, f"project_{m}")
        call.scalars(meta)
        call.blocks((rim_tokens, pl.BlockSpec((None, RIM, model), lambda i: (m, 0, 0))))
        call.blocks((tokens, rows_in(m, model, ahead)))
        call.whole(weights, table, spread, wedge).after(*waits)
        call.out((length, model), BF, rows_of(model, ahead))
        call.out((length, channels), F32, rows_of(channels, ahead))
        call.out((length, width), BF, rows_of(width, ahead))
        call.out((length, width), BF, rows_of(width, ahead))
        call.out((length, width), BF, rows_of(width, ahead))
        call.out((length, 128), F32, rows_of(128, ahead))
        call.out((blocks, 128, channels), F32, chunks_of(ahead, 128, channels))
        call.out((blocks, 8, 128), F32, chunks_of(ahead, 8, 128))
        call.out((STATES + 16, channels), BF)
        call.out((RIM, width), BF)
        call.temp((tile + 8, width), F32).temp((128, channels), F32).temp((8, 128), F32)
        return call.run(22)

    def inside(m, kept, parts, *waits):
        conv, deltas = kept[4:6]
        call = Call(partial(inside_kernel, tile, channels, m=m, sources=len(parts)), steps, f"inside_{m}")
        call.scalars(meta)
        call.blocks((conv, rows_of(width, ahead)), (deltas, rows_of(128, ahead)))
        call.whole(table, wedge, *parts).after(*waits)
        call.out((length, channels), F32, rows_of(channels, ahead))
        call.out((STATES + 8, channels), F32).out((STATES + 16, channels), BF)
        return call.run(11)

    def mix(m, kept, inner, parts, *waits):
        normed, gate, xbc, pre, conv, deltas, held, sums = kept[:8]
        call = Call(partial(mix_kernel, tile, channels, m=m, sources=len(parts)), steps, f"mix_{m}")
        call.scalars(meta)
        call.blocks(
            (inner, rows_of(channels, ahead)),
            (conv, rows_of(width, ahead)),
            (deltas, rows_of(128, ahead)),
            (gate, rows_of(channels, ahead)),
            (held, chunks_of(ahead, 128, channels)),
            (sums, chunks_of(ahead, 8, 128)),
            (cotangent, rows_in(m, model, ahead)),
        )
        call.whole(out_weight, table, spread, wedge, *parts).after(*waits)
        call.out((length, channels), F32, rows_of(channels, ahead))
        call.out((8, length), F32, stat_spec(ahead))
        call.out((STATES, channels), F32)
        return call.run(12)

    def norm(m, kept, mixed, stats, chain, *waits):
        normed, gate, xbc, pre, conv, deltas = kept[:6]
        call = Call(partial(third_kernel, tile, channels, float(full), bool(chain), m=m), steps, f"gate_{m}")
        call.scalars(meta)
        call.blocks(
            (mixed, rows_of(channels, astern)),
            (gate, rows_of(channels, astern)),
            (conv, rows_of(width, astern)),
            (deltas, rows_of(128, astern)),
            (normed, rows_of(model, astern)),
            (cotangent, rows_in(m, model, astern)),
        )
        call.whole(out_weight, table, spread, wedge)
        call.blocks(*[(part, stat_spec(astern)) for part in stats])
        call.whole(*chain).after(*waits)
        call.out((length, model), BF, rows_of(model, astern))
        call.out((length, channels), BF, rows_of(channels, astern))
        call.out((length, channels), BF, rows_of(channels, astern))
        call.out((blocks, 128, channels), F32, chunks_of(astern, 128, channels))
        call.out((blocks, 8, 128), F32, chunks_of(astern, 8, 128))
        call.out((STATES + 16, channels), BF)
        call.out((channels, model), F32)
        call.out((model, channels), F32)
        call.out((16, channels), F32)
        call.temp((128, channels), F32).temp((8, 128), F32)
        return call.run(19)

    def within(m, kept, ssd_back, parts, *waits):
        conv, deltas = kept[4:6]
        call = Call(partial(within_kernel, small, channels, m=m, sources=len(parts)), length // small, f"within_{m}")
        call.scalars(meta)
        call.blocks((conv, rows_of(width, ahead, small)), (deltas, rows_of(128, ahead, small)), (ssd_back, rows_of(channels, ahead, small)))
        call.whole(table, wedge, *parts).after(*waits)
        call.out((length, width), F32, rows_of(width, ahead, small))
        call.out((length, 128), F32, rows_of(128, ahead, small))
        call.out((STATES + 8, channels), F32).out((STATES + 16, channels), BF)
        return call.run(14)

    def across(m, kept, carry, third, inner, parts, chain, *waits):
        normed, gate, xbc, pre, conv, deltas, held, sums, leaving, edge = kept
        call = Call(partial(across_kernel, tile, channels, bool(chain), m=m, sources=len(parts)), steps, f"across_{m}")
        call.scalars(meta)
        call.blocks((conv, rows_of(width, astern)), (pre, rows_of(width, astern)), (xbc, rows_of(width, astern)))
        call.whole(edge)
        call.blocks(
            (deltas, rows_of(128, astern)),
            (third[2], rows_of(channels, astern)),
            (inner[0], rows_of(width, astern)),
            (inner[1], rows_of(128, astern)),
            (held, chunks_of(astern, 128, channels)),
            (sums, chunks_of(astern, 8, 128)),
        )
        call.whole(carry)
        call.blocks((third[3], chunks_of(astern, 128, channels)), (third[4], chunks_of(astern, 8, 128)))
        call.whole(table, spread, gather, wedge, wedge_up, wedge_below, *parts, *chain).after(*waits)
        call.out((length, width + 256), BF, rows_of(width + 256, astern))
        call.out((length, 128), BF, rows_of(128, astern))
        call.out((RIM, width), F32)
        call.out((RIM, width), F32)
        call.out((40, width), F32)
        call.out((16, 128), F32)
        call.temp((3, tile + 24, width), F32).temp((tile, width), F32).temp((STATES, channels), F32)
        return call.run(32)

    def part_of(m, gate_back, fourth, span, rows, rim, chain, earlier, micros, *waits):
        count = span[1] - span[0]
        turn = lambda i: i + span[0]
        put = lambda i: i + span[0] - rows[0]
        call = Call(partial(part_kernel, tile, channels, bool(chain), rim is not None, count), count, f"input_{m}_{span[0]}")
        call.blocks(
            (tokens, rows_in(m, model, turn)),
            (gate_back, rows_of(channels, turn)),
            (fourth[0], rows_of(width + 256, turn)),
            (fourth[1], rows_of(128, turn)),
        )
        call.whole(weights)
        if rim is not None:
            call.whole(fourth[3], rim)
        call.whole(*chain)
        if earlier is not None:
            call.alias(earlier)
        call.after(*waits)
        call.out((rows[1] * tile, model), BF, rows_of(model, put))
        call.out((8, model), F32)
        call.temp((tile, channels + width + 256 + 128), BF)
        return call.run(micros)

    def weight_back(m, kept, fourth, rim, chain, kind, *waits):
        call = Call(partial(weight_kernel, tile, channels, bool(chain), steps), steps, f"weigh_{m}")
        call.blocks(
            (kept[0], rows_of(model, ahead)), (fourth[0], rows_of(width + 256, ahead)), (fourth[1], rows_of(128, ahead))
        )
        call.whole(fourth[3], rim, *chain).after(*waits)
        call.out((model, width), kind)
        call.out((8, model), F32)
        call.temp((tile, width + 256), BF).temp((model, width), F32).temp((128, model), F32)
        return call.run(8)

    side = (lax.axis_index("head") % 2).astype(jnp.int32)[None]

    def place(m, begin, totals, token, earlier, *waits):
        low = totals.astype(BF)
        other = swap(low, "head", 1)
        big = min(512, low.shape[0])
        half = low.shape[0] // big
        call = Call(partial(place_kernel, token), 2 * half, f"place_{m}_{begin}_{token:d}")

        def source(flip):
            return pl.BlockSpec(
                (big, model), lambda i, s: (jnp.clip(i - (s[0] if flip == 0 else 1 - s[0]) * half, 0, half - 1), 0)
            )

        spot = pl.BlockSpec((None, big, model), lambda i, s: (m, i + begin // big, 0))
        call.blocks((low, source(0)), (other, source(1)), (tokens, spot))
        if token:
            call.blocks((cotangent, spot))
            call.args.append(table)
            call.in_specs.append(pl.BlockSpec(table.shape, lambda i, s: (0, 0)))
        if earlier is not None:
            call.alias(earlier)
        call.after(*waits)
        call.out((micro, length, model), BF, spot)
        return call.run(4, side)[0]

    every = range(micro)
    kept, inner, mixes, thirds, order_by, chain = [], [], [], [], [], ()
    for m in every:
        kept.append(project(m, *order_by))
        order_by = [kept[m][8]]
    for m in every:
        inner.append(inside(m, kept[m], near_parts(kept[m][8], "seq", 1), *order_by))
        order_by = [inner[m][1]]
    for m in every:
        mixes.append(mix(m, kept[m], inner[m][0], far_parts(inner[m][1], inner[m][2], "seq", 1), *order_by))
        order_by = [mixes[m][1]]
    for m in every:
        stats = [mixes[m][1]] + [swap(mixes[m][1], "head", bits) for bits in range(1, lax.axis_size("head"))]
        thirds.append(norm(m, kept[m], mixes[m][0], stats, chain, *order_by))
        chain = thirds[m][6:9]
        order_by = [thirds[m][5]]
    grad_out, grad_gate, gate_rows = chain
    grad_out, grad_gate = lax.psum((grad_out, grad_gate), "seq")
    mixed_pair = [head_pair(thirds[m][0]) for m in every]
    mixed_all = [head_rest(mixed_pair[m]) for m in every]
    inner_b, fourths, chain = [], [], ()
    for m in every:
        inner_b.append(within(m, kept[m], thirds[m][2], near_parts(thirds[m][5], "seq", -1), *order_by))
        order_by = [inner_b[m][2], mixed_pair[m]]
    far = [far_parts(inner_b[m][2], inner_b[m][3], "seq", -1) for m in every]
    gain_rows, grads, token_all, half_steps = (), (), [], steps // 2
    for m in every:
        final = m + 1 == micro
        fourths.append(across(m, kept[m], mixes[m][2], thirds[m], inner_b[m], far[m], chain, *order_by))
        chain = fourths[m][4:6]
        rim = from_behind(fourths[m][2], "seq", -1)
        gate_back = thirds[m][1]
        if not final:
            both = (0, steps)
            first = part_of(m, gate_back, fourths[m], (0, half_steps), both, None, gain_rows, None, 6, mixed_all[m], *far[m + 1])
            second = part_of(m, gate_back, fourths[m], (half_steps, steps), both, rim, first[1:], first[0], 6)
            grads = weight_back(m, kept[m], fourths[m], rim, grads, F32, second[1])
            pair = head_pair(second[0])
            token_all.append(head_rest(pair))
            gain_rows = second[1:]
            order_by = [pair, grads[1], mixed_all[m + 1]]
        else:
            first = part_of(m, gate_back, fourths[m], (0, half_steps), (0, half_steps), None, gain_rows, None, 6, token_all[-1])
            grads = weight_back(m, kept[m], fourths[m], rim, grads, BF, first[1])
            pair = head_pair(first[0])
            second = part_of(
                m, gate_back, fourths[m], (half_steps, steps), (half_steps, half_steps), rim, first[1:], None, 6,
                pair, grads[1],
            )
            gain_rows = second[1:]
            last_pair = [pair, head_pair(second[0])]
    tap_rows, head_rows = chain
    grads, dt_rows = grads
    gain_rows = gain_rows[0]
    halved = pair_parts(grads, "seq")
    last_all = [head_rest(last_pair[0])]
    halved, last_pair, dt_rows = lax.optimization_barrier((halved, last_pair, dt_rows))
    last_all.append(head_rest(last_pair[1]))
    halved = sum_rows(halved).astype(BF)
    pieces = scatter_parts(halved, "seq")
    mixed_out = token_grad = None
    for m in every:
        mixed_out = place(m, 0, mixed_all[m], False, mixed_out, halved, last_all[0], grad_out, grad_gate)
    pieces, mixed_out = lax.optimization_barrier((pieces, mixed_out))
    part = sum_rows(pieces)
    share = 2 * states // lax.axis_size("head")
    bc_parts = [part[:, channels:width]]
    bc_parts += [swap(bc_parts[0], "head", bits) for bits in range(1, lax.axis_size("head"))]
    for m in range(micro - 1):
        token_grad = place(m, 0, token_all[m], True, token_grad, part, last_all[1])
    bc_parts, token_grad = lax.optimization_barrier((bc_parts, token_grad))
    bc_mine = lax.dynamic_slice_in_dim(sum_rows(bc_parts), lax.axis_index("head") * share, share, 1)
    gathered = gather_half(
        jnp.concatenate(
            [part[:, :channels], bc_mine, jnp.zeros((part.shape[0], -share % 128), F32)], axis=1
        ).astype(BF),
        "seq",
    )
    gathered = gather_pair(gathered, "seq")
    grad_x = gathered[:, :channels].astype(F32)
    grad_bc = gathered[:, channels : channels + share].astype(F32)

    token_grad = place(micro - 1, 0, last_all[0], True, token_grad)
    token_grad = place(micro - 1, length // 2, last_all[1], True, token_grad)

    def folded(rows):
        return jnp.sum(rows.reshape(-1, 8, rows.shape[1]), axis=1)

    by_tap = folded(tap_rows)
    by_row = folded(gate_rows)
    by_head = folded(head_rows)[:, :heads]
    skip_sum = jnp.sum(by_row[1].reshape(heads, dim), axis=1)
    gain_sum = jnp.sum(gain_rows, axis=0)
    small = jnp.concatenate(
        [by_tap[:, channels:].reshape(-1), gain_sum,
         dt_rows[:heads].reshape(-1), by_tap[:, :channels].reshape(-1), by_row[0], by_head.reshape(-1), skip_sum]
    )
    shared_size = by_tap[:, channels:].size + model
    small = jnp.pad(small, (0, -small.size % 1024)).reshape(-1, 128)
    small = all_sum(small, "seq")
    shared_rows = shared_size // 128
    shared = all_sum(small[:shared_rows], "head").reshape(-1)
    rest = small[shared_rows:].reshape(-1)
    tap_count = conv_x_weight.shape[0]
    bc_taps = shared[: (tap_count + 1) * 2 * states].reshape(tap_count + 1, 2 * states)
    grad_norm_gain = shared[(tap_count + 1) * 2 * states : shared_size]
    grad_dt = rest[: heads * model].reshape(heads, model).T
    rest = rest[heads * model :]
    cut = (tap_count + 1) * channels
    x_taps = rest[:cut].reshape(tap_count + 1, channels)
    grad_gate_gain = rest[cut : cut + channels]
    tails = rest[cut + channels : cut + channels + 3 * heads].reshape(3, heads)
    return (
        mixed_out,
        token_grad,
        grad_norm_gain,
        jnp.stack([grad_gate, grad_x], axis=1),
        grad_bc,
        grad_dt,
        x_taps[:tap_count],
        x_taps[tap_count],
        bc_taps[:tap_count],
        bc_taps[tap_count],
        tails[0],
        tails[1] * decay_rate,
        tails[2],
        grad_gate_gain,
        grad_out,
    )


def solution(mesh):
    in_specs = (
        P(None, "seq", None),
        P(),
        P(),
        P(None, None, "head"),
        P(),
        P(None, "head"),
        P(None, "head"),
        P("head"),
        P(),
        P(),
        P("head"),
        P("head"),
        P("head"),
        P("head"),
        P("head", None),
        P(None, "seq", None),
    )
    out_specs = (
        P(None, "seq", None),
        P(None, "seq", None),
        P(),
        P(None, None, "head"),
        P(None, "head"),
        P(None, "head"),
        P(None, "head"),
        P("head"),
        P(),
        P(),
        P("head"),
        P("head"),
        P("head"),
        P("head"),
        P("head", None),
    )
    return jax.shard_map(local, mesh=mesh, in_specs=in_specs, out_specs=out_specs, check_vma=False)
```

```python
from functools import partial

import jax
import jax.numpy as jnp
import numpy as np
from jax import lax
from jax.experimental import pallas as pl
from jax.experimental.pallas import tpu as pltpu
from jax.sharding import PartitionSpec as P

EPS = 1e-05
Q = 128
STATES = 128
TILE = 512
SMALL = 256
RIM = 16
NEVER = -1e30
TINY = 1e-37
BF = jnp.bfloat16
F32 = jnp.float32
VMEM_BYTES = 48 * 2**20
SCALE = 1.0
GAIN, TAPS, SHIFT, GATE, SKIP, RATE, BIAS, TABLE = 0, 1, 5, 6, 7, 8, 9, 16


def dot(a, b):
    return jnp.dot(a, b, preferred_element_type=F32)


def dot_nt(a, b):
    return lax.dot_general(a, b, (((1,), (1,)), ((), ())), preferred_element_type=F32)


def dot_tn(a, b):
    return lax.dot_general(a, b, (((0,), (0,)), ((), ())), preferred_element_type=F32)


def halves(value):
    high = value.astype(BF)
    return high, (value - high.astype(F32)).astype(BF)


def twice(value, axis):
    return jnp.concatenate([value, value], axis=axis)


def stacked(value, axis):
    return jnp.concatenate(halves(value), axis=axis)


def cut_rows(value, likes):
    pieces, at = [], 0
    for like in likes:
        pieces.append(value[at : at + like.shape[0]])
        at += like.shape[0]
    return pieces


def spread_heads(values, spread):
    both = stacked(jnp.concatenate(values, axis=0), 1)
    return cut_rows(dot(both, spread), values)


def gather_heads(values, gather):
    both = stacked(jnp.concatenate(values, axis=0), 1)
    return cut_rows(dot(both, gather), values)


def add_up(values, wedge):
    result = dot(wedge, jnp.concatenate([stacked(value, 0) for value in values], axis=1))
    return [result[:, 128 * c : 128 * c + 128] for c in range(len(values))]


def near_f32(left, right):
    rows, columns = left.shape[0], right.shape[0]
    product = dot_nt(stacked(left, 0), stacked(right, 0))
    return product[:rows, :columns] + product[:rows, columns:] + product[rows:, :columns]


def sigmoid(value):
    return jax.nn.sigmoid(value)


def softplus(value):
    return jnp.maximum(value, 0.0) + jnp.log1p(jnp.exp(-jnp.abs(value)))


def iota(shape, axis):
    return lax.broadcasted_iota(jnp.int32, shape, axis)


class Docs:
    def __init__(self, meta, m):
        self.count = meta.shape[1] - 1
        self.starts = [meta[m, j] for j in range(self.count)]
        self.anchor = meta[m, self.count]

    def counts(self, places):
        total = (places >= self.starts[0]).astype(jnp.int32)
        for start in self.starts[1:]:
            total = total + (places >= start).astype(jnp.int32)
        return total

    def starts_at(self, places):
        hit = places == self.starts[0]
        for start in self.starts[1:]:
            hit = hit | (places == start)
        return hit

    def none_near(self, first, rows):
        near = (self.starts[0] >= first - 2) & (self.starts[0] <= first + rows + 2)
        for start in self.starts[1:]:
            near = near | ((start >= first - 2) & (start <= first + rows + 2))
        return jnp.logical_not(near)

    def tap_masks(self, first, rows):
        places = first + iota((rows, 128), 0)
        masks = []
        broken = None
        for back in range(3):
            hit = self.starts_at(places - back)
            broken = hit if broken is None else broken | hit
            masks.append(jnp.where(broken, 0.0, 1.0))
        return masks


class Tile:
    def __init__(self, docs, first, deltas, rate, wedge):
        count = deltas.shape[0] // Q
        self.docs, self.first = docs, first
        self.parts = [slice(Q * c, Q * c + Q) for c in range(count)]
        self.deltas = [deltas[rows] for rows in self.parts]
        runs = add_up([part * rate for part in self.deltas], wedge)
        self.run = runs
        self.total = [run[Q - 1 : Q] for run in runs]
        self.before = [docs.counts(first + Q * c - 1) for c in range(count)]
        self.last = [docs.counts(first + Q * c + Q - 1) for c in range(count)]
        self.column = [docs.counts(first + Q * c + iota((Q, 128), 0)) for c in range(count)]

    def same(self, c):
        return self.column[c] == self.docs.counts(self.first + Q * c + iota((8, 128), 1))[0:1]

    def entry(self, c):
        return jnp.exp(self.run[c] + jnp.where(self.column[c] == self.before[c], 0.0, NEVER))

    def leaving(self, c):
        bias = jnp.where(self.column[c] == self.last[c], 0.0, NEVER)
        return jnp.exp(self.total[c] - self.run[c] + bias) * self.deltas[c]

    def overall(self, c):
        return jnp.exp(self.total[c] + jnp.where(self.last[c] == self.before[c], 0.0, NEVER))


def wide_row(row):
    return jnp.broadcast_to(row, (8, row.shape[1]))


def pair_blocks(value, pair, lanes):
    both = value[:, 128 * pair : 128 * pair + 128]
    zero = jnp.zeros_like(both)
    return jnp.concatenate([jnp.where(lanes, both, zero), jnp.where(lanes, zero, both)], axis=0)


def first_kernel(
    tile, channels,
    meta, rim, tokens, weights, table, spread, wedge, *rest, m,
):
    normed_o, gate_o, xbc_o, pre_o, conv_o, deltas_o, held_o, sums_o, leaving_o, edge_o, ext, state, total = rest[-13:]
    step = pl.program_id(0)
    docs = Docs(meta, m)
    width = xbc_o.shape[1]
    taps = table[TAPS : TAPS + 4, :width]
    shift = table[SHIFT : SHIFT + 1, :width]
    gain = table[GAIN : GAIN + 1, : tokens.shape[1]]
    rate = table[RATE : RATE + 1, :128]
    dt_bias = table[BIAS : BIAS + 1, :128]

    def normalize(rows):
        x = rows.astype(F32)
        scale = lax.rsqrt(jnp.mean(x * x, axis=1, keepdims=True) + EPS)
        return (x * scale * gain).astype(BF)

    @pl.when(step == 0)
    def _():
        edge = dot(normalize(rim[...]), weights[:, channels : channels + width]).astype(BF)
        edge_o[...] = edge
        ext[0:8, :] = edge.astype(F32)[RIM - 8 :]
        state[...] = jnp.zeros_like(state)
        total[...] = jnp.zeros_like(total)

    @pl.when(step > 0)
    def _():
        ext[0:8, :] = ext[tile : tile + 8, :]

    normed = normalize(tokens[...])
    normed_o[...] = normed
    gate_o[...] = dot(normed, weights[:, :channels])
    xbc = dot(normed, weights[:, channels : channels + width]).astype(BF)
    xbc_o[...] = xbc
    ext[8:, :] = xbc.astype(F32)
    deltas = softplus(dot(normed, weights[:, channels + width + 256 :]) + dt_bias)
    deltas_o[...] = deltas
    first = docs.anchor + step * tile
    plain = docs.none_near(first, tile)

    def convolve(masks):
        for slab in range(width // 128):
            lanes = slice(128 * slab, 128 * slab + 128)
            if masks is None:
                source = ext[:, lanes]
                pre = shift[:, lanes] + taps[3:4, lanes] * source[8:]
            else:
                pre = shift[:, lanes] + taps[3:4, lanes] * ext[8 : 8 + tile, lanes]
            for back in range(1, 4):
                if masks is None:
                    moved = pltpu.roll(source, back, 0)[8:]
                else:
                    moved = ext[8 - back : 8 - back + tile, lanes] * masks[back - 1]
                pre = pre + taps[3 - back : 4 - back, lanes] * moved
            pre_o[:, lanes] = pre.astype(BF)
            conv_o[:, lanes] = (pre * sigmoid(pre)).astype(BF)

    @pl.when(plain)
    def _():
        convolve(None)

    @pl.when(jnp.logical_not(plain))
    def _():
        convolve(docs.tap_masks(first, tile))

    parts = Tile(docs, first, deltas, rate, wedge[...])
    count = len(parts.parts)
    wide = spread_heads(
        [parts.leaving(c) for c in range(count)] + [wide_row(parts.overall(c)) for c in range(count)], spread[...]
    )
    for c, rows in enumerate(parts.parts):
        held_o[c] = state[...]
        sums_o[c] = total[...]
        total[...] = total[...] + parts.total[c]
        writes = conv_o[rows, channels : channels + 128]
        scaled = conv_o[rows, :channels].astype(F32) * wide[c]
        state[...] = state[...] * wide[count + c][0:1] + dot_tn(twice(writes, 0), stacked(scaled, 0))

    @pl.when(step == pl.num_programs(0) - 1)
    def _():
        end = docs.anchor + (step + 1) * tile - 1
        through = jnp.where(docs.counts(end) == docs.counts(docs.anchor - 1), 0.0, NEVER)
        leaving_o[...] = packed(state[...], spread_heads([jnp.exp(total[...] + through)], spread[...])[0][0:1])


def inside_kernel(
    tile, channels,
    meta, conv, deltas, table, wedge, *rest, m, sources,
):
    mixed_o, near_o, send_o = rest[-3:]
    step = pl.program_id(0)

    @pl.when(step == 0)
    def _():
        state, decay = joined([part[...] for part in rest[:sources]])
        near_o[:STATES, :] = state
        near_o[STATES:, :] = jnp.broadcast_to(decay, (8, channels))
        send_o[...] = packed(state, decay)

    docs = Docs(meta, m)
    first = docs.anchor + step * tile
    lanes_q = iota((Q, 128), 1)
    causal = iota((Q, Q), 0) >= iota((Q, Q), 1)
    low = lanes_q < 64
    skip = table[SKIP : SKIP + 1, :channels]
    rate = table[RATE : RATE + 1, :128]
    parts = Tile(docs, first, deltas[...], rate, wedge[...])
    for c, rows in enumerate(parts.parts):
        u = conv[rows, :channels]
        writes = conv[rows, channels : channels + 128]
        reads = conv[rows, channels + 128 :]
        scores = dot_nt(reads, writes)
        run = parts.run[c]
        bias = jnp.where(parts.same(c) & causal, 0.0, NEVER)
        behind = jnp.transpose(jnp.log(jnp.maximum(parts.deltas[c], TINY)) - run)
        pieces = []
        for pair in range(channels // 128):
            both = []
            for head in (2 * pair, 2 * pair + 1):
                decay = jnp.exp(run[:, head : head + 1] + behind[head : head + 1] + bias)
                both.append((decay * scores).astype(BF))
            pieces.append(dot(jnp.concatenate(both, axis=1), pair_blocks(u, pair, low)))
        mixed_o[rows, :] = jnp.concatenate(pieces, axis=1) + skip * u.astype(F32)


def mix_kernel(
    tile, channels,
    meta, inside, conv, deltas, gate, held, sums, cotangent, out_weight, table, spread, wedge, *rest, m, sources,
):
    mixed_o, stats_o, carry = rest[-3:]
    step = pl.program_id(0)

    @pl.when(step == 0)
    def _():
        carry[...] = joined([part[...] for part in rest[:sources]])[0]

    back = dot_nt(cotangent[...], out_weight[...]) * table[GATE : GATE + 1, :channels]
    docs = Docs(meta, m)
    first = docs.anchor + step * tile
    lanes_q = iota((Q, 128), 1)
    rate = table[RATE : RATE + 1, :128]
    parts = Tile(docs, first, deltas[...], rate, wedge[...])
    count = len(parts.parts)
    start = docs.counts(docs.anchor - 1)
    arrived = [jnp.exp(sums[c] + jnp.where(parts.before[c] == start, 0.0, NEVER)) for c in range(count)]
    wide = spread_heads([parts.entry(c) for c in range(count)] + arrived, spread[...])
    for c, rows in enumerate(parts.parts):
        reads = conv[rows, channels + 128 :]
        state = stacked(held[c] + wide[count + c][0:1] * carry[...], 0)
        mixed = inside[rows, :] + dot(twice(reads, 1), state) * wide[c]
        mixed_o[rows, :] = mixed
        gate_rows = gate[rows, :]
        gated = mixed * gate_rows * sigmoid(gate_rows)
        squares = jnp.sum(gated * gated, axis=1, keepdims=True)
        inner = jnp.sum(gated * back[rows], axis=1, keepdims=True)
        columns = jnp.where(lanes_q == 0, squares, jnp.where(lanes_q == 1, inner, 0.0))
        stats_o[:, rows] = jnp.transpose(columns)[0:8]


def third_kernel(
    tile, channels, full, chained, final,
    side, meta, mixed, gate, conv, deltas, normed, cotangent, out_weight, table, spread, wedge,
    stats_a, stats_b, stats_c, stats_d, *rest, m,
):
    if chained:
        grad_out_i, grad_gate_i, rows_i, *rest = rest
    grad_out, grad_gate, state, total = rest[-4:]
    *grads_o, rows_o = rest[: -4][-2 if final else -3 :]
    mine_o, other_o, gate_back_o, ssd_back_o, held_o, sums_o, leaving_o = rest[: -4 - len(grads_o) - 1][-7:]
    step = pl.program_id(0)
    gate_gain = table[GATE : GATE + 1, :channels]
    rate = table[RATE : RATE + 1, :128]
    docs = Docs(meta, m)
    place = pl.num_programs(0) - 1 - step
    first = docs.anchor + place * tile

    @pl.when(step == 0)
    def _():
        state[...] = jnp.zeros_like(state)
        total[...] = jnp.zeros_like(total)
        if chained:
            grad_out[...] = grad_out_i[...]
            grad_gate[...] = grad_gate_i[...]
            rows_o[...] = rows_i[...]
        else:
            grad_out[...] = jnp.zeros_like(grad_out)
            grad_gate[...] = jnp.zeros_like(grad_gate)
            rows_o[...] = jnp.zeros_like(rows_o)

    stats = stats_a[...] + stats_b[...] + stats_c[...] + stats_d[...]
    branches = []
    back = dot_nt(cotangent[...], out_weight[...])
    parts = Tile(docs, first, deltas[...], rate, wedge[...])
    count = len(parts.parts)
    wide = spread_heads(
        [parts.entry(c) for c in range(count)] + [wide_row(parts.overall(c)) for c in range(count)], spread[...]
    )
    for c in reversed(range(count)):
        rows = parts.parts[c]
        sides = jnp.transpose(jnp.concatenate([stats[:, rows], jnp.zeros((120, Q), F32)], axis=0))
        scale = lax.rsqrt(sides[:, 0:1] / full + EPS)
        inner = sides[:, 1:2]
        mixed_rows = mixed[rows, :]
        gate_rows = gate[rows, :]
        sigma = sigmoid(gate_rows)
        act = gate_rows * sigma
        gated = mixed_rows * act
        unit = gated * scale
        branch = (unit * gate_gain).astype(BF)
        branches.append(branch)
        back_rows = back[rows]
        grad_gated = scale * (back_rows * gate_gain) - unit * (scale * scale * (inner / full))
        grad_mixed = grad_gated * act
        gate_back_o[rows, :] = (grad_gated * mixed_rows * (sigma * (1.0 + gate_rows * (1.0 - sigma)))).astype(BF)
        ssd_back = grad_mixed.astype(BF)
        ssd_back_o[rows, :] = ssd_back
        u = conv[rows, :channels].astype(F32)
        rows_o[0:8, :] += jnp.sum((back_rows * unit).reshape(Q // 8, 8, channels), axis=0)
        rows_o[8:16, :] += jnp.sum((grad_mixed * u).reshape(Q // 8, 8, channels), axis=0)
        held_o[c] = state[...]
        sums_o[c] = total[...]
        total[...] = total[...] + parts.total[c]
        reads = conv[rows, channels + 128 :]
        entered = stacked(ssd_back.astype(F32) * wide[c], 0)
        state[...] = state[...] * wide[count + c][0:1] + dot_tn(twice(reads, 0), entered)
    branch = jnp.concatenate(branches[::-1], axis=0)
    part = dot(branch, out_weight[...]).astype(BF)
    here = place // (pl.num_programs(0) // 2) == side[0]

    @pl.when(here)
    def _():
        mine_o[...] = part

    @pl.when(jnp.logical_not(here))
    def _():
        other_o[...] = part

    grad_out[...] += dot_tn(branch, cotangent[...])
    grad_gate[...] += dot_tn(normed[...], gate_back_o[...])

    @pl.when(step == pl.num_programs(0) - 1)
    def _():
        if final:
            depth = grad_gate.shape[0]
            grads_o[0][:depth, :] = grad_gate[...].astype(BF)
            for block in range(grad_out.shape[1] // channels):
                lanes = slice(channels * block, channels * block + channels)
                grads_o[0][depth + channels * block : depth + channels * (block + 1), :] = grad_out[:, lanes].astype(BF)
        else:
            grads_o[0][...] = grad_out[...]
            grads_o[1][...] = grad_gate[...]
        end = docs.anchor + pl.num_programs(0) * tile - 1
        through = jnp.where(docs.counts(end) == docs.counts(docs.anchor - 1), 0.0, NEVER)
        leaving_o[...] = packed(state[...], spread_heads([jnp.exp(total[...] + through)], spread[...])[0][0:1])


def within_kernel(
    tile, channels,
    meta, conv, deltas, ssd_back, table, wedge, *rest, m, sources,
):
    grads_o, ends_o, near_o, send_o = rest[-4:]
    step = pl.program_id(0)

    @pl.when(step == 0)
    def _():
        state, decay = joined([part[...] for part in rest[:sources]])
        near_o[:STATES, :] = state
        near_o[STATES:, :] = jnp.broadcast_to(decay, (8, channels))
        send_o[...] = packed(state, decay)

    docs = Docs(meta, m)
    first = docs.anchor + step * tile
    lanes_q = iota((Q, 128), 1)
    rows_16 = iota((16, 128), 0)
    causal = iota((Q, Q), 1) >= iota((Q, Q), 0)
    low = lanes_q < 64
    skip = table[SKIP : SKIP + 1, :channels]
    rate = table[RATE : RATE + 1, :128]
    parts = Tile(docs, first, deltas[...], rate, wedge[...])
    for c, rows in enumerate(parts.parts):
        u = conv[rows, :channels]
        writes = conv[rows, channels : channels + 128]
        reads = conv[rows, channels + 128 :]
        grad = ssd_back[rows, :]
        scores = dot_nt(writes, reads)
        bias = jnp.where(parts.same(c) & causal, 0.0, NEVER)
        ahead = jnp.transpose(parts.run[c])
        behind = jnp.log(jnp.maximum(parts.deltas[c], TINY)) - parts.run[c]
        grad_scores = jnp.zeros((Q, Q), F32)
        by_source = jnp.zeros((Q, 128), F32)
        by_target = jnp.zeros((16, 128), F32)
        pieces = []
        for pair in range(channels // 128):
            blocks = pair_blocks(grad, pair, low)
            meets = dot_nt(u[:, 128 * pair : 128 * pair + 128], blocks)
            both = []
            for side in range(2):
                head = 2 * pair + side
                decay = jnp.exp(behind[:, head : head + 1] + ahead[head : head + 1] + bias)
                both.append((decay * scores).astype(BF))
                weighed = decay * meets[:, Q * side : Q * side + Q]
                grad_scores = grad_scores + weighed
                pairs = weighed * scores
                by_source = jnp.where(lanes_q == head, jnp.sum(pairs, axis=1, keepdims=True), by_source)
                by_target = jnp.where(rows_16 == head + 8, jnp.sum(pairs, axis=0, keepdims=True), by_target)
            pieces.append(dot(jnp.concatenate(both, axis=1), blocks))
        ends_o[rows, :] = by_source + jnp.transpose(jnp.concatenate([by_target, jnp.zeros((112, Q), F32)], axis=0))
        high, low_part = halves(grad_scores)
        grads_o[rows, :channels] = jnp.concatenate(pieces, axis=1) + skip * grad.astype(F32)
        grads_o[rows, channels : channels + 128] = dot(jnp.concatenate([high, low_part], axis=1), twice(reads, 0))
        grads_o[rows, channels + 128 :] = dot_tn(jnp.concatenate([high, low_part], axis=0), twice(writes, 0))


def across_kernel(
    tile, channels, chained,
    meta, conv, pre, xbc, edge, deltas, ssd_back, inside, ends,
    held, sums, carry, held_b, sums_b,
    table, spread, gather, wedge, wedge_up, wedge_below, *rest, m, sources,
):
    far, rest = rest[:sources], rest[sources:]
    if chained:
        taps_i, heads_i, *rest = rest
    in_back_o, dt_back_o, rim_o, tail_o, taps_o, heads_o, ext, grads, carry_b = rest[-9:]
    step = pl.program_id(0)
    docs = Docs(meta, m)
    places = pl.num_programs(0)
    place = places - 1 - step
    first = docs.anchor + place * tile
    end = docs.anchor + places * tile - 1
    width = pre.shape[1]
    taps = table[TAPS : TAPS + 4, :width]
    rate = table[RATE : RATE + 1, :128]
    lanes_q = iota((Q, 128), 1)

    @pl.when(step == 0)
    def _():
        if chained:
            taps_o[...] = taps_i[...]
            heads_o[...] = heads_i[...]
        else:
            taps_o[...] = jnp.zeros_like(taps_o)
            heads_o[...] = jnp.zeros_like(heads_o)
        carry_b[...] = joined([part[...] for part in far])[0]
        ext[:, 0:16, :] = jnp.zeros_like(ext[:, 0:16, :])
        ext[:, 16 + tile :, :] = jnp.zeros_like(ext[:, 16 + tile :, :])

    @pl.when(step > 0)
    def _():
        ext[:, 16 + tile :, :] = ext[:, 16:24, :]

    parts = Tile(docs, first, deltas[...], rate, wedge[...])
    count = len(parts.parts)
    start, stop = docs.counts(docs.anchor - 1), docs.counts(end)
    each = range(count)
    arrived = [jnp.exp(sums[c] + jnp.where(parts.before[c] == start, 0.0, NEVER)) for c in each]
    arrived_b = [jnp.exp(sums_b[c] + jnp.where(parts.last[c] == stop, 0.0, NEVER)) for c in each]
    wide = spread_heads(
        [parts.entry(c) for c in each] + [parts.leaving(c) for c in each] + arrived + arrived_b, spread[...]
    )
    crossings, products = [], []
    for c, rows in enumerate(parts.parts):
        u = conv[rows, :channels].astype(F32)
        writes = conv[rows, channels : channels + 128]
        reads = conv[rows, channels + 128 :]
        outward = wide[count + c]
        state = held[c] + wide[2 * count + c][0:1] * carry[...]
        state_b = held_b[c] + wide[3 * count + c][0:1] * carry_b[...]
        grad_in = ssd_back[rows, :].astype(F32) * wide[c]
        crossing = dot(twice(writes, 1), stacked(state_b, 0)) * outward
        products.append(u * crossing)
        crossings.append(grad_in * dot(twice(reads, 1), stacked(state, 0)))
        products.append(jnp.sum((state * state_b).reshape(16, 8, channels), axis=0))
        grads[rows, :channels] = inside[rows, :channels] + crossing
        grads[rows, channels : channels + 128] = inside[rows, channels : channels + 128] + near_f32(u * outward, state_b)
        grads[rows, channels + 128 :] = inside[rows, channels + 128 :] + near_f32(grad_in, state)
    gathered = gather_heads(crossings + products, gather[...])
    in_parts, out_parts = gathered[:count], gathered[count : count + 2 * count : 2]
    ups, sources = [], []
    for c, rows in enumerate(parts.parts):
        both_ends = ends[rows, :]
        sources.append(jnp.where(lanes_q < 8, both_ends, 0.0))
        target = jnp.where(lanes_q < 8, pltpu.roll(both_ends, 120, 1), 0.0)
        ups.append(in_parts[c] + target - sources[c])
    ups = add_up(ups, wedge_up[...])
    belows = add_up(out_parts, wedge_below[...])
    for c, rows in enumerate(parts.parts):
        between = jnp.sum(gathered[count + 2 * c + 1], axis=0, keepdims=True) * parts.overall(c)
        grad_run = between + ups[c] + belows[c]
        part_deltas = parts.deltas[c]
        slope = 1.0 - jnp.exp(-part_deltas)
        ratio = jnp.where(part_deltas > 1e-6, slope / jnp.maximum(part_deltas, 1e-6), 1.0)
        dt_back = (sources[c] + out_parts[c]) * ratio + rate * grad_run * slope
        dt_back_o[rows, :] = dt_back.astype(BF)
        heads_o[0:8, :] += jnp.sum(dt_back.reshape(Q // 8, 8, 128), axis=0)
        heads_o[8:16, :] += jnp.sum((grad_run * part_deltas).reshape(Q // 8, 8, 128), axis=0)

    plain = docs.none_near(first, tile)

    def convolve_back(masks):
        for slab in range(width // 128):
            lanes = slice(128 * slab, 128 * slab + 128)
            pre_rows = pre[:, lanes].astype(F32)
            sigma = sigmoid(pre_rows)
            grad_pre = grads[:, lanes] * (sigma * (1.0 + pre_rows * (1.0 - sigma)))
            source = xbc[:, lanes].astype(F32)
            result = taps[3:4, lanes] * grad_pre
            taps_o[24:32, lanes] += jnp.sum((grad_pre * source).reshape(tile // 8, 8, 128), axis=0)
            taps_o[32:40, lanes] += jnp.sum(grad_pre.reshape(tile // 8, 8, 128), axis=0)
            if masks is None:
                longer = jnp.concatenate([grad_pre, ext[0, 16 + tile :, lanes]], axis=0)
            for back in range(1, 4):
                if masks is None:
                    ext[back - 1, 16:24, lanes] = grad_pre[0:8]
                    moved = pltpu.roll(longer, tile + 8 - back, 0)[:tile]
                else:
                    ext[back - 1, 16 : 16 + tile, lanes] = grad_pre * masks[back - 1]
                    moved = ext[back - 1, 16 + back : 16 + back + tile, lanes]
                result = result + taps[3 - back : 4 - back, lanes] * moved
                taps_o[8 * (3 - back) : 8 * (4 - back), lanes] += jnp.sum(
                    (moved * source).reshape(tile // 8, 8, 128), axis=0
                )
            high = result.astype(BF)
            in_back_o[:, lanes] = high
            if 128 * slab >= channels:
                in_back_o[:, slice(256 + 128 * slab, 384 + 128 * slab)] = (result - high.astype(F32)).astype(BF)

            @pl.when(step == 0)
            def _():
                tail_o[:, lanes] = result[tile - RIM :]

    @pl.when(plain)
    def _():
        convolve_back(None)

    @pl.when(jnp.logical_not(plain))
    def _():
        convolve_back(docs.tap_masks(first, tile))

    @pl.when(place == 0)
    def _():
        total = jnp.zeros((RIM, width), F32)
        source = edge[...].astype(F32)
        for back in range(1, 4):
            moved = ext[back - 1, back : back + RIM, :]
            total = total + taps[3 - back : 4 - back, :] * moved
            taps_o[8 * (3 - back) : 8 * (4 - back), :] += jnp.sum((moved * source).reshape(RIM // 8, 8, width), axis=0)
        rim_o[...] = total


def part_kernel(
    tile, channels, chained, last, tiles,
    tokens, gate_back, in_back, dt_back, weights, *rest,
):
    if last:
        tail, rim, *rest = rest
    if chained:
        rows_i, *rest = rest
    part_o, rows_o, every = rest[-3:]
    step = pl.program_id(0)
    wide = in_back.shape[1]
    width = wide - 256

    @pl.when(step == 0)
    def _():
        rows_o[...] = rows_i[...] if chained else jnp.zeros_like(rows_o)

    every[:, :channels] = gate_back[...]
    every[:, channels : channels + wide] = in_back[...]
    every[:, channels + wide :] = dt_back[...]
    if last:

        @pl.when(step == tiles - 1)
        def _():
            high, low = halves(tail[...] + rim[...])
            every[tile - RIM :, channels : channels + width] = high
            every[tile - RIM :, channels + width : channels + wide] = low[:, channels:]

    x = tokens[...].astype(F32)
    scale = lax.rsqrt(jnp.mean(x * x, axis=1, keepdims=True) + EPS)
    part = dot_nt(every[...], weights[...])
    part_o[...] = part.astype(BF)
    rows_o[...] += jnp.sum((part * (x * scale)).reshape(tile // 8, 8, x.shape[1]), axis=0)


def weight_kernel(
    tile, channels, chained, tiles,
    normed, in_back, dt_back, tail, rim, *rest,
):
    if chained:
        grads_i, dt_i, *rest = rest
    grads_o, dt_o, every, total, dt_total = rest[-5:]
    step = pl.program_id(0)
    wide = in_back.shape[1]
    width = wide - 256

    @pl.when(step == 0)
    def _():
        total[...] = grads_i[...] if chained else jnp.zeros_like(total)
        dt_total[...] = jnp.zeros_like(dt_total)

    every[...] = in_back[...]

    @pl.when(step == tiles - 1)
    def _():
        high, low = halves(tail[...] + rim[...])
        every[tile - RIM :, :width] = high
        every[tile - RIM :, width:] = low[:, channels:]

    turned = jnp.transpose(normed[...])
    total[:, :channels] += dot(turned, every[:, :channels])
    total[:, channels:] += dot(
        twice(turned, 1), jnp.concatenate([every[:, channels:width], every[:, width:]], axis=0)
    )
    dt_total[...] += dot_nt(jnp.transpose(dt_back[...]), turned)

    @pl.when(step == tiles - 1)
    def _():
        grads_o[...] = total[...].astype(grads_o.dtype)
        dt_o[...] = dt_total[0:8] + dt_i[...] if chained else dt_total[0:8]


def place_kernel(
    token,
    side, mine, other, tokens, *rest,
):
    if token:
        cotangent, table, *rest = rest
    out = rest[-1]
    step = pl.program_id(0)

    def finish(total):
        x = tokens[...].astype(F32)
        total = total.astype(F32)
        if not token:
            return (x + total).astype(BF)
        scale = lax.rsqrt(jnp.mean(x * x, axis=1, keepdims=True) + EPS)
        grad_hat = total * table[GAIN : GAIN + 1, :]
        inner = jnp.mean(grad_hat * x, axis=1, keepdims=True)
        return (cotangent[...].astype(F32) + scale * grad_hat - x * (scale * scale * scale * inner)).astype(BF)

    here = step // (pl.num_programs(0) // 2) == side[0]

    @pl.when(here)
    def _():
        out[...] = finish(mine[...])

    @pl.when(jnp.logical_not(here))
    def _():
        out[...] = finish(other[...])


class Call:
    def __init__(self, kernel, steps, name):
        self.kernel, self.steps, self.name = kernel, steps, name
        self.args, self.in_specs, self.outs, self.out_specs, self.scratch = [], [], [], [], []
        self.aliases = {}

    def whole(self, *arrays):
        for array in arrays:
            self.args.append(array)
            self.in_specs.append(pl.BlockSpec(array.shape, lambda i, *s, rank=array.ndim: (0,) * rank))
        return self

    def scalars(self, array):
        self.args.append(array)
        self.in_specs.append(pl.BlockSpec(memory_space=pltpu.SMEM))
        return self

    def blocks(self, *arrays_specs):
        for array, spec in arrays_specs:
            self.args.append(array)
            self.in_specs.append(spec)
        return self

    def out(self, shape, dtype, spec=None):
        self.outs.append(jax.ShapeDtypeStruct(shape, dtype))
        self.out_specs.append(spec or pl.BlockSpec(shape, lambda i, *s, rank=len(shape): (0,) * rank))
        return self

    def after(self, *arrays):
        for array in arrays:
            self.args.append(array)
            self.in_specs.append(pl.BlockSpec(memory_space=pl.ANY))
        return self

    def alias(self, array):
        self.aliases = {len(self.args): 0}
        return self.after(array)

    def temp(self, shape, dtype):
        self.scratch.append(pltpu.VMEM(shape, dtype))
        return self

    def run(self, micros, scalars=None):
        ahead = () if scalars is None else (scalars,)
        return pl.pallas_call(
            self.kernel,
            grid_spec=pltpu.PrefetchScalarGridSpec(
                num_scalar_prefetch=len(ahead),
                grid=(self.steps,),
                in_specs=self.in_specs,
                out_specs=tuple(self.out_specs),
                scratch_shapes=self.scratch,
            ),
            out_shape=tuple(self.outs),
            input_output_aliases={at + len(ahead): to for at, to in self.aliases.items()},
            compiler_params=pltpu.CompilerParams(
                dimension_semantics=("arbitrary",), vmem_limit_bytes=VMEM_BYTES
            ),
            cost_estimate=pl.CostEstimate(flops=int(micros * SCALE * 1.15e9), bytes_accessed=0, transcendentals=0),
            name=self.name,
        )(*ahead, *self.args)


def swap(value, axis, bits):
    count = lax.axis_size(axis)
    return lax.ppermute(value, axis, [(i, i ^ bits) for i in range(count)])


def from_behind(value, axis, steps):
    count = lax.axis_size(axis)
    sources = range(max(0, -steps), min(count, count - steps))
    return lax.ppermute(value, axis, [(i, i + steps) for i in sources])


def packed(state, decay):
    high, low = halves(jnp.broadcast_to(decay, (8, decay.shape[1])))
    return jnp.concatenate([state.astype(BF), high, low], axis=0)


def unpacked(part):
    if part.dtype == F32:
        return part[:STATES], part[STATES : STATES + 1]
    part = part.astype(F32)
    return part[:STATES], part[STATES : STATES + 1] + part[STATES + 8 : STATES + 9]


def joined(parts):
    state, decay = unpacked(parts[0])
    for part in parts[1:]:
        more, keep = unpacked(part)
        state = state + decay * more
        decay = decay * keep
    return state, decay


def near_parts(leaving, axis, sign):
    return [from_behind(leaving, axis, sign * k) for k in range(1, min(4, lax.axis_size(axis)))]


def far_parts(carry, sent, axis, sign):
    count = lax.axis_size(axis)
    window = 3
    parts = [carry]
    while window < count - 1:
        if len(parts) > 1:
            state, decay = joined(parts)
            sent = packed(state, decay)
            carry = jnp.concatenate([state, jnp.broadcast_to(decay, (8, decay.shape[1]))], axis=0)
        parts = [carry] + [from_behind(sent, axis, sign * k) for k in (window, 2 * window) if k < count]
        window *= 3
    return parts


def sum_rows(parts):
    total = parts[0].astype(F32)
    for part in parts[1:]:
        total = total + part.astype(F32)
    return total


def pair_sum(mine, other):
    return (mine.astype(F32) + swap(other, "head", 1).astype(F32)).astype(BF)


def head_pair(part):
    rows = part.shape[0] // 2
    side = lax.axis_index("head") % 2
    mine = lax.dynamic_slice_in_dim(part, side * rows, rows, 0)
    return pair_sum(mine, lax.dynamic_slice_in_dim(part, (1 - side) * rows, rows, 0))


def head_rest(low):
    bit = 2
    while bit < lax.axis_size("head"):
        low = (low.astype(F32) + swap(low, "head", bit).astype(F32)).astype(BF)
        bit *= 2
    return low


class Reduction:
    def __init__(self, value, axis):
        self.value, self.axis, self.bits, self.out = value, axis, 1, True
        self.count, self.me = lax.axis_size(axis), lax.axis_index(axis)
        self.start()

    def start(self):
        if self.out:
            rows, half = self.value.shape[0] // 2, self.me // self.bits % 2
            sent = lax.dynamic_slice_in_dim(self.value, (1 - half) * rows, rows, 0)
            self.value = lax.dynamic_slice_in_dim(self.value, half * rows, rows, 0)
        else:
            sent = self.value
        self.other = swap(sent, self.axis, self.bits)

    def done(self):
        return not self.out and self.bits == 0

    def step(self, after):
        other, _ = lax.optimization_barrier((self.other, after))
        if self.out:
            self.value = (self.value.astype(F32) + other.astype(F32)).astype(BF)
            self.out = self.bits * 2 < self.count
            self.bits = self.bits * 2 if self.out else self.bits
        else:
            first = self.me // self.bits % 2 == 0
            pieces = [jnp.where(first, self.value, other), jnp.where(first, other, self.value)]
            self.value = jnp.concatenate(pieces, axis=0)
            self.bits //= 2
        if not self.done():
            self.start()


def pair_parts(value, axis):
    rows = value.shape[0] // 2
    half = lax.axis_index(axis) % 2
    mine = lax.dynamic_slice_in_dim(value, half * rows, rows, 0)
    return mine, swap(lax.dynamic_slice_in_dim(value, (1 - half) * rows, rows, 0), axis, 1)


def scatter_parts(value, axis):
    count = lax.axis_size(axis) // 2
    me = lax.axis_index(axis) // 2
    rows = value.shape[0] // count
    parts = [lax.dynamic_slice_in_dim(value, me * rows, rows, 0)]
    for bits in range(1, count):
        piece = lax.dynamic_slice_in_dim(value, jnp.bitwise_xor(me, bits) * rows, rows, 0)
        parts.append(swap(piece, axis, 2 * bits))
    return parts


def gather_half(value, axis):
    count = lax.axis_size(axis) // 2
    me = lax.axis_index(axis) // 2
    rows = value.shape[0]
    result = jnp.zeros((count * rows, value.shape[1]), value.dtype)
    result = lax.dynamic_update_slice_in_dim(result, value, me * rows, 0)
    for bits in range(1, count):
        result = lax.dynamic_update_slice_in_dim(
            result, swap(value, axis, 2 * bits), jnp.bitwise_xor(me, bits) * rows, 0
        )
    return result


def gather_pair(half, axis):
    other = swap(half, axis, 1)
    first = lax.axis_index(axis) % 2 == 0
    return jnp.concatenate([jnp.where(first, half, other), jnp.where(first, other, half)], axis=0)


def add_swaps(value, axis):
    return sum_rows([value] + [swap(value, axis, bits) for bits in range(1, lax.axis_size(axis))])


def all_sum(value, axis):
    bit = 1
    while bit < lax.axis_size(axis):
        value = value + swap(value, axis, bit)
        bit *= 2
    return value


def local(
    tokens,
    doc_starts,
    norm_gain,
    gate_x_weight,
    bc_weight,
    dt_weight,
    conv_x_weight,
    conv_x_bias,
    conv_bc_weight,
    conv_bc_bias,
    dt_bias,
    a_log,
    d_skip,
    gate_gain,
    out_weight,
    cotangent,
):
    micro, length, model = tokens.shape
    channels = gate_x_weight.shape[2]
    heads = dt_weight.shape[1]
    dim = channels // heads
    states = bc_weight.shape[1] // 2
    width = channels + 2 * states
    full = channels * lax.axis_size("head")
    tile, small = min(TILE, length), min(SMALL, length)
    steps = length // tile
    per = tile // Q
    blocks = length // Q

    rim_tokens = from_behind(tokens[:, length - RIM :], "seq", 1)
    weights = jnp.concatenate(
        [gate_x_weight[:, 0], gate_x_weight[:, 1], bc_weight, bc_weight,
         jnp.pad(dt_weight, ((0, 0), (0, 128 - heads)))], axis=1
    )
    decay_rate = -jnp.exp(a_log)

    def table_rows(*parts):
        row = jnp.concatenate(parts, axis=-1)
        row = row if row.ndim == 2 else row[None]
        return jnp.pad(row, ((0, 0), (0, model - row.shape[1])))

    table = jnp.concatenate(
        [
            table_rows(norm_gain),
            table_rows(conv_x_weight, conv_bc_weight),
            table_rows(conv_x_bias, conv_bc_bias),
            table_rows(gate_gain),
            table_rows(jnp.repeat(d_skip, dim)),
            table_rows(decay_rate),
            table_rows(dt_bias, jnp.full((128 - heads,), -200.0, F32)),
            jnp.zeros((TABLE - BIAS - 1, model), F32),
        ],
        axis=0,
    )
    owner = np.arange(channels)[None, :] // dim == np.arange(128)[:, None]
    spread = np.concatenate([owner, owner], axis=0).astype(BF)
    gather = np.concatenate([owner.T, owner.T], axis=0).astype(BF)
    order = np.arange(Q)
    until_here = order[:, None] >= order[None, :]
    below = order[:, None] > order[None, :]
    wedge = np.concatenate([until_here] * 2, axis=1).astype(BF)
    wedge_up = np.concatenate([until_here.T] * 2, axis=1).astype(BF)
    wedge_below = np.concatenate([below] * 2, axis=1).astype(BF)
    anchor = lax.axis_index("seq") * length
    meta = jnp.concatenate(
        [jnp.where(doc_starts >= 1, doc_starts, 2**30), jnp.full((micro, 1), anchor)], axis=1
    ).astype(jnp.int32)

    side = (lax.axis_index("head") % 2).astype(jnp.int32)[None]
    ahead = lambda i: i
    astern = lambda i: steps - 1 - i

    def rows_of(cols, turn, rows=tile):
        return pl.BlockSpec((rows, cols), lambda i, *s: (turn(i), 0))

    def rows_in(m, cols, turn):
        return pl.BlockSpec((None, tile, cols), lambda i, *s: (m, turn(i), 0))

    def chunks_of(turn, rows, cols):
        return pl.BlockSpec((per, rows, cols), lambda i, *s: (turn(i), 0, 0))

    def stat_spec(turn):
        return pl.BlockSpec((8, tile), lambda i, *s: (0, turn(i)))

    def project(m, *waits):
        call = Call(partial(first_kernel, tile, channels, m=m), steps, f"project_{m}")
        call.scalars(meta)
        call.blocks((rim_tokens, pl.BlockSpec((None, RIM, model), lambda i, *s: (m, 0, 0))))
        call.blocks((tokens, rows_in(m, model, ahead)))
        call.whole(weights, table, spread, wedge).after(*waits)
        call.out((length, model), BF, rows_of(model, ahead))
        call.out((length, channels), F32, rows_of(channels, ahead))
        call.out((length, width), BF, rows_of(width, ahead))
        call.out((length, width), BF, rows_of(width, ahead))
        call.out((length, width), BF, rows_of(width, ahead))
        call.out((length, 128), F32, rows_of(128, ahead))
        call.out((blocks, 128, channels), F32, chunks_of(ahead, 128, channels))
        call.out((blocks, 8, 128), F32, chunks_of(ahead, 8, 128))
        call.out((STATES + 16, channels), BF)
        call.out((RIM, width), BF)
        call.temp((tile + 8, width), F32).temp((128, channels), F32).temp((8, 128), F32)
        return call.run(22)

    def inside(m, kept, parts, *waits):
        conv, deltas = kept[4:6]
        call = Call(partial(inside_kernel, tile, channels, m=m, sources=len(parts)), steps, f"inside_{m}")
        call.scalars(meta)
        call.blocks((conv, rows_of(width, ahead)), (deltas, rows_of(128, ahead)))
        call.whole(table, wedge, *parts).after(*waits)
        call.out((length, channels), F32, rows_of(channels, ahead))
        call.out((STATES + 8, channels), F32).out((STATES + 16, channels), BF)
        return call.run(11)

    def mix(m, kept, inner, parts, *waits):
        normed, gate, xbc, pre, conv, deltas, held, sums = kept[:8]
        call = Call(partial(mix_kernel, tile, channels, m=m, sources=len(parts)), steps, f"mix_{m}")
        call.scalars(meta)
        call.blocks(
            (inner, rows_of(channels, ahead)),
            (conv, rows_of(width, ahead)),
            (deltas, rows_of(128, ahead)),
            (gate, rows_of(channels, ahead)),
            (held, chunks_of(ahead, 128, channels)),
            (sums, chunks_of(ahead, 8, 128)),
            (cotangent, rows_in(m, model, ahead)),
        )
        call.whole(out_weight, table, spread, wedge, *parts).after(*waits)
        call.out((length, channels), F32, rows_of(channels, ahead))
        call.out((8, length), F32, stat_spec(ahead))
        call.out((STATES, channels), F32)
        return call.run(12)

    def norm(m, kept, mixed, stats, chain, *waits):
        normed, gate, xbc, pre, conv, deltas = kept[:6]
        final = m + 1 == micro
        call = Call(partial(third_kernel, tile, channels, float(full), bool(chain), final, m=m), steps, f"gate_{m}")
        call.scalars(meta)
        call.blocks(
            (mixed, rows_of(channels, astern)),
            (gate, rows_of(channels, astern)),
            (conv, rows_of(width, astern)),
            (deltas, rows_of(128, astern)),
            (normed, rows_of(model, astern)),
            (cotangent, rows_in(m, model, astern)),
        )
        call.whole(out_weight, table, spread, wedge)
        call.blocks(*[(part, stat_spec(astern)) for part in stats])
        call.whole(*chain).after(*waits)
        half = steps // 2

        def spot(flip):
            return pl.BlockSpec(
                (tile, model),
                lambda i, s: (jnp.clip(astern(i) - (s[0] if flip == 0 else 1 - s[0]) * half, 0, half - 1), 0),
            )

        call.out((length // 2, model), BF, spot(0)).out((length // 2, model), BF, spot(1))
        call.out((length, channels), BF, rows_of(channels, astern))
        call.out((length, channels), BF, rows_of(channels, astern))
        call.out((blocks, 128, channels), F32, chunks_of(astern, 128, channels))
        call.out((blocks, 8, 128), F32, chunks_of(astern, 8, 128))
        call.out((STATES + 16, channels), BF)
        if final:
            call.out((2 * model, channels), BF)
        else:
            call.out((channels, model), F32)
            call.out((model, channels), F32)
        call.out((16, channels), F32)
        call.temp((channels, model), F32).temp((model, channels), F32)
        call.temp((128, channels), F32).temp((8, 128), F32)
        return call.run(17, side)

    def within(m, kept, ssd_back, parts, *waits):
        conv, deltas = kept[4:6]
        call = Call(partial(within_kernel, small, channels, m=m, sources=len(parts)), length // small, f"within_{m}")
        call.scalars(meta)
        call.blocks((conv, rows_of(width, ahead, small)), (deltas, rows_of(128, ahead, small)), (ssd_back, rows_of(channels, ahead, small)))
        call.whole(table, wedge, *parts).after(*waits)
        call.out((length, width), F32, rows_of(width, ahead, small))
        call.out((length, 128), F32, rows_of(128, ahead, small))
        call.out((STATES + 8, channels), F32).out((STATES + 16, channels), BF)
        return call.run(14)

    def across(m, kept, carry, third, inner, parts, chain, *waits):
        normed, gate, xbc, pre, conv, deltas, held, sums, leaving, edge = kept
        call = Call(partial(across_kernel, tile, channels, bool(chain), m=m, sources=len(parts)), steps, f"across_{m}")
        call.scalars(meta)
        call.blocks((conv, rows_of(width, astern)), (pre, rows_of(width, astern)), (xbc, rows_of(width, astern)))
        call.whole(edge)
        call.blocks(
            (deltas, rows_of(128, astern)),
            (third[3], rows_of(channels, astern)),
            (inner[0], rows_of(width, astern)),
            (inner[1], rows_of(128, astern)),
            (held, chunks_of(astern, 128, channels)),
            (sums, chunks_of(astern, 8, 128)),
        )
        call.whole(carry)
        call.blocks((third[4], chunks_of(astern, 128, channels)), (third[5], chunks_of(astern, 8, 128)))
        call.whole(table, spread, gather, wedge, wedge_up, wedge_below, *parts, *chain).after(*waits)
        call.out((length, width + 256), BF, rows_of(width + 256, astern))
        call.out((length, 128), BF, rows_of(128, astern))
        call.out((RIM, width), F32)
        call.out((RIM, width), F32)
        call.out((40, width), F32)
        call.out((16, 128), F32)
        call.temp((3, tile + 24, width), F32).temp((tile, width), F32).temp((STATES, channels), F32)
        return call.run(32)

    def part_of(m, gate_back, fourth, span, rows, rim, chain, earlier, micros, *waits):
        count = span[1] - span[0]
        turn = lambda i: i + span[0]
        put = lambda i: i + span[0] - rows[0]
        call = Call(partial(part_kernel, tile, channels, bool(chain), rim is not None, count), count, f"input_{m}_{span[0]}")
        call.blocks(
            (tokens, rows_in(m, model, turn)),
            (gate_back, rows_of(channels, turn)),
            (fourth[0], rows_of(width + 256, turn)),
            (fourth[1], rows_of(128, turn)),
        )
        call.whole(weights)
        if rim is not None:
            call.whole(fourth[3], rim)
        call.whole(*chain)
        if earlier is not None:
            call.alias(earlier)
        call.after(*waits)
        call.out((rows[1] * tile, model), BF, rows_of(model, put))
        call.out((8, model), F32)
        call.temp((tile, channels + width + 256 + 128), BF)
        return call.run(micros)

    def weight_back(m, kept, fourth, rim, chain, kind, *waits):
        call = Call(partial(weight_kernel, tile, channels, bool(chain), steps), steps, f"weigh_{m}")
        call.blocks(
            (kept[0], rows_of(model, ahead)), (fourth[0], rows_of(width + 256, ahead)), (fourth[1], rows_of(128, ahead))
        )
        call.whole(fourth[3], rim, *chain).after(*waits)
        call.out((model, width), kind)
        call.out((8, model), F32)
        call.temp((tile, width + 256), BF).temp((model, width), F32).temp((128, model), F32)
        return call.run(8)

    def place(m, begin, low, other, token, earlier, *waits):
        big = min(512, low.shape[0])
        half = low.shape[0] // big
        call = Call(partial(place_kernel, token), 2 * half, f"place_{m}_{begin}_{token:d}")

        def source(flip):
            return pl.BlockSpec(
                (big, model), lambda i, s: (jnp.clip(i - (s[0] if flip == 0 else 1 - s[0]) * half, 0, half - 1), 0)
            )

        spot = pl.BlockSpec((None, big, model), lambda i, s: (m, i + begin // big, 0))
        call.blocks((low, source(0)), (other, source(1)), (tokens, spot))
        if token:
            call.blocks((cotangent, spot))
            call.args.append(table)
            call.in_specs.append(pl.BlockSpec(table.shape, lambda i, s: (0, 0)))
        if earlier is not None:
            call.alias(earlier)
        call.after(*waits)
        call.out((micro, length, model), BF, spot)
        return call.run(4, side)[0]

    every = range(micro)
    kept, inner, mixes, thirds, order_by, chain = [], [], [], [], [], ()
    for m in every:
        kept.append(project(m, *order_by))
        order_by = [kept[m][8]]
    for m in every:
        inner.append(inside(m, kept[m], near_parts(kept[m][8], "seq", 1), *order_by))
        order_by = [inner[m][1]]
    for m in every:
        mixes.append(mix(m, kept[m], inner[m][0], far_parts(inner[m][1], inner[m][2], "seq", 1), *order_by))
        order_by = [mixes[m][1]]
    for m in every:
        stats = [mixes[m][1]] + [swap(mixes[m][1], "head", bits) for bits in range(1, lax.axis_size("head"))]
        thirds.append(norm(m, kept[m], mixes[m][0], stats, chain, *order_by))
        chain = thirds[m][7:]
        order_by = [thirds[m][6]]
    packed_grads, gate_rows = chain
    reduction = Reduction(packed_grads, "seq")
    mixed_pair = [pair_sum(thirds[m][0], thirds[m][1]) for m in every]
    mixed_all = [head_rest(mixed_pair[m]) for m in every]
    inner_b, fourths, chain = [], [], ()
    for m in every:
        near = near_parts(thirds[m][6], "seq", -1)
        inner_b.append(within(m, kept[m], thirds[m][3], near, mixed_pair[m], *order_by))
        order_by = [inner_b[m][2]]
        reduction.step(inner_b[m][2])
    far = [far_parts(inner_b[m][2], inner_b[m][3], "seq", -1) for m in every]
    order_by.append(mixed_all[0])
    mixed_other = [swap(mixed_all[m], "head", 1) for m in every]
    token_other = []
    gain_rows, grads, token_all, half_steps = (), (), [], steps // 2
    for m in every:
        final = m + 1 == micro
        fourths.append(across(m, kept[m], mixes[m][2], thirds[m], inner_b[m], far[m], chain, *order_by))
        chain = fourths[m][4:6]
        if not reduction.done():
            reduction.step(fourths[m][4])
        rim = from_behind(fourths[m][2], "seq", -1)
        gate_back = thirds[m][2]
        if not final:
            both = (0, steps)
            first = part_of(m, gate_back, fourths[m], (0, half_steps), both, None, gain_rows, None, 6, mixed_all[m + 1], *far[m + 1])
            second = part_of(m, gate_back, fourths[m], (half_steps, steps), both, rim, first[1:], first[0], 6)
            grads = weight_back(m, kept[m], fourths[m], rim, grads, F32, second[1])
            reduction.step(second[1])
            reduction.step(grads[1])
            pair = head_pair(second[0])
            token_all.append(head_rest(pair))
            token_other.append(swap(token_all[m], "head", 1))
            gain_rows = second[1:]
            order_by = [pair, grads[1]]
        else:
            first = part_of(m, gate_back, fourths[m], (0, half_steps), (0, half_steps), None, gain_rows, None, 6, token_all[-1], *mixed_other)
            pair = head_pair(first[0])
            second = part_of(
                m, gate_back, fourths[m], (half_steps, steps), (half_steps, half_steps), rim, first[1:], None, 6
            )
            grads = weight_back(m, kept[m], fourths[m], rim, grads, BF, second[1], pair, *token_other)
            gain_rows = second[1:]
            last_pair = [pair, head_pair(second[0])]
    tap_rows, head_rows = chain
    grads, dt_rows = grads
    gain_rows = gain_rows[0]

    def folded(rows):
        return jnp.sum(rows.reshape(-1, 8, rows.shape[1]), axis=1)

    by_tap = folded(tap_rows)
    by_row = folded(gate_rows)
    by_head = folded(head_rows)[:, :heads]
    skip_sum = jnp.sum(by_row[1].reshape(heads, dim), axis=1)
    small = jnp.concatenate(
        [by_tap[:, channels:].reshape(-1), jnp.sum(gain_rows, axis=0), dt_rows[:heads].reshape(-1),
         by_tap[:, :channels].reshape(-1), by_row[0], by_head.reshape(-1), skip_sum]
    )
    small = jnp.pad(small, (0, -small.size % 1024)).reshape(-1, 128)
    shared_size = by_tap[:, channels:].size + model
    halved = pair_parts(grads, "seq")
    last_all = [head_rest(last_pair[0])]
    halved, last_pair = lax.optimization_barrier((halved, last_pair))
    last_all.append(head_rest(last_pair[1]))
    halved = sum_rows(halved).astype(BF)
    pieces = scatter_parts(halved, "seq")
    small = all_sum(lax.optimization_barrier((small, halved))[0], "seq")
    mixed_out = place(0, 0, mixed_all[0], mixed_other[0], False, None, halved, last_all[0])
    pieces, mixed_out = lax.optimization_barrier((pieces, mixed_out))
    part = sum_rows(pieces)
    while not reduction.done():
        reduction.step(part)
    packed_grads = reduction.value
    share = 2 * states // lax.axis_size("head")
    bc_parts = [part[:, channels:width]]
    bc_parts += [swap(bc_parts[0], "head", bits) for bits in range(1, lax.axis_size("head"))]
    for m in range(1, micro):
        mixed_out = place(m, 0, mixed_all[m], mixed_other[m], False, mixed_out, part, last_all[1])
    bc_parts, mixed_out = lax.optimization_barrier((bc_parts, mixed_out))
    bc_mine = lax.dynamic_slice_in_dim(sum_rows(bc_parts), lax.axis_index("head") * share, share, 1)
    payload = jnp.concatenate(
        [part[:, :channels], bc_mine, jnp.zeros((part.shape[0], -share % 128), F32)], axis=1
    ).astype(BF)
    gathered = gather_half(payload, "seq")
    token_grad = None
    for m in range(micro - 1):
        token_grad = place(m, 0, token_all[m], token_other[m], True, token_grad, payload)
    gathered, token_grad = lax.optimization_barrier((gathered, token_grad))
    gathered = gather_pair(gathered, "seq")
    grad_x = gathered[:, :channels].astype(F32)
    grad_bc = gathered[:, channels : channels + share].astype(F32)

    token_grad = place(micro - 1, 0, last_all[0], swap(last_all[0], "head", 1), True, token_grad)
    last_other = swap(last_all[1], "head", 1)
    token_grad = place(micro - 1, length // 2, last_all[1], last_other, True, token_grad)

    tap_count = conv_x_weight.shape[0]
    shared, _ = lax.optimization_barrier((small[: shared_size // 128], payload))
    shared = add_swaps(shared, "head").reshape(-1)
    rest = small[shared_size // 128 :].reshape(-1)
    bc_taps = shared[: (tap_count + 1) * 2 * states].reshape(tap_count + 1, 2 * states)
    grad_norm_gain = shared[(tap_count + 1) * 2 * states :]
    grad_dt = rest[: heads * model].reshape(heads, model).T
    rest = rest[heads * model :]
    cut = (tap_count + 1) * channels
    x_taps = rest[:cut].reshape(tap_count + 1, channels)
    grad_gate_gain = rest[cut : cut + channels]
    tails = rest[cut + channels : cut + channels + 3 * heads].reshape(3, heads)
    grad_gate = packed_grads[:model].astype(F32)
    grad_out = jnp.concatenate(
        [packed_grads[row : row + channels] for row in range(model, 2 * model, channels)], axis=1
    ).astype(F32)
    return (
        mixed_out,
        token_grad,
        grad_norm_gain,
        jnp.stack([grad_gate, grad_x], axis=1),
        grad_bc,
        grad_dt,
        x_taps[:tap_count],
        x_taps[tap_count],
        bc_taps[:tap_count],
        bc_taps[tap_count],
        tails[0],
        tails[1] * decay_rate,
        tails[2],
        grad_gate_gain,
        grad_out,
    )


def solution(mesh):
    in_specs = (
        P(None, "seq", None),
        P(),
        P(),
        P(None, None, "head"),
        P(),
        P(None, "head"),
        P(None, "head"),
        P("head"),
        P(),
        P(),
        P("head"),
        P("head"),
        P("head"),
        P("head"),
        P("head", None),
        P(None, "seq", None),
    )
    out_specs = (
        P(None, "seq", None),
        P(None, "seq", None),
        P(),
        P(None, None, "head"),
        P(None, "head"),
        P(None, "head"),
        P(None, "head"),
        P("head"),
        P(),
        P(),
        P("head"),
        P("head"),
        P("head"),
        P("head"),
        P("head", None),
    )
    return jax.shard_map(local, mesh=mesh, in_specs=in_specs, out_specs=out_specs, check_vma=False)
```

```python
from functools import partial

import jax
import jax.numpy as jnp
import numpy as np
from jax import lax
from jax.experimental import pallas as pl
from jax.experimental.pallas import tpu as pltpu
from jax.sharding import PartitionSpec as P

EPS = 1e-05
Q = 128
STATES = 128
TILE = 512
SMALL = 256
RIM = 16
NEVER = -1e30
TINY = 1e-37
BF = jnp.bfloat16
F32 = jnp.float32
VMEM_BYTES = 48 * 2**20
SCALE = 1.0
GAIN, TAPS, SHIFT, GATE, SKIP, RATE, BIAS, TABLE = 0, 1, 5, 6, 7, 8, 9, 16


def dot(a, b):
    return jnp.dot(a, b, preferred_element_type=F32)


def dot_nt(a, b):
    return lax.dot_general(a, b, (((1,), (1,)), ((), ())), preferred_element_type=F32)


def dot_tn(a, b):
    return lax.dot_general(a, b, (((0,), (0,)), ((), ())), preferred_element_type=F32)


def halves(value):
    high = value.astype(BF)
    return high, (value - high.astype(F32)).astype(BF)


def twice(value, axis):
    return jnp.concatenate([value, value], axis=axis)


def stacked(value, axis):
    return jnp.concatenate(halves(value), axis=axis)


def cut_rows(value, likes):
    pieces, at = [], 0
    for like in likes:
        pieces.append(value[at : at + like.shape[0]])
        at += like.shape[0]
    return pieces


def spread_heads(values, spread):
    both = stacked(jnp.concatenate(values, axis=0), 1)
    return cut_rows(dot(both, spread), values)


def gather_heads(values, gather):
    both = stacked(jnp.concatenate(values, axis=0), 1)
    return cut_rows(dot(both, gather), values)


def add_up(values, wedge):
    result = dot(wedge, jnp.concatenate([stacked(value, 0) for value in values], axis=1))
    return [result[:, 128 * c : 128 * c + 128] for c in range(len(values))]


def near_f32(left, right):
    rows, columns = left.shape[0], right.shape[0]
    product = dot_nt(stacked(left, 0), stacked(right, 0))
    return product[:rows, :columns] + product[:rows, columns:] + product[rows:, :columns]


def sigmoid(value):
    return jax.nn.sigmoid(value)


def softplus(value):
    return jnp.maximum(value, 0.0) + jnp.log1p(jnp.exp(-jnp.abs(value)))


def iota(shape, axis):
    return lax.broadcasted_iota(jnp.int32, shape, axis)


class Docs:
    def __init__(self, meta, m):
        self.count = meta.shape[1] - 1
        self.starts = [meta[m, j] for j in range(self.count)]
        self.anchor = meta[m, self.count]

    def counts(self, places):
        total = (places >= self.starts[0]).astype(jnp.int32)
        for start in self.starts[1:]:
            total = total + (places >= start).astype(jnp.int32)
        return total

    def starts_at(self, places):
        hit = places == self.starts[0]
        for start in self.starts[1:]:
            hit = hit | (places == start)
        return hit

    def none_near(self, first, rows):
        near = (self.starts[0] >= first - 2) & (self.starts[0] <= first + rows + 2)
        for start in self.starts[1:]:
            near = near | ((start >= first - 2) & (start <= first + rows + 2))
        return jnp.logical_not(near)

    def tap_masks(self, first, rows):
        places = first + iota((rows, 128), 0)
        masks = []
        broken = None
        for back in range(3):
            hit = self.starts_at(places - back)
            broken = hit if broken is None else broken | hit
            masks.append(jnp.where(broken, 0.0, 1.0))
        return masks


class Tile:
    def __init__(self, docs, first, deltas, rate, wedge):
        count = deltas.shape[0] // Q
        self.docs, self.first = docs, first
        self.parts = [slice(Q * c, Q * c + Q) for c in range(count)]
        self.deltas = [deltas[rows] for rows in self.parts]
        runs = add_up([part * rate for part in self.deltas], wedge)
        self.run = runs
        self.total = [run[Q - 1 : Q] for run in runs]
        self.before = [docs.counts(first + Q * c - 1) for c in range(count)]
        self.last = [docs.counts(first + Q * c + Q - 1) for c in range(count)]
        self.column = [docs.counts(first + Q * c + iota((Q, 128), 0)) for c in range(count)]

    def same(self, c):
        return self.column[c] == self.docs.counts(self.first + Q * c + iota((8, 128), 1))[0:1]

    def entry(self, c):
        return jnp.exp(self.run[c] + jnp.where(self.column[c] == self.before[c], 0.0, NEVER))

    def leaving(self, c):
        bias = jnp.where(self.column[c] == self.last[c], 0.0, NEVER)
        return jnp.exp(self.total[c] - self.run[c] + bias) * self.deltas[c]

    def overall(self, c):
        return jnp.exp(self.total[c] + jnp.where(self.last[c] == self.before[c], 0.0, NEVER))


def wide_row(row):
    return jnp.broadcast_to(row, (8, row.shape[1]))


def pair_blocks(value, pair, lanes):
    both = value[:, 128 * pair : 128 * pair + 128]
    zero = jnp.zeros_like(both)
    return jnp.concatenate([jnp.where(lanes, both, zero), jnp.where(lanes, zero, both)], axis=0)


def first_kernel(
    tile, channels,
    meta, rim, tokens, weights, table, spread, wedge, *rest, m,
):
    normed_o, gate_o, xbc_o, pre_o, conv_o, deltas_o, held_o, sums_o, leaving_o, edge_o, ext, state, total = rest[-13:]
    step = pl.program_id(0)
    docs = Docs(meta, m)
    width = xbc_o.shape[1]
    taps = table[TAPS : TAPS + 4, :width]
    shift = table[SHIFT : SHIFT + 1, :width]
    gain = table[GAIN : GAIN + 1, : tokens.shape[1]]
    rate = table[RATE : RATE + 1, :128]
    dt_bias = table[BIAS : BIAS + 1, :128]

    def normalize(rows):
        x = rows.astype(F32)
        scale = lax.rsqrt(jnp.mean(x * x, axis=1, keepdims=True) + EPS)
        return (x * scale * gain).astype(BF)

    @pl.when(step == 0)
    def _():
        edge = dot(normalize(rim[...]), weights[:, channels : channels + width]).astype(BF)
        edge_o[...] = edge
        ext[0:8, :] = edge.astype(F32)[RIM - 8 :]
        state[...] = jnp.zeros_like(state)
        total[...] = jnp.zeros_like(total)

    @pl.when(step > 0)
    def _():
        ext[0:8, :] = ext[tile : tile + 8, :]

    normed = normalize(tokens[...])
    normed_o[...] = normed
    gate_o[...] = dot(normed, weights[:, :channels])
    xbc = dot(normed, weights[:, channels : channels + width]).astype(BF)
    xbc_o[...] = xbc
    ext[8:, :] = xbc.astype(F32)
    deltas = softplus(dot(normed, weights[:, channels + width + 256 :]) + dt_bias)
    deltas_o[...] = deltas
    first = docs.anchor + step * tile
    plain = docs.none_near(first, tile)

    def convolve(masks):
        for slab in range(width // 128):
            lanes = slice(128 * slab, 128 * slab + 128)
            if masks is None:
                source = ext[:, lanes]
                pre = shift[:, lanes] + taps[3:4, lanes] * source[8:]
            else:
                pre = shift[:, lanes] + taps[3:4, lanes] * ext[8 : 8 + tile, lanes]
            for back in range(1, 4):
                if masks is None:
                    moved = pltpu.roll(source, back, 0)[8:]
                else:
                    moved = ext[8 - back : 8 - back + tile, lanes] * masks[back - 1]
                pre = pre + taps[3 - back : 4 - back, lanes] * moved
            pre_o[:, lanes] = pre.astype(BF)
            conv_o[:, lanes] = (pre * sigmoid(pre)).astype(BF)

    @pl.when(plain)
    def _():
        convolve(None)

    @pl.when(jnp.logical_not(plain))
    def _():
        convolve(docs.tap_masks(first, tile))

    parts = Tile(docs, first, deltas, rate, wedge[...])
    count = len(parts.parts)
    wide = spread_heads(
        [parts.leaving(c) for c in range(count)] + [wide_row(parts.overall(c)) for c in range(count)], spread[...]
    )
    for c, rows in enumerate(parts.parts):
        held_o[c] = state[...]
        sums_o[c] = total[...]
        total[...] = total[...] + parts.total[c]
        writes = conv_o[rows, channels : channels + 128]
        scaled = conv_o[rows, :channels].astype(F32) * wide[c]
        state[...] = state[...] * wide[count + c][0:1] + dot_tn(twice(writes, 0), stacked(scaled, 0))

    @pl.when(step == pl.num_programs(0) - 1)
    def _():
        end = docs.anchor + (step + 1) * tile - 1
        through = jnp.where(docs.counts(end) == docs.counts(docs.anchor - 1), 0.0, NEVER)
        leaving_o[...] = packed(state[...], spread_heads([jnp.exp(total[...] + through)], spread[...])[0][0:1])


def inside_kernel(
    tile, channels,
    meta, conv, deltas, table, wedge, *rest, m, sources,
):
    mixed_o, near_o, send_o = rest[-3:]
    step = pl.program_id(0)

    @pl.when(step == 0)
    def _():
        state, decay = joined([part[...] for part in rest[:sources]])
        near_o[:STATES, :] = state
        near_o[STATES:, :] = jnp.broadcast_to(decay, (8, channels))
        send_o[...] = packed(state, decay)

    docs = Docs(meta, m)
    first = docs.anchor + step * tile
    lanes_q = iota((Q, 128), 1)
    causal = iota((Q, Q), 0) >= iota((Q, Q), 1)
    low = lanes_q < 64
    skip = table[SKIP : SKIP + 1, :channels]
    rate = table[RATE : RATE + 1, :128]
    parts = Tile(docs, first, deltas[...], rate, wedge[...])
    for c, rows in enumerate(parts.parts):
        u = conv[rows, :channels]
        writes = conv[rows, channels : channels + 128]
        reads = conv[rows, channels + 128 :]
        scores = dot_nt(reads, writes)
        run = parts.run[c]
        bias = jnp.where(parts.same(c) & causal, 0.0, NEVER)
        behind = jnp.transpose(jnp.log(jnp.maximum(parts.deltas[c], TINY)) - run)
        pieces = []
        for pair in range(channels // 128):
            both = []
            for head in (2 * pair, 2 * pair + 1):
                decay = jnp.exp(run[:, head : head + 1] + behind[head : head + 1] + bias)
                both.append((decay * scores).astype(BF))
            pieces.append(dot(jnp.concatenate(both, axis=1), pair_blocks(u, pair, low)))
        mixed_o[rows, :] = jnp.concatenate(pieces, axis=1) + skip * u.astype(F32)


def mix_kernel(
    tile, channels,
    meta, inside, conv, deltas, gate, held, sums, cotangent, out_weight, table, spread, wedge, *rest, m, sources,
):
    mixed_o, stats_o, carry = rest[-3:]
    step = pl.program_id(0)

    @pl.when(step == 0)
    def _():
        carry[...] = joined([part[...] for part in rest[:sources]])[0]

    back = dot_nt(cotangent[...], out_weight[...]) * table[GATE : GATE + 1, :channels]
    docs = Docs(meta, m)
    first = docs.anchor + step * tile
    lanes_q = iota((Q, 128), 1)
    rate = table[RATE : RATE + 1, :128]
    parts = Tile(docs, first, deltas[...], rate, wedge[...])
    count = len(parts.parts)
    start = docs.counts(docs.anchor - 1)
    arrived = [jnp.exp(sums[c] + jnp.where(parts.before[c] == start, 0.0, NEVER)) for c in range(count)]
    wide = spread_heads([parts.entry(c) for c in range(count)] + arrived, spread[...])
    for c, rows in enumerate(parts.parts):
        reads = conv[rows, channels + 128 :]
        state = stacked(held[c] + wide[count + c][0:1] * carry[...], 0)
        mixed = inside[rows, :] + dot(twice(reads, 1), state) * wide[c]
        mixed_o[rows, :] = mixed
        gate_rows = gate[rows, :]
        gated = mixed * gate_rows * sigmoid(gate_rows)
        squares = jnp.sum(gated * gated, axis=1, keepdims=True)
        inner = jnp.sum(gated * back[rows], axis=1, keepdims=True)
        columns = jnp.where(lanes_q == 0, squares, jnp.where(lanes_q == 1, inner, 0.0))
        stats_o[:, rows] = jnp.transpose(columns)[0:8]


def third_kernel(
    tile, channels, full, chained, final,
    side, meta, mixed, gate, conv, deltas, normed, cotangent, out_weight, table, spread, wedge,
    stats_a, stats_b, stats_c, stats_d, *rest, m,
):
    if chained:
        grad_out_i, grad_gate_i, rows_i, *rest = rest
    grad_out, grad_gate, state, total = rest[-4:]
    *grads_o, rows_o = rest[: -4][-2 if final else -3 :]
    mine_o, other_o, gate_back_o, ssd_back_o, held_o, sums_o, leaving_o = rest[: -4 - len(grads_o) - 1][-7:]
    step = pl.program_id(0)
    gate_gain = table[GATE : GATE + 1, :channels]
    rate = table[RATE : RATE + 1, :128]
    docs = Docs(meta, m)
    place = pl.num_programs(0) - 1 - step
    first = docs.anchor + place * tile

    @pl.when(step == 0)
    def _():
        state[...] = jnp.zeros_like(state)
        total[...] = jnp.zeros_like(total)
        if chained:
            grad_out[...] = grad_out_i[...]
            grad_gate[...] = grad_gate_i[...]
            rows_o[...] = rows_i[...]
        else:
            grad_out[...] = jnp.zeros_like(grad_out)
            grad_gate[...] = jnp.zeros_like(grad_gate)
            rows_o[...] = jnp.zeros_like(rows_o)

    stats = stats_a[...] + stats_b[...] + stats_c[...] + stats_d[...]
    branches = []
    back = dot_nt(cotangent[...], out_weight[...])
    parts = Tile(docs, first, deltas[...], rate, wedge[...])
    count = len(parts.parts)
    wide = spread_heads(
        [parts.entry(c) for c in range(count)] + [wide_row(parts.overall(c)) for c in range(count)], spread[...]
    )
    for c in reversed(range(count)):
        rows = parts.parts[c]
        sides = jnp.transpose(jnp.concatenate([stats[:, rows], jnp.zeros((120, Q), F32)], axis=0))
        scale = lax.rsqrt(sides[:, 0:1] / full + EPS)
        inner = sides[:, 1:2]
        mixed_rows = mixed[rows, :]
        gate_rows = gate[rows, :]
        sigma = sigmoid(gate_rows)
        act = gate_rows * sigma
        gated = mixed_rows * act
        unit = gated * scale
        branch = (unit * gate_gain).astype(BF)
        branches.append(branch)
        back_rows = back[rows]
        grad_gated = scale * (back_rows * gate_gain) - unit * (scale * scale * (inner / full))
        grad_mixed = grad_gated * act
        gate_back_o[rows, :] = (grad_gated * mixed_rows * (sigma * (1.0 + gate_rows * (1.0 - sigma)))).astype(BF)
        ssd_back = grad_mixed.astype(BF)
        ssd_back_o[rows, :] = ssd_back
        u = conv[rows, :channels].astype(F32)
        rows_o[0:8, :] += jnp.sum((back_rows * unit).reshape(Q // 8, 8, channels), axis=0)
        rows_o[8:16, :] += jnp.sum((grad_mixed * u).reshape(Q // 8, 8, channels), axis=0)
        held_o[c] = state[...]
        sums_o[c] = total[...]
        total[...] = total[...] + parts.total[c]
        reads = conv[rows, channels + 128 :]
        entered = stacked(ssd_back.astype(F32) * wide[c], 0)
        state[...] = state[...] * wide[count + c][0:1] + dot_tn(twice(reads, 0), entered)
    branch = jnp.concatenate(branches[::-1], axis=0)
    part = dot(branch, out_weight[...]).astype(BF)
    here = place // (pl.num_programs(0) // 2) == side[0]

    @pl.when(here)
    def _():
        mine_o[...] = part

    @pl.when(jnp.logical_not(here))
    def _():
        other_o[...] = part

    grad_out[...] += dot_tn(branch, cotangent[...])
    grad_gate[...] += dot_tn(normed[...], gate_back_o[...])

    @pl.when(step == pl.num_programs(0) - 1)
    def _():
        if final:
            depth = grad_gate.shape[0]
            grads_o[0][:depth, :] = grad_gate[...].astype(BF)
            for block in range(grad_out.shape[1] // channels):
                lanes = slice(channels * block, channels * block + channels)
                grads_o[0][depth + channels * block : depth + channels * (block + 1), :] = grad_out[:, lanes].astype(BF)
        else:
            grads_o[0][...] = grad_out[...]
            grads_o[1][...] = grad_gate[...]
        end = docs.anchor + pl.num_programs(0) * tile - 1
        through = jnp.where(docs.counts(end) == docs.counts(docs.anchor - 1), 0.0, NEVER)
        leaving_o[...] = packed(state[...], spread_heads([jnp.exp(total[...] + through)], spread[...])[0][0:1])


def within_kernel(
    tile, channels,
    meta, conv, deltas, ssd_back, table, wedge, *rest, m, sources,
):
    grads_o, ends_o, near_o, send_o = rest[-4:]
    step = pl.program_id(0)

    @pl.when(step == 0)
    def _():
        state, decay = joined([part[...] for part in rest[:sources]])
        near_o[:STATES, :] = state
        near_o[STATES:, :] = jnp.broadcast_to(decay, (8, channels))
        send_o[...] = packed(state, decay)

    docs = Docs(meta, m)
    first = docs.anchor + step * tile
    lanes_q = iota((Q, 128), 1)
    rows_16 = iota((16, 128), 0)
    causal = iota((Q, Q), 1) >= iota((Q, Q), 0)
    low = lanes_q < 64
    skip = table[SKIP : SKIP + 1, :channels]
    rate = table[RATE : RATE + 1, :128]
    parts = Tile(docs, first, deltas[...], rate, wedge[...])
    for c, rows in enumerate(parts.parts):
        u = conv[rows, :channels]
        writes = conv[rows, channels : channels + 128]
        reads = conv[rows, channels + 128 :]
        grad = ssd_back[rows, :]
        scores = dot_nt(writes, reads)
        bias = jnp.where(parts.same(c) & causal, 0.0, NEVER)
        ahead = jnp.transpose(parts.run[c])
        behind = jnp.log(jnp.maximum(parts.deltas[c], TINY)) - parts.run[c]
        grad_scores = jnp.zeros((Q, Q), F32)
        by_source = jnp.zeros((Q, 128), F32)
        by_target = jnp.zeros((16, 128), F32)
        pieces = []
        for pair in range(channels // 128):
            blocks = pair_blocks(grad, pair, low)
            meets = dot_nt(u[:, 128 * pair : 128 * pair + 128], blocks)
            both = []
            for side in range(2):
                head = 2 * pair + side
                decay = jnp.exp(behind[:, head : head + 1] + ahead[head : head + 1] + bias)
                both.append((decay * scores).astype(BF))
                weighed = decay * meets[:, Q * side : Q * side + Q]
                grad_scores = grad_scores + weighed
                pairs = weighed * scores
                by_source = jnp.where(lanes_q == head, jnp.sum(pairs, axis=1, keepdims=True), by_source)
                by_target = jnp.where(rows_16 == head + 8, jnp.sum(pairs, axis=0, keepdims=True), by_target)
            pieces.append(dot(jnp.concatenate(both, axis=1), blocks))
        ends_o[rows, :] = by_source + jnp.transpose(jnp.concatenate([by_target, jnp.zeros((112, Q), F32)], axis=0))
        high, low_part = halves(grad_scores)
        grads_o[rows, :channels] = jnp.concatenate(pieces, axis=1) + skip * grad.astype(F32)
        grads_o[rows, channels : channels + 128] = dot(jnp.concatenate([high, low_part], axis=1), twice(reads, 0))
        grads_o[rows, channels + 128 :] = dot_tn(jnp.concatenate([high, low_part], axis=0), twice(writes, 0))


def across_kernel(
    tile, channels, chained,
    meta, conv, pre, xbc, edge, deltas, ssd_back, inside, ends,
    held, sums, carry, held_b, sums_b,
    table, spread, gather, wedge, wedge_up, wedge_below, *rest, m, sources,
):
    far, rest = rest[:sources], rest[sources:]
    if chained:
        taps_i, heads_i, *rest = rest
    in_back_o, dt_back_o, rim_o, tail_o, taps_o, heads_o, ext, grads, carry_b = rest[-9:]
    step = pl.program_id(0)
    docs = Docs(meta, m)
    places = pl.num_programs(0)
    place = places - 1 - step
    first = docs.anchor + place * tile
    end = docs.anchor + places * tile - 1
    width = pre.shape[1]
    taps = table[TAPS : TAPS + 4, :width]
    rate = table[RATE : RATE + 1, :128]
    lanes_q = iota((Q, 128), 1)

    @pl.when(step == 0)
    def _():
        if chained:
            taps_o[...] = taps_i[...]
            heads_o[...] = heads_i[...]
        else:
            taps_o[...] = jnp.zeros_like(taps_o)
            heads_o[...] = jnp.zeros_like(heads_o)
        carry_b[...] = joined([part[...] for part in far])[0]
        ext[:, 0:16, :] = jnp.zeros_like(ext[:, 0:16, :])
        ext[:, 16 + tile :, :] = jnp.zeros_like(ext[:, 16 + tile :, :])

    @pl.when(step > 0)
    def _():
        ext[:, 16 + tile :, :] = ext[:, 16:24, :]

    parts = Tile(docs, first, deltas[...], rate, wedge[...])
    count = len(parts.parts)
    start, stop = docs.counts(docs.anchor - 1), docs.counts(end)
    each = range(count)
    arrived = [jnp.exp(sums[c] + jnp.where(parts.before[c] == start, 0.0, NEVER)) for c in each]
    arrived_b = [jnp.exp(sums_b[c] + jnp.where(parts.last[c] == stop, 0.0, NEVER)) for c in each]
    wide = spread_heads(
        [parts.entry(c) for c in each] + [parts.leaving(c) for c in each] + arrived + arrived_b, spread[...]
    )
    crossings, products = [], []
    for c, rows in enumerate(parts.parts):
        u = conv[rows, :channels].astype(F32)
        writes = conv[rows, channels : channels + 128]
        reads = conv[rows, channels + 128 :]
        outward = wide[count + c]
        state = held[c] + wide[2 * count + c][0:1] * carry[...]
        state_b = held_b[c] + wide[3 * count + c][0:1] * carry_b[...]
        grad_in = ssd_back[rows, :].astype(F32) * wide[c]
        crossing = dot(twice(writes, 1), stacked(state_b, 0)) * outward
        products.append(u * crossing)
        crossings.append(grad_in * dot(twice(reads, 1), stacked(state, 0)))
        products.append(jnp.sum((state * state_b).reshape(16, 8, channels), axis=0))
        grads[rows, :channels] = inside[rows, :channels] + crossing
        grads[rows, channels : channels + 128] = inside[rows, channels : channels + 128] + near_f32(u * outward, state_b)
        grads[rows, channels + 128 :] = inside[rows, channels + 128 :] + near_f32(grad_in, state)
    gathered = gather_heads(crossings + products, gather[...])
    in_parts, out_parts = gathered[:count], gathered[count : count + 2 * count : 2]
    ups, sources = [], []
    for c, rows in enumerate(parts.parts):
        both_ends = ends[rows, :]
        sources.append(jnp.where(lanes_q < 8, both_ends, 0.0))
        target = jnp.where(lanes_q < 8, pltpu.roll(both_ends, 120, 1), 0.0)
        ups.append(in_parts[c] + target - sources[c])
    ups = add_up(ups, wedge_up[...])
    belows = add_up(out_parts, wedge_below[...])
    for c, rows in enumerate(parts.parts):
        between = jnp.sum(gathered[count + 2 * c + 1], axis=0, keepdims=True) * parts.overall(c)
        grad_run = between + ups[c] + belows[c]
        part_deltas = parts.deltas[c]
        slope = 1.0 - jnp.exp(-part_deltas)
        ratio = jnp.where(part_deltas > 1e-6, slope / jnp.maximum(part_deltas, 1e-6), 1.0)
        dt_back = (sources[c] + out_parts[c]) * ratio + rate * grad_run * slope
        dt_back_o[rows, :] = dt_back.astype(BF)
        heads_o[0:8, :] += jnp.sum(dt_back.reshape(Q // 8, 8, 128), axis=0)
        heads_o[8:16, :] += jnp.sum((grad_run * part_deltas).reshape(Q // 8, 8, 128), axis=0)

    plain = docs.none_near(first, tile)

    def convolve_back(masks):
        for slab in range(width // 128):
            lanes = slice(128 * slab, 128 * slab + 128)
            pre_rows = pre[:, lanes].astype(F32)
            sigma = sigmoid(pre_rows)
            grad_pre = grads[:, lanes] * (sigma * (1.0 + pre_rows * (1.0 - sigma)))
            source = xbc[:, lanes].astype(F32)
            result = taps[3:4, lanes] * grad_pre
            taps_o[24:32, lanes] += jnp.sum((grad_pre * source).reshape(tile // 8, 8, 128), axis=0)
            taps_o[32:40, lanes] += jnp.sum(grad_pre.reshape(tile // 8, 8, 128), axis=0)
            if masks is None:
                longer = jnp.concatenate([grad_pre, ext[0, 16 + tile :, lanes]], axis=0)
            for back in range(1, 4):
                if masks is None:
                    ext[back - 1, 16:24, lanes] = grad_pre[0:8]
                    moved = pltpu.roll(longer, tile + 8 - back, 0)[:tile]
                else:
                    ext[back - 1, 16 : 16 + tile, lanes] = grad_pre * masks[back - 1]
                    moved = ext[back - 1, 16 + back : 16 + back + tile, lanes]
                result = result + taps[3 - back : 4 - back, lanes] * moved
                taps_o[8 * (3 - back) : 8 * (4 - back), lanes] += jnp.sum(
                    (moved * source).reshape(tile // 8, 8, 128), axis=0
                )
            high = result.astype(BF)
            in_back_o[:, lanes] = high
            if 128 * slab >= channels:
                in_back_o[:, slice(256 + 128 * slab, 384 + 128 * slab)] = (result - high.astype(F32)).astype(BF)

            @pl.when(step == 0)
            def _():
                tail_o[:, lanes] = result[tile - RIM :]

    @pl.when(plain)
    def _():
        convolve_back(None)

    @pl.when(jnp.logical_not(plain))
    def _():
        convolve_back(docs.tap_masks(first, tile))

    @pl.when(place == 0)
    def _():
        total = jnp.zeros((RIM, width), F32)
        source = edge[...].astype(F32)
        for back in range(1, 4):
            moved = ext[back - 1, back : back + RIM, :]
            total = total + taps[3 - back : 4 - back, :] * moved
            taps_o[8 * (3 - back) : 8 * (4 - back), :] += jnp.sum((moved * source).reshape(RIM // 8, 8, width), axis=0)
        rim_o[...] = total


def part_kernel(
    tile, channels, chained, last, tiles,
    tokens, gate_back, in_back, dt_back, weights, *rest,
):
    if last:
        tail, rim, *rest = rest
    if chained:
        rows_i, *rest = rest
    part_o, rows_o, every = rest[-3:]
    step = pl.program_id(0)
    wide = in_back.shape[1]
    width = wide - 256

    @pl.when(step == 0)
    def _():
        rows_o[...] = rows_i[...] if chained else jnp.zeros_like(rows_o)

    every[:, :channels] = gate_back[...]
    every[:, channels : channels + wide] = in_back[...]
    every[:, channels + wide :] = dt_back[...]
    if last:

        @pl.when(step == tiles - 1)
        def _():
            high, low = halves(tail[...] + rim[...])
            every[tile - RIM :, channels : channels + width] = high
            every[tile - RIM :, channels + width : channels + wide] = low[:, channels:]

    x = tokens[...].astype(F32)
    scale = lax.rsqrt(jnp.mean(x * x, axis=1, keepdims=True) + EPS)
    part = dot_nt(every[...], weights[...])
    part_o[...] = part.astype(BF)
    rows_o[...] += jnp.sum((part * (x * scale)).reshape(tile // 8, 8, x.shape[1]), axis=0)


def weight_kernel(
    tile, channels, chained, tiles,
    normed, in_back, dt_back, tail, rim, *rest,
):
    if chained:
        grads_i, dt_i, *rest = rest
    grads_o, dt_o, every, total, dt_total = rest[-5:]
    step = pl.program_id(0)
    wide = in_back.shape[1]
    width = wide - 256

    @pl.when(step == 0)
    def _():
        total[...] = grads_i[...] if chained else jnp.zeros_like(total)
        dt_total[...] = jnp.zeros_like(dt_total)

    every[...] = in_back[...]

    @pl.when(step == tiles - 1)
    def _():
        high, low = halves(tail[...] + rim[...])
        every[tile - RIM :, :width] = high
        every[tile - RIM :, width:] = low[:, channels:]

    turned = jnp.transpose(normed[...])
    total[:, :channels] += dot(turned, every[:, :channels])
    total[:, channels:] += dot(
        twice(turned, 1), jnp.concatenate([every[:, channels:width], every[:, width:]], axis=0)
    )
    dt_total[...] += dot_nt(jnp.transpose(dt_back[...]), turned)

    @pl.when(step == tiles - 1)
    def _():
        grads_o[...] = total[...].astype(grads_o.dtype)
        dt_o[...] = dt_total[0:8] + dt_i[...] if chained else dt_total[0:8]


def place_kernel(
    token,
    side, mine, other, tokens, *rest,
):
    if token:
        cotangent, table, *rest = rest
    out = rest[-1]
    step = pl.program_id(0)

    def finish(total):
        x = tokens[...].astype(F32)
        total = total.astype(F32)
        if not token:
            return (x + total).astype(BF)
        scale = lax.rsqrt(jnp.mean(x * x, axis=1, keepdims=True) + EPS)
        grad_hat = total * table[GAIN : GAIN + 1, :]
        inner = jnp.mean(grad_hat * x, axis=1, keepdims=True)
        return (cotangent[...].astype(F32) + scale * grad_hat - x * (scale * scale * scale * inner)).astype(BF)

    here = step // (pl.num_programs(0) // 2) == side[0]

    @pl.when(here)
    def _():
        out[...] = finish(mine[...])

    @pl.when(jnp.logical_not(here))
    def _():
        out[...] = finish(other[...])


class Call:
    def __init__(self, kernel, steps, name):
        self.kernel, self.steps, self.name = kernel, steps, name
        self.args, self.in_specs, self.outs, self.out_specs, self.scratch = [], [], [], [], []
        self.aliases = {}

    def whole(self, *arrays):
        for array in arrays:
            self.args.append(array)
            self.in_specs.append(pl.BlockSpec(array.shape, lambda i, *s, rank=array.ndim: (0,) * rank))
        return self

    def scalars(self, array):
        self.args.append(array)
        self.in_specs.append(pl.BlockSpec(memory_space=pltpu.SMEM))
        return self

    def blocks(self, *arrays_specs):
        for array, spec in arrays_specs:
            self.args.append(array)
            self.in_specs.append(spec)
        return self

    def out(self, shape, dtype, spec=None):
        self.outs.append(jax.ShapeDtypeStruct(shape, dtype))
        self.out_specs.append(spec or pl.BlockSpec(shape, lambda i, *s, rank=len(shape): (0,) * rank))
        return self

    def after(self, *arrays):
        for array in arrays:
            self.args.append(array)
            self.in_specs.append(pl.BlockSpec(memory_space=pl.ANY))
        return self

    def alias(self, array):
        self.aliases = {len(self.args): 0}
        return self.after(array)

    def temp(self, shape, dtype):
        self.scratch.append(pltpu.VMEM(shape, dtype))
        return self

    def run(self, micros, scalars=None):
        ahead = () if scalars is None else (scalars,)
        return pl.pallas_call(
            self.kernel,
            grid_spec=pltpu.PrefetchScalarGridSpec(
                num_scalar_prefetch=len(ahead),
                grid=(self.steps,),
                in_specs=self.in_specs,
                out_specs=tuple(self.out_specs),
                scratch_shapes=self.scratch,
            ),
            out_shape=tuple(self.outs),
            input_output_aliases={at + len(ahead): to for at, to in self.aliases.items()},
            compiler_params=pltpu.CompilerParams(
                dimension_semantics=("arbitrary",), vmem_limit_bytes=VMEM_BYTES
            ),
            cost_estimate=pl.CostEstimate(flops=int(micros * SCALE * 1.15e9), bytes_accessed=0, transcendentals=0),
            name=self.name,
        )(*ahead, *self.args)


def swap(value, axis, bits):
    count = lax.axis_size(axis)
    return lax.ppermute(value, axis, [(i, i ^ bits) for i in range(count)])


def from_behind(value, axis, steps):
    count = lax.axis_size(axis)
    sources = range(max(0, -steps), min(count, count - steps))
    return lax.ppermute(value, axis, [(i, i + steps) for i in sources])


def packed(state, decay):
    high, low = halves(jnp.broadcast_to(decay, (8, decay.shape[1])))
    return jnp.concatenate([state.astype(BF), high, low], axis=0)


def unpacked(part):
    if part.dtype == F32:
        return part[:STATES], part[STATES : STATES + 1]
    part = part.astype(F32)
    return part[:STATES], part[STATES : STATES + 1] + part[STATES + 8 : STATES + 9]


def joined(parts):
    state, decay = unpacked(parts[0])
    for part in parts[1:]:
        more, keep = unpacked(part)
        state = state + decay * more
        decay = decay * keep
    return state, decay


def near_parts(leaving, axis, sign):
    return [from_behind(leaving, axis, sign * k) for k in range(1, min(4, lax.axis_size(axis)))]


def far_parts(carry, sent, axis, sign):
    count = lax.axis_size(axis)
    window = 3
    parts = [carry]
    while window < count - 1:
        if len(parts) > 1:
            state, decay = joined(parts)
            sent = packed(state, decay)
            carry = jnp.concatenate([state, jnp.broadcast_to(decay, (8, decay.shape[1]))], axis=0)
        parts = [carry] + [from_behind(sent, axis, sign * k) for k in (window, 2 * window) if k < count]
        window *= 3
    return parts


def sum_rows(parts):
    total = parts[0].astype(F32)
    for part in parts[1:]:
        total = total + part.astype(F32)
    return total


def pair_sum(mine, other):
    return (mine.astype(F32) + swap(other, "head", 1).astype(F32)).astype(BF)


def head_pair(part):
    rows = part.shape[0] // 2
    side = lax.axis_index("head") % 2
    mine = lax.dynamic_slice_in_dim(part, side * rows, rows, 0)
    return pair_sum(mine, lax.dynamic_slice_in_dim(part, (1 - side) * rows, rows, 0))


def head_rest(low):
    bit = 2
    while bit < lax.axis_size("head"):
        low = (low.astype(F32) + swap(low, "head", bit).astype(F32)).astype(BF)
        bit *= 2
    return low


class Reduction:
    def __init__(self, value, axis):
        self.value, self.axis, self.bits, self.out = value, axis, 1, True
        self.count, self.me = lax.axis_size(axis), lax.axis_index(axis)
        self.start()

    def start(self):
        if self.out:
            rows, half = self.value.shape[0] // 2, self.me // self.bits % 2
            sent = lax.dynamic_slice_in_dim(self.value, (1 - half) * rows, rows, 0)
            self.value = lax.dynamic_slice_in_dim(self.value, half * rows, rows, 0)
        else:
            sent = self.value
        self.other = swap(sent, self.axis, self.bits)

    def done(self):
        return not self.out and self.bits == 0

    def step(self, after):
        other, _ = lax.optimization_barrier((self.other, after))
        if self.out:
            self.value = (self.value.astype(F32) + other.astype(F32)).astype(BF)
            self.out = self.bits * 2 < self.count
            self.bits = self.bits * 2 if self.out else self.bits
        else:
            first = self.me // self.bits % 2 == 0
            pieces = [jnp.where(first, self.value, other), jnp.where(first, other, self.value)]
            self.value = jnp.concatenate(pieces, axis=0)
            self.bits //= 2
        if not self.done():
            self.start()


def pair_parts(value, axis):
    rows = value.shape[0] // 2
    half = lax.axis_index(axis) % 2
    mine = lax.dynamic_slice_in_dim(value, half * rows, rows, 0)
    return mine, swap(lax.dynamic_slice_in_dim(value, (1 - half) * rows, rows, 0), axis, 1)


def scatter_parts(value, axis):
    count = lax.axis_size(axis) // 2
    me = lax.axis_index(axis) // 2
    rows = value.shape[0] // count
    parts = [lax.dynamic_slice_in_dim(value, me * rows, rows, 0)]
    for bits in range(1, count):
        piece = lax.dynamic_slice_in_dim(value, jnp.bitwise_xor(me, bits) * rows, rows, 0)
        parts.append(swap(piece, axis, 2 * bits))
    return parts


def gather_half(value, axis):
    count = lax.axis_size(axis) // 2
    me = lax.axis_index(axis) // 2
    rows = value.shape[0]
    result = jnp.zeros((count * rows, value.shape[1]), value.dtype)
    result = lax.dynamic_update_slice_in_dim(result, value, me * rows, 0)
    for bits in range(1, count):
        result = lax.dynamic_update_slice_in_dim(
            result, swap(value, axis, 2 * bits), jnp.bitwise_xor(me, bits) * rows, 0
        )
    return result


def gather_pair(half, axis):
    other = swap(half, axis, 1)
    first = lax.axis_index(axis) % 2 == 0
    return jnp.concatenate([jnp.where(first, half, other), jnp.where(first, other, half)], axis=0)


def add_swaps(value, axis):
    return sum_rows([value] + [swap(value, axis, bits) for bits in range(1, lax.axis_size(axis))])


def all_sum(value, axis):
    bit = 1
    while bit < lax.axis_size(axis):
        value = value + swap(value, axis, bit)
        bit *= 2
    return value


def local(
    tokens,
    doc_starts,
    norm_gain,
    gate_x_weight,
    bc_weight,
    dt_weight,
    conv_x_weight,
    conv_x_bias,
    conv_bc_weight,
    conv_bc_bias,
    dt_bias,
    a_log,
    d_skip,
    gate_gain,
    out_weight,
    cotangent,
):
    micro, length, model = tokens.shape
    channels = gate_x_weight.shape[2]
    heads = dt_weight.shape[1]
    dim = channels // heads
    states = bc_weight.shape[1] // 2
    width = channels + 2 * states
    full = channels * lax.axis_size("head")
    tile, small = min(TILE, length), min(SMALL, length)
    steps = length // tile
    per = tile // Q
    blocks = length // Q

    rim_tokens = from_behind(tokens[:, length - RIM :], "seq", 1)
    weights = jnp.concatenate(
        [gate_x_weight[:, 0], gate_x_weight[:, 1], bc_weight, bc_weight,
         jnp.pad(dt_weight, ((0, 0), (0, 128 - heads)))], axis=1
    )
    decay_rate = -jnp.exp(a_log)

    def table_rows(*parts):
        row = jnp.concatenate(parts, axis=-1)
        row = row if row.ndim == 2 else row[None]
        return jnp.pad(row, ((0, 0), (0, model - row.shape[1])))

    table = jnp.concatenate(
        [
            table_rows(norm_gain),
            table_rows(conv_x_weight, conv_bc_weight),
            table_rows(conv_x_bias, conv_bc_bias),
            table_rows(gate_gain),
            table_rows(jnp.repeat(d_skip, dim)),
            table_rows(decay_rate),
            table_rows(dt_bias, jnp.full((128 - heads,), -200.0, F32)),
            jnp.zeros((TABLE - BIAS - 1, model), F32),
        ],
        axis=0,
    )
    owner = np.arange(channels)[None, :] // dim == np.arange(128)[:, None]
    spread = np.concatenate([owner, owner], axis=0).astype(BF)
    gather = np.concatenate([owner.T, owner.T], axis=0).astype(BF)
    order = np.arange(Q)
    until_here = order[:, None] >= order[None, :]
    below = order[:, None] > order[None, :]
    wedge = np.concatenate([until_here] * 2, axis=1).astype(BF)
    wedge_up = np.concatenate([until_here.T] * 2, axis=1).astype(BF)
    wedge_below = np.concatenate([below] * 2, axis=1).astype(BF)
    anchor = lax.axis_index("seq") * length
    meta = jnp.concatenate(
        [jnp.where(doc_starts >= 1, doc_starts, 2**30), jnp.full((micro, 1), anchor)], axis=1
    ).astype(jnp.int32)

    side = (lax.axis_index("head") % 2).astype(jnp.int32)[None]
    ahead = lambda i: i
    astern = lambda i: steps - 1 - i

    def rows_of(cols, turn, rows=tile):
        return pl.BlockSpec((rows, cols), lambda i, *s: (turn(i), 0))

    def rows_in(m, cols, turn):
        return pl.BlockSpec((None, tile, cols), lambda i, *s: (m, turn(i), 0))

    def chunks_of(turn, rows, cols):
        return pl.BlockSpec((per, rows, cols), lambda i, *s: (turn(i), 0, 0))

    def stat_spec(turn):
        return pl.BlockSpec((8, tile), lambda i, *s: (0, turn(i)))

    def project(m, *waits):
        call = Call(partial(first_kernel, tile, channels, m=m), steps, f"project_{m}")
        call.scalars(meta)
        call.blocks((rim_tokens, pl.BlockSpec((None, RIM, model), lambda i, *s: (m, 0, 0))))
        call.blocks((tokens, rows_in(m, model, ahead)))
        call.whole(weights, table, spread, wedge).after(*waits)
        call.out((length, model), BF, rows_of(model, ahead))
        call.out((length, channels), F32, rows_of(channels, ahead))
        call.out((length, width), BF, rows_of(width, ahead))
        call.out((length, width), BF, rows_of(width, ahead))
        call.out((length, width), BF, rows_of(width, ahead))
        call.out((length, 128), F32, rows_of(128, ahead))
        call.out((blocks, 128, channels), F32, chunks_of(ahead, 128, channels))
        call.out((blocks, 8, 128), F32, chunks_of(ahead, 8, 128))
        call.out((STATES + 16, channels), BF)
        call.out((RIM, width), BF)
        call.temp((tile + 8, width), F32).temp((128, channels), F32).temp((8, 128), F32)
        return call.run(22)

    def inside(m, kept, parts, *waits):
        conv, deltas = kept[4:6]
        call = Call(partial(inside_kernel, tile, channels, m=m, sources=len(parts)), steps, f"inside_{m}")
        call.scalars(meta)
        call.blocks((conv, rows_of(width, ahead)), (deltas, rows_of(128, ahead)))
        call.whole(table, wedge, *parts).after(*waits)
        call.out((length, channels), F32, rows_of(channels, ahead))
        call.out((STATES + 8, channels), F32).out((STATES + 16, channels), BF)
        return call.run(11)

    def mix(m, kept, inner, parts, *waits):
        normed, gate, xbc, pre, conv, deltas, held, sums = kept[:8]
        call = Call(partial(mix_kernel, tile, channels, m=m, sources=len(parts)), steps, f"mix_{m}")
        call.scalars(meta)
        call.blocks(
            (inner, rows_of(channels, ahead)),
            (conv, rows_of(width, ahead)),
            (deltas, rows_of(128, ahead)),
            (gate, rows_of(channels, ahead)),
            (held, chunks_of(ahead, 128, channels)),
            (sums, chunks_of(ahead, 8, 128)),
            (cotangent, rows_in(m, model, ahead)),
        )
        call.whole(out_weight, table, spread, wedge, *parts).after(*waits)
        call.out((length, channels), F32, rows_of(channels, ahead))
        call.out((8, length), F32, stat_spec(ahead))
        call.out((STATES, channels), F32)
        return call.run(12)

    def norm(m, kept, mixed, stats, chain, *waits):
        normed, gate, xbc, pre, conv, deltas = kept[:6]
        final = m + 1 == micro
        call = Call(partial(third_kernel, tile, channels, float(full), bool(chain), final, m=m), steps, f"gate_{m}")
        call.scalars(meta)
        call.blocks(
            (mixed, rows_of(channels, astern)),
            (gate, rows_of(channels, astern)),
            (conv, rows_of(width, astern)),
            (deltas, rows_of(128, astern)),
            (normed, rows_of(model, astern)),
            (cotangent, rows_in(m, model, astern)),
        )
        call.whole(out_weight, table, spread, wedge)
        call.blocks(*[(part, stat_spec(astern)) for part in stats])
        call.whole(*chain).after(*waits)
        half = steps // 2

        def spot(flip):
            return pl.BlockSpec(
                (tile, model),
                lambda i, s: (jnp.clip(astern(i) - (s[0] if flip == 0 else 1 - s[0]) * half, 0, half - 1), 0),
            )

        call.out((length // 2, model), BF, spot(0)).out((length // 2, model), BF, spot(1))
        call.out((length, channels), BF, rows_of(channels, astern))
        call.out((length, channels), BF, rows_of(channels, astern))
        call.out((blocks, 128, channels), F32, chunks_of(astern, 128, channels))
        call.out((blocks, 8, 128), F32, chunks_of(astern, 8, 128))
        call.out((STATES + 16, channels), BF)
        if final:
            call.out((2 * model, channels), BF)
        else:
            call.out((channels, model), F32)
            call.out((model, channels), F32)
        call.out((16, channels), F32)
        call.temp((channels, model), F32).temp((model, channels), F32)
        call.temp((128, channels), F32).temp((8, 128), F32)
        return call.run(17, side)

    def within(m, kept, ssd_back, parts, *waits):
        conv, deltas = kept[4:6]
        call = Call(partial(within_kernel, small, channels, m=m, sources=len(parts)), length // small, f"within_{m}")
        call.scalars(meta)
        call.blocks((conv, rows_of(width, ahead, small)), (deltas, rows_of(128, ahead, small)), (ssd_back, rows_of(channels, ahead, small)))
        call.whole(table, wedge, *parts).after(*waits)
        call.out((length, width), F32, rows_of(width, ahead, small))
        call.out((length, 128), F32, rows_of(128, ahead, small))
        call.out((STATES + 8, channels), F32).out((STATES + 16, channels), BF)
        return call.run(3)

    def across(m, kept, carry, third, inner, parts, chain, *waits):
        normed, gate, xbc, pre, conv, deltas, held, sums, leaving, edge = kept
        call = Call(partial(across_kernel, tile, channels, bool(chain), m=m, sources=len(parts)), steps, f"across_{m}")
        call.scalars(meta)
        call.blocks((conv, rows_of(width, astern)), (pre, rows_of(width, astern)), (xbc, rows_of(width, astern)))
        call.whole(edge)
        call.blocks(
            (deltas, rows_of(128, astern)),
            (third[3], rows_of(channels, astern)),
            (inner[0], rows_of(width, astern)),
            (inner[1], rows_of(128, astern)),
            (held, chunks_of(astern, 128, channels)),
            (sums, chunks_of(astern, 8, 128)),
        )
        call.whole(carry)
        call.blocks((third[4], chunks_of(astern, 128, channels)), (third[5], chunks_of(astern, 8, 128)))
        call.whole(table, spread, gather, wedge, wedge_up, wedge_below, *parts, *chain).after(*waits)
        call.out((length, width + 256), BF, rows_of(width + 256, astern))
        call.out((length, 128), BF, rows_of(128, astern))
        call.out((RIM, width), F32)
        call.out((RIM, width), F32)
        call.out((40, width), F32)
        call.out((16, 128), F32)
        call.temp((3, tile + 24, width), F32).temp((tile, width), F32).temp((STATES, channels), F32)
        return call.run(10)

    def part_of(m, gate_back, fourth, span, rows, rim, chain, earlier, micros, *waits):
        count = span[1] - span[0]
        turn = lambda i: i + span[0]
        put = lambda i: i + span[0] - rows[0]
        call = Call(partial(part_kernel, tile, channels, bool(chain), rim is not None, count), count, f"input_{m}_{span[0]}")
        call.blocks(
            (tokens, rows_in(m, model, turn)),
            (gate_back, rows_of(channels, turn)),
            (fourth[0], rows_of(width + 256, turn)),
            (fourth[1], rows_of(128, turn)),
        )
        call.whole(weights)
        if rim is not None:
            call.whole(fourth[3], rim)
        call.whole(*chain)
        if earlier is not None:
            call.alias(earlier)
        call.after(*waits)
        call.out((rows[1] * tile, model), BF, rows_of(model, put))
        call.out((8, model), F32)
        call.temp((tile, channels + width + 256 + 128), BF)
        return call.run(micros)

    def weight_back(m, kept, fourth, rim, chain, kind, *waits):
        call = Call(partial(weight_kernel, tile, channels, bool(chain), steps), steps, f"weigh_{m}")
        call.blocks(
            (kept[0], rows_of(model, ahead)), (fourth[0], rows_of(width + 256, ahead)), (fourth[1], rows_of(128, ahead))
        )
        call.whole(fourth[3], rim, *chain).after(*waits)
        call.out((model, width), kind)
        call.out((8, model), F32)
        call.temp((tile, width + 256), BF).temp((model, width), F32).temp((128, model), F32)
        return call.run(8)

    def place(m, begin, low, other, token, earlier, *waits):
        big = min(512, low.shape[0])
        half = low.shape[0] // big
        call = Call(partial(place_kernel, token), 2 * half, f"place_{m}_{begin}_{token:d}")

        def source(flip):
            return pl.BlockSpec(
                (big, model), lambda i, s: (jnp.clip(i - (s[0] if flip == 0 else 1 - s[0]) * half, 0, half - 1), 0)
            )

        spot = pl.BlockSpec((None, big, model), lambda i, s: (m, i + begin // big, 0))
        call.blocks((low, source(0)), (other, source(1)), (tokens, spot))
        if token:
            call.blocks((cotangent, spot))
            call.args.append(table)
            call.in_specs.append(pl.BlockSpec(table.shape, lambda i, s: (0, 0)))
        if earlier is not None:
            call.alias(earlier)
        call.after(*waits)
        call.out((micro, length, model), BF, spot)
        return call.run(4, side)[0]

    every = range(micro)
    kept, inner, mixes, thirds, order_by, chain = [], [], [], [], [], ()
    for m in every:
        kept.append(project(m, *order_by))
        order_by = [kept[m][8]]
    for m in every:
        inner.append(inside(m, kept[m], near_parts(kept[m][8], "seq", 1), *order_by))
        order_by = [inner[m][1]]
    for m in every:
        mixes.append(mix(m, kept[m], inner[m][0], far_parts(inner[m][1], inner[m][2], "seq", 1), *order_by))
        order_by = [mixes[m][1]]
    for m in every:
        stats = [mixes[m][1]] + [swap(mixes[m][1], "head", bits) for bits in range(1, lax.axis_size("head"))]
        thirds.append(norm(m, kept[m], mixes[m][0], stats, chain, *order_by))
        chain = thirds[m][7:]
        order_by = [thirds[m][6]]
    packed_grads, gate_rows = chain
    reduction = Reduction(packed_grads, "seq")
    mixed_pair = [pair_sum(thirds[m][0], thirds[m][1]) for m in every]
    mixed_all = [head_rest(mixed_pair[m]) for m in every]
    inner_b, fourths, chain = [], [], ()
    for m in every:
        near = near_parts(thirds[m][6], "seq", -1)
        inner_b.append(within(m, kept[m], thirds[m][3], near, mixed_pair[m], *order_by))
        order_by = [inner_b[m][2]]
        reduction.step(inner_b[m][2])
    far = [far_parts(inner_b[m][2], inner_b[m][3], "seq", -1) for m in every]
    order_by.append(mixed_all[0])
    mixed_other = [swap(mixed_all[m], "head", 1) for m in every]
    token_other = []
    gain_rows, grads, token_all, half_steps = (), (), [], steps // 2
    for m in every:
        final = m + 1 == micro
        fourths.append(across(m, kept[m], mixes[m][2], thirds[m], inner_b[m], far[m], chain, *order_by))
        chain = fourths[m][4:6]
        if not reduction.done():
            reduction.step(fourths[m][4])
        rim = from_behind(fourths[m][2], "seq", -1)
        gate_back = thirds[m][2]
        if not final:
            both = (0, steps)
            first = part_of(m, gate_back, fourths[m], (0, half_steps), both, None, gain_rows, None, 6, mixed_all[m + 1], *far[m + 1])
            second = part_of(m, gate_back, fourths[m], (half_steps, steps), both, rim, first[1:], first[0], 6)
            grads = weight_back(m, kept[m], fourths[m], rim, grads, F32, second[1])
            reduction.step(second[1])
            reduction.step(grads[1])
            pair = head_pair(second[0])
            token_all.append(head_rest(pair))
            token_other.append(swap(token_all[m], "head", 1))
            gain_rows = second[1:]
            order_by = [pair, grads[1]]
        else:
            first = part_of(m, gate_back, fourths[m], (0, half_steps), (0, half_steps), None, gain_rows, None, 6, token_all[-1], *mixed_other)
            pair = head_pair(first[0])
            second = part_of(
                m, gate_back, fourths[m], (half_steps, steps), (half_steps, half_steps), rim, first[1:], None, 6
            )
            grads = weight_back(m, kept[m], fourths[m], rim, grads, BF, second[1], pair, *token_other)
            gain_rows = second[1:]
            last_pair = [pair, head_pair(second[0])]
    tap_rows, head_rows = chain
    grads, dt_rows = grads
    gain_rows = gain_rows[0]

    def folded(rows):
        return jnp.sum(rows.reshape(-1, 8, rows.shape[1]), axis=1)

    by_tap = folded(tap_rows)
    by_row = folded(gate_rows)
    by_head = folded(head_rows)[:, :heads]
    skip_sum = jnp.sum(by_row[1].reshape(heads, dim), axis=1)
    small = jnp.concatenate(
        [by_tap[:, channels:].reshape(-1), jnp.sum(gain_rows, axis=0), dt_rows[:heads].reshape(-1),
         by_tap[:, :channels].reshape(-1), by_row[0], by_head.reshape(-1), skip_sum]
    )
    small = jnp.pad(small, (0, -small.size % 1024)).reshape(-1, 128)
    shared_size = by_tap[:, channels:].size + model
    halved = pair_parts(grads, "seq")
    last_all = [head_rest(last_pair[0])]
    halved, last_pair = lax.optimization_barrier((halved, last_pair))
    last_all.append(head_rest(last_pair[1]))
    halved = sum_rows(halved).astype(BF)
    pieces = scatter_parts(halved, "seq")
    small = all_sum(lax.optimization_barrier((small, halved))[0], "seq")
    mixed_out = place(0, 0, mixed_all[0], mixed_other[0], False, None, halved, last_all[0])
    pieces, mixed_out = lax.optimization_barrier((pieces, mixed_out))
    part = sum_rows(pieces)
    while not reduction.done():
        reduction.step(part)
    packed_grads = reduction.value
    share = 2 * states // lax.axis_size("head")
    bc_parts = [part[:, channels:width]]
    bc_parts += [swap(bc_parts[0], "head", bits) for bits in range(1, lax.axis_size("head"))]
    for m in range(1, micro):
        mixed_out = place(m, 0, mixed_all[m], mixed_other[m], False, mixed_out, part, last_all[1])
    bc_parts, mixed_out = lax.optimization_barrier((bc_parts, mixed_out))
    bc_mine = lax.dynamic_slice_in_dim(sum_rows(bc_parts), lax.axis_index("head") * share, share, 1)
    payload = jnp.concatenate(
        [part[:, :channels], bc_mine, jnp.zeros((part.shape[0], -share % 128), F32)], axis=1
    ).astype(BF)
    gathered = gather_half(payload, "seq")
    token_grad = None
    for m in range(micro - 1):
        token_grad = place(m, 0, token_all[m], token_other[m], True, token_grad, payload)
    gathered, token_grad = lax.optimization_barrier((gathered, token_grad))
    gathered = gather_pair(gathered, "seq")
    grad_x = gathered[:, :channels].astype(F32)
    grad_bc = gathered[:, channels : channels + share].astype(F32)

    token_grad = place(micro - 1, 0, last_all[0], swap(last_all[0], "head", 1), True, token_grad)
    last_other = swap(last_all[1], "head", 1)
    token_grad = place(micro - 1, length // 2, last_all[1], last_other, True, token_grad)

    tap_count = conv_x_weight.shape[0]
    shared, _ = lax.optimization_barrier((small[: shared_size // 128], payload))
    shared = add_swaps(shared, "head").reshape(-1)
    rest = small[shared_size // 128 :].reshape(-1)
    bc_taps = shared[: (tap_count + 1) * 2 * states].reshape(tap_count + 1, 2 * states)
    grad_norm_gain = shared[(tap_count + 1) * 2 * states :]
    grad_dt = rest[: heads * model].reshape(heads, model).T
    rest = rest[heads * model :]
    cut = (tap_count + 1) * channels
    x_taps = rest[:cut].reshape(tap_count + 1, channels)
    grad_gate_gain = rest[cut : cut + channels]
    tails = rest[cut + channels : cut + channels + 3 * heads].reshape(3, heads)
    grad_gate = packed_grads[:model].astype(F32)
    grad_out = jnp.concatenate(
        [packed_grads[row : row + channels] for row in range(model, 2 * model, channels)], axis=1
    ).astype(F32)
    return (
        mixed_out,
        token_grad,
        grad_norm_gain,
        jnp.stack([grad_gate, grad_x], axis=1),
        grad_bc,
        grad_dt,
        x_taps[:tap_count],
        x_taps[tap_count],
        bc_taps[:tap_count],
        bc_taps[tap_count],
        tails[0],
        tails[1] * decay_rate,
        tails[2],
        grad_gate_gain,
        grad_out,
    )


def solution(mesh):
    in_specs = (
        P(None, "seq", None),
        P(),
        P(),
        P(None, None, "head"),
        P(),
        P(None, "head"),
        P(None, "head"),
        P("head"),
        P(),
        P(),
        P("head"),
        P("head"),
        P("head"),
        P("head"),
        P("head", None),
        P(None, "seq", None),
    )
    out_specs = (
        P(None, "seq", None),
        P(None, "seq", None),
        P(),
        P(None, None, "head"),
        P(None, "head"),
        P(None, "head"),
        P(None, "head"),
        P("head"),
        P(),
        P(),
        P("head"),
        P("head"),
        P("head"),
        P("head"),
        P("head", None),
    )
    return jax.shard_map(local, mesh=mesh, in_specs=in_specs, out_specs=out_specs, check_vma=False)
```

```python
from functools import partial

import jax
import jax.numpy as jnp
import numpy as np
from jax import lax
from jax.experimental import pallas as pl
from jax.experimental.pallas import tpu as pltpu
from jax.sharding import PartitionSpec as P

EPS = 1e-05
Q = 128
STATES = 128
TILE = 512
SMALL = 256
RIM = 16
NEVER = -1e30
TINY = 1e-37
BF = jnp.bfloat16
F32 = jnp.float32
VMEM_BYTES = 48 * 2**20
SCALE = 1.0
GAIN, TAPS, SHIFT, GATE, SKIP, RATE, BIAS, TABLE = 0, 1, 5, 6, 7, 8, 9, 16


def dot(a, b):
    return jnp.dot(a, b, preferred_element_type=F32)


def dot_nt(a, b):
    return lax.dot_general(a, b, (((1,), (1,)), ((), ())), preferred_element_type=F32)


def dot_tn(a, b):
    return lax.dot_general(a, b, (((0,), (0,)), ((), ())), preferred_element_type=F32)


def halves(value):
    high = value.astype(BF)
    return high, (value - high.astype(F32)).astype(BF)


def twice(value, axis):
    return jnp.concatenate([value, value], axis=axis)


def stacked(value, axis):
    return jnp.concatenate(halves(value), axis=axis)


def cut_rows(value, likes):
    pieces, at = [], 0
    for like in likes:
        pieces.append(value[at : at + like.shape[0]])
        at += like.shape[0]
    return pieces


def spread_heads(values, spread):
    both = stacked(jnp.concatenate(values, axis=0), 1)
    return cut_rows(dot(both, spread), values)


def gather_heads(values, gather):
    both = stacked(jnp.concatenate(values, axis=0), 1)
    return cut_rows(dot(both, gather), values)


def add_up(values, wedge):
    result = dot(wedge, jnp.concatenate([stacked(value, 0) for value in values], axis=1))
    return [result[:, 128 * c : 128 * c + 128] for c in range(len(values))]


def near_f32(left, right):
    rows, columns = left.shape[0], right.shape[0]
    product = dot_nt(stacked(left, 0), stacked(right, 0))
    return product[:rows, :columns] + product[:rows, columns:] + product[rows:, :columns]


def sigmoid(value):
    return jax.nn.sigmoid(value)


def softplus(value):
    return jnp.maximum(value, 0.0) + jnp.log1p(jnp.exp(-jnp.abs(value)))


def iota(shape, axis):
    return lax.broadcasted_iota(jnp.int32, shape, axis)


class Docs:
    def __init__(self, meta, m):
        self.count = meta.shape[1] - 1
        self.starts = [meta[m, j] for j in range(self.count)]
        self.anchor = meta[m, self.count]

    def counts(self, places):
        total = (places >= self.starts[0]).astype(jnp.int32)
        for start in self.starts[1:]:
            total = total + (places >= start).astype(jnp.int32)
        return total

    def starts_at(self, places):
        hit = places == self.starts[0]
        for start in self.starts[1:]:
            hit = hit | (places == start)
        return hit

    def none_near(self, first, rows):
        near = (self.starts[0] >= first - 2) & (self.starts[0] <= first + rows + 2)
        for start in self.starts[1:]:
            near = near | ((start >= first - 2) & (start <= first + rows + 2))
        return jnp.logical_not(near)

    def tap_masks(self, first, rows):
        places = first + iota((rows, 128), 0)
        masks = []
        broken = None
        for back in range(3):
            hit = self.starts_at(places - back)
            broken = hit if broken is None else broken | hit
            masks.append(jnp.where(broken, 0.0, 1.0))
        return masks


class Tile:
    def __init__(self, docs, first, deltas, rate, wedge):
        count = deltas.shape[0] // Q
        self.docs, self.first = docs, first
        self.parts = [slice(Q * c, Q * c + Q) for c in range(count)]
        self.deltas = [deltas[rows] for rows in self.parts]
        runs = add_up([part * rate for part in self.deltas], wedge)
        self.run = runs
        self.total = [run[Q - 1 : Q] for run in runs]
        self.before = [docs.counts(first + Q * c - 1) for c in range(count)]
        self.last = [docs.counts(first + Q * c + Q - 1) for c in range(count)]
        self.column = [docs.counts(first + Q * c + iota((Q, 128), 0)) for c in range(count)]

    def same(self, c):
        return self.column[c] == self.docs.counts(self.first + Q * c + iota((8, 128), 1))[0:1]

    def entry(self, c):
        return jnp.exp(self.run[c] + jnp.where(self.column[c] == self.before[c], 0.0, NEVER))

    def leaving(self, c):
        bias = jnp.where(self.column[c] == self.last[c], 0.0, NEVER)
        return jnp.exp(self.total[c] - self.run[c] + bias) * self.deltas[c]

    def overall(self, c):
        return jnp.exp(self.total[c] + jnp.where(self.last[c] == self.before[c], 0.0, NEVER))


def wide_row(row):
    return jnp.broadcast_to(row, (8, row.shape[1]))


def pair_blocks(value, pair, lanes):
    both = value[:, 128 * pair : 128 * pair + 128]
    zero = jnp.zeros_like(both)
    return jnp.concatenate([jnp.where(lanes, both, zero), jnp.where(lanes, zero, both)], axis=0)


def first_kernel(
    tile, channels,
    meta, rim, tokens, weights, table, spread, wedge, *rest, m,
):
    normed_o, gate_o, xbc_o, pre_o, conv_o, deltas_o, held_o, sums_o, leaving_o, edge_o, ext, state, total = rest[-13:]
    step = pl.program_id(0)
    docs = Docs(meta, m)
    width = xbc_o.shape[1]
    taps = table[TAPS : TAPS + 4, :width]
    shift = table[SHIFT : SHIFT + 1, :width]
    gain = table[GAIN : GAIN + 1, : tokens.shape[1]]
    rate = table[RATE : RATE + 1, :128]
    dt_bias = table[BIAS : BIAS + 1, :128]

    def normalize(rows):
        x = rows.astype(F32)
        scale = lax.rsqrt(jnp.mean(x * x, axis=1, keepdims=True) + EPS)
        return (x * scale * gain).astype(BF)

    @pl.when(step == 0)
    def _():
        edge = dot(normalize(rim[...]), weights[:, channels : channels + width]).astype(BF)
        edge_o[...] = edge
        ext[0:8, :] = edge.astype(F32)[RIM - 8 :]
        state[...] = jnp.zeros_like(state)
        total[...] = jnp.zeros_like(total)

    @pl.when(step > 0)
    def _():
        ext[0:8, :] = ext[tile : tile + 8, :]

    normed = normalize(tokens[...])
    normed_o[...] = normed
    gate_o[...] = dot(normed, weights[:, :channels])
    xbc = dot(normed, weights[:, channels : channels + width]).astype(BF)
    xbc_o[...] = xbc
    ext[8:, :] = xbc.astype(F32)
    deltas = softplus(dot(normed, weights[:, channels + width + 256 :]) + dt_bias)
    deltas_o[...] = deltas
    first = docs.anchor + step * tile
    plain = docs.none_near(first, tile)

    def convolve(masks):
        for slab in range(width // 128):
            lanes = slice(128 * slab, 128 * slab + 128)
            if masks is None:
                source = ext[:, lanes]
                pre = shift[:, lanes] + taps[3:4, lanes] * source[8:]
            else:
                pre = shift[:, lanes] + taps[3:4, lanes] * ext[8 : 8 + tile, lanes]
            for back in range(1, 4):
                if masks is None:
                    moved = pltpu.roll(source, back, 0)[8:]
                else:
                    moved = ext[8 - back : 8 - back + tile, lanes] * masks[back - 1]
                pre = pre + taps[3 - back : 4 - back, lanes] * moved
            pre_o[:, lanes] = pre.astype(BF)
            conv_o[:, lanes] = (pre * sigmoid(pre)).astype(BF)

    @pl.when(plain)
    def _():
        convolve(None)

    @pl.when(jnp.logical_not(plain))
    def _():
        convolve(docs.tap_masks(first, tile))

    parts = Tile(docs, first, deltas, rate, wedge[...])
    count = len(parts.parts)
    wide = spread_heads(
        [parts.leaving(c) for c in range(count)] + [wide_row(parts.overall(c)) for c in range(count)], spread[...]
    )
    for c, rows in enumerate(parts.parts):
        held_o[c] = state[...]
        sums_o[c] = total[...]
        total[...] = total[...] + parts.total[c]
        writes = conv_o[rows, channels : channels + 128]
        scaled = conv_o[rows, :channels].astype(F32) * wide[c]
        state[...] = state[...] * wide[count + c][0:1] + dot_tn(twice(writes, 0), stacked(scaled, 0))

    @pl.when(step == pl.num_programs(0) - 1)
    def _():
        end = docs.anchor + (step + 1) * tile - 1
        through = jnp.where(docs.counts(end) == docs.counts(docs.anchor - 1), 0.0, NEVER)
        leaving_o[...] = packed(state[...], spread_heads([jnp.exp(total[...] + through)], spread[...])[0][0:1])


def inside_kernel(
    tile, channels,
    meta, conv, deltas, table, wedge, *rest, m, sources,
):
    mixed_o, near_o, send_o = rest[-3:]
    step = pl.program_id(0)

    @pl.when(step == 0)
    def _():
        state, decay = joined([part[...] for part in rest[:sources]])
        near_o[:STATES, :] = state
        near_o[STATES:, :] = jnp.broadcast_to(decay, (8, channels))
        send_o[...] = packed(state, decay)

    docs = Docs(meta, m)
    first = docs.anchor + step * tile
    lanes_q = iota((Q, 128), 1)
    causal = iota((Q, Q), 0) >= iota((Q, Q), 1)
    low = lanes_q < 64
    skip = table[SKIP : SKIP + 1, :channels]
    rate = table[RATE : RATE + 1, :128]
    parts = Tile(docs, first, deltas[...], rate, wedge[...])
    for c, rows in enumerate(parts.parts):
        u = conv[rows, :channels]
        writes = conv[rows, channels : channels + 128]
        reads = conv[rows, channels + 128 :]
        scores = dot_nt(reads, writes)
        run = parts.run[c]
        bias = jnp.where(parts.same(c) & causal, 0.0, NEVER)
        behind = jnp.transpose(jnp.log(jnp.maximum(parts.deltas[c], TINY)) - run)
        pieces = []
        for pair in range(channels // 128):
            both = []
            for head in (2 * pair, 2 * pair + 1):
                decay = jnp.exp(run[:, head : head + 1] + behind[head : head + 1] + bias)
                both.append((decay * scores).astype(BF))
            pieces.append(dot(jnp.concatenate(both, axis=1), pair_blocks(u, pair, low)))
        mixed_o[rows, :] = jnp.concatenate(pieces, axis=1) + skip * u.astype(F32)


def mix_kernel(
    tile, channels,
    meta, inside, conv, deltas, gate, held, sums, cotangent, out_weight, table, spread, wedge, *rest, m, sources,
):
    mixed_o, stats_o, carry = rest[-3:]
    step = pl.program_id(0)

    @pl.when(step == 0)
    def _():
        carry[...] = joined([part[...] for part in rest[:sources]])[0]

    back = dot_nt(cotangent[...], out_weight[...]) * table[GATE : GATE + 1, :channels]
    docs = Docs(meta, m)
    first = docs.anchor + step * tile
    lanes_q = iota((Q, 128), 1)
    rate = table[RATE : RATE + 1, :128]
    parts = Tile(docs, first, deltas[...], rate, wedge[...])
    count = len(parts.parts)
    start = docs.counts(docs.anchor - 1)
    arrived = [jnp.exp(sums[c] + jnp.where(parts.before[c] == start, 0.0, NEVER)) for c in range(count)]
    wide = spread_heads([parts.entry(c) for c in range(count)] + arrived, spread[...])
    for c, rows in enumerate(parts.parts):
        reads = conv[rows, channels + 128 :]
        state = stacked(held[c] + wide[count + c][0:1] * carry[...], 0)
        mixed = inside[rows, :] + dot(twice(reads, 1), state) * wide[c]
        mixed_o[rows, :] = mixed
        gate_rows = gate[rows, :]
        gated = mixed * gate_rows * sigmoid(gate_rows)
        squares = jnp.sum(gated * gated, axis=1, keepdims=True)
        inner = jnp.sum(gated * back[rows], axis=1, keepdims=True)
        columns = jnp.where(lanes_q == 0, squares, jnp.where(lanes_q == 1, inner, 0.0))
        stats_o[:, rows] = jnp.transpose(columns)[0:8]


def third_kernel(
    tile, channels, full, chained, final,
    side, meta, mixed, gate, conv, deltas, normed, cotangent, out_weight, table, spread, wedge,
    stats_a, stats_b, stats_c, stats_d, *rest, m,
):
    if chained:
        grad_out_i, grad_gate_i, rows_i, *rest = rest
    grad_out, grad_gate, state, total = rest[-4:]
    *grads_o, rows_o = rest[: -4][-2 if final else -3 :]
    mine_o, other_o, gate_back_o, ssd_back_o, held_o, sums_o, leaving_o = rest[: -4 - len(grads_o) - 1][-7:]
    step = pl.program_id(0)
    gate_gain = table[GATE : GATE + 1, :channels]
    rate = table[RATE : RATE + 1, :128]
    docs = Docs(meta, m)
    place = pl.num_programs(0) - 1 - step
    first = docs.anchor + place * tile

    @pl.when(step == 0)
    def _():
        state[...] = jnp.zeros_like(state)
        total[...] = jnp.zeros_like(total)
        if chained:
            grad_out[...] = grad_out_i[...]
            grad_gate[...] = grad_gate_i[...]
            rows_o[...] = rows_i[...]
        else:
            grad_out[...] = jnp.zeros_like(grad_out)
            grad_gate[...] = jnp.zeros_like(grad_gate)
            rows_o[...] = jnp.zeros_like(rows_o)

    stats = stats_a[...] + stats_b[...] + stats_c[...] + stats_d[...]
    branches = []
    back = dot_nt(cotangent[...], out_weight[...])
    parts = Tile(docs, first, deltas[...], rate, wedge[...])
    count = len(parts.parts)
    wide = spread_heads(
        [parts.entry(c) for c in range(count)] + [wide_row(parts.overall(c)) for c in range(count)], spread[...]
    )
    for c in reversed(range(count)):
        rows = parts.parts[c]
        sides = jnp.transpose(jnp.concatenate([stats[:, rows], jnp.zeros((120, Q), F32)], axis=0))
        scale = lax.rsqrt(sides[:, 0:1] / full + EPS)
        inner = sides[:, 1:2]
        mixed_rows = mixed[rows, :]
        gate_rows = gate[rows, :]
        sigma = sigmoid(gate_rows)
        act = gate_rows * sigma
        gated = mixed_rows * act
        unit = gated * scale
        branch = (unit * gate_gain).astype(BF)
        branches.append(branch)
        back_rows = back[rows]
        grad_gated = scale * (back_rows * gate_gain) - unit * (scale * scale * (inner / full))
        grad_mixed = grad_gated * act
        gate_back_o[rows, :] = (grad_gated * mixed_rows * (sigma * (1.0 + gate_rows * (1.0 - sigma)))).astype(BF)
        ssd_back = grad_mixed.astype(BF)
        ssd_back_o[rows, :] = ssd_back
        u = conv[rows, :channels].astype(F32)
        rows_o[0:8, :] += jnp.sum((back_rows * unit).reshape(Q // 8, 8, channels), axis=0)
        rows_o[8:16, :] += jnp.sum((grad_mixed * u).reshape(Q // 8, 8, channels), axis=0)
        held_o[c] = state[...]
        sums_o[c] = total[...]
        total[...] = total[...] + parts.total[c]
        reads = conv[rows, channels + 128 :]
        entered = stacked(ssd_back.astype(F32) * wide[c], 0)
        state[...] = state[...] * wide[count + c][0:1] + dot_tn(twice(reads, 0), entered)
    branch = jnp.concatenate(branches[::-1], axis=0)
    part = dot(branch, out_weight[...]).astype(BF)
    here = place // (pl.num_programs(0) // 2) == side[0]

    @pl.when(here)
    def _():
        mine_o[...] = part

    @pl.when(jnp.logical_not(here))
    def _():
        other_o[...] = part

    grad_out[...] += dot_tn(branch, cotangent[...])
    grad_gate[...] += dot_tn(normed[...], gate_back_o[...])

    @pl.when(step == pl.num_programs(0) - 1)
    def _():
        if final:
            depth = grad_gate.shape[0]
            grads_o[0][:depth, :] = grad_gate[...].astype(BF)
            for block in range(grad_out.shape[1] // channels):
                lanes = slice(channels * block, channels * block + channels)
                grads_o[0][depth + channels * block : depth + channels * (block + 1), :] = grad_out[:, lanes].astype(BF)
        else:
            grads_o[0][...] = grad_out[...]
            grads_o[1][...] = grad_gate[...]
        end = docs.anchor + pl.num_programs(0) * tile - 1
        through = jnp.where(docs.counts(end) == docs.counts(docs.anchor - 1), 0.0, NEVER)
        leaving_o[...] = packed(state[...], spread_heads([jnp.exp(total[...] + through)], spread[...])[0][0:1])


def within_kernel(
    tile, channels,
    meta, conv, deltas, ssd_back, table, wedge, *rest, m, sources,
):
    grads_o, ends_o, near_o, send_o = rest[-4:]
    step = pl.program_id(0)

    @pl.when(step == 0)
    def _():
        state, decay = joined([part[...] for part in rest[:sources]])
        near_o[:STATES, :] = state
        near_o[STATES:, :] = jnp.broadcast_to(decay, (8, channels))
        send_o[...] = packed(state, decay)

    docs = Docs(meta, m)
    first = docs.anchor + step * tile
    lanes_q = iota((Q, 128), 1)
    rows_16 = iota((16, 128), 0)
    causal = iota((Q, Q), 1) >= iota((Q, Q), 0)
    low = lanes_q < 64
    skip = table[SKIP : SKIP + 1, :channels]
    rate = table[RATE : RATE + 1, :128]
    parts = Tile(docs, first, deltas[...], rate, wedge[...])
    for c, rows in enumerate(parts.parts):
        u = conv[rows, :channels]
        writes = conv[rows, channels : channels + 128]
        reads = conv[rows, channels + 128 :]
        grad = ssd_back[rows, :]
        scores = dot_nt(writes, reads)
        bias = jnp.where(parts.same(c) & causal, 0.0, NEVER)
        ahead = jnp.transpose(parts.run[c])
        behind = jnp.log(jnp.maximum(parts.deltas[c], TINY)) - parts.run[c]
        grad_scores = jnp.zeros((Q, Q), F32)
        by_source = jnp.zeros((Q, 128), F32)
        by_target = jnp.zeros((16, 128), F32)
        pieces = []
        for pair in range(channels // 128):
            blocks = pair_blocks(grad, pair, low)
            meets = dot_nt(u[:, 128 * pair : 128 * pair + 128], blocks)
            both = []
            for side in range(2):
                head = 2 * pair + side
                decay = jnp.exp(behind[:, head : head + 1] + ahead[head : head + 1] + bias)
                both.append((decay * scores).astype(BF))
                weighed = decay * meets[:, Q * side : Q * side + Q]
                grad_scores = grad_scores + weighed
                pairs = weighed * scores
                by_source = jnp.where(lanes_q == head, jnp.sum(pairs, axis=1, keepdims=True), by_source)
                by_target = jnp.where(rows_16 == head + 8, jnp.sum(pairs, axis=0, keepdims=True), by_target)
            pieces.append(dot(jnp.concatenate(both, axis=1), blocks))
        ends_o[rows, :] = by_source + jnp.transpose(jnp.concatenate([by_target, jnp.zeros((112, Q), F32)], axis=0))
        high, low_part = halves(grad_scores)
        grads_o[rows, :channels] = jnp.concatenate(pieces, axis=1) + skip * grad.astype(F32)
        grads_o[rows, channels : channels + 128] = dot(jnp.concatenate([high, low_part], axis=1), twice(reads, 0))
        grads_o[rows, channels + 128 :] = dot_tn(jnp.concatenate([high, low_part], axis=0), twice(writes, 0))


def across_kernel(
    tile, channels, chained,
    meta, conv, pre, xbc, edge, deltas, ssd_back, inside, ends,
    held, sums, carry, held_b, sums_b,
    table, spread, gather, wedge, wedge_up, wedge_below, *rest, m, sources,
):
    far, rest = rest[:sources], rest[sources:]
    if chained:
        taps_i, heads_i, *rest = rest
    in_back_o, dt_back_o, rim_o, tail_o, taps_o, heads_o, ext, grads, carry_b = rest[-9:]
    step = pl.program_id(0)
    docs = Docs(meta, m)
    places = pl.num_programs(0)
    place = places - 1 - step
    first = docs.anchor + place * tile
    end = docs.anchor + places * tile - 1
    width = pre.shape[1]
    taps = table[TAPS : TAPS + 4, :width]
    rate = table[RATE : RATE + 1, :128]
    lanes_q = iota((Q, 128), 1)

    @pl.when(step == 0)
    def _():
        if chained:
            taps_o[...] = taps_i[...]
            heads_o[...] = heads_i[...]
        else:
            taps_o[...] = jnp.zeros_like(taps_o)
            heads_o[...] = jnp.zeros_like(heads_o)
        carry_b[...] = joined([part[...] for part in far])[0]
        ext[:, 0:16, :] = jnp.zeros_like(ext[:, 0:16, :])
        ext[:, 16 + tile :, :] = jnp.zeros_like(ext[:, 16 + tile :, :])

    @pl.when(step > 0)
    def _():
        ext[:, 16 + tile :, :] = ext[:, 16:24, :]

    parts = Tile(docs, first, deltas[...], rate, wedge[...])
    count = len(parts.parts)
    start, stop = docs.counts(docs.anchor - 1), docs.counts(end)
    each = range(count)
    arrived = [jnp.exp(sums[c] + jnp.where(parts.before[c] == start, 0.0, NEVER)) for c in each]
    arrived_b = [jnp.exp(sums_b[c] + jnp.where(parts.last[c] == stop, 0.0, NEVER)) for c in each]
    wide = spread_heads(
        [parts.entry(c) for c in each] + [parts.leaving(c) for c in each] + arrived + arrived_b, spread[...]
    )
    crossings, products = [], []
    for c, rows in enumerate(parts.parts):
        u = conv[rows, :channels].astype(F32)
        writes = conv[rows, channels : channels + 128]
        reads = conv[rows, channels + 128 :]
        outward = wide[count + c]
        state = held[c] + wide[2 * count + c][0:1] * carry[...]
        state_b = held_b[c] + wide[3 * count + c][0:1] * carry_b[...]
        grad_in = ssd_back[rows, :].astype(F32) * wide[c]
        crossing = dot(twice(writes, 1), stacked(state_b, 0)) * outward
        products.append(u * crossing)
        crossings.append(grad_in * dot(twice(reads, 1), stacked(state, 0)))
        products.append(jnp.sum((state * state_b).reshape(16, 8, channels), axis=0))
        grads[rows, :channels] = inside[rows, :channels] + crossing
        grads[rows, channels : channels + 128] = inside[rows, channels : channels + 128] + near_f32(u * outward, state_b)
        grads[rows, channels + 128 :] = inside[rows, channels + 128 :] + near_f32(grad_in, state)
    gathered = gather_heads(crossings + products, gather[...])
    in_parts, out_parts = gathered[:count], gathered[count : count + 2 * count : 2]
    ups, sources = [], []
    for c, rows in enumerate(parts.parts):
        both_ends = ends[rows, :]
        sources.append(jnp.where(lanes_q < 8, both_ends, 0.0))
        target = jnp.where(lanes_q < 8, pltpu.roll(both_ends, 120, 1), 0.0)
        ups.append(in_parts[c] + target - sources[c])
    ups = add_up(ups, wedge_up[...])
    belows = add_up(out_parts, wedge_below[...])
    for c, rows in enumerate(parts.parts):
        between = jnp.sum(gathered[count + 2 * c + 1], axis=0, keepdims=True) * parts.overall(c)
        grad_run = between + ups[c] + belows[c]
        part_deltas = parts.deltas[c]
        slope = 1.0 - jnp.exp(-part_deltas)
        ratio = jnp.where(part_deltas > 1e-6, slope / jnp.maximum(part_deltas, 1e-6), 1.0)
        dt_back = (sources[c] + out_parts[c]) * ratio + rate * grad_run * slope
        dt_back_o[rows, :] = dt_back.astype(BF)
        heads_o[0:8, :] += jnp.sum(dt_back.reshape(Q // 8, 8, 128), axis=0)
        heads_o[8:16, :] += jnp.sum((grad_run * part_deltas).reshape(Q // 8, 8, 128), axis=0)

    plain = docs.none_near(first, tile)

    def convolve_back(masks):
        for slab in range(width // 128):
            lanes = slice(128 * slab, 128 * slab + 128)
            pre_rows = pre[:, lanes].astype(F32)
            sigma = sigmoid(pre_rows)
            grad_pre = grads[:, lanes] * (sigma * (1.0 + pre_rows * (1.0 - sigma)))
            source = xbc[:, lanes].astype(F32)
            result = taps[3:4, lanes] * grad_pre
            taps_o[24:32, lanes] += jnp.sum((grad_pre * source).reshape(tile // 8, 8, 128), axis=0)
            taps_o[32:40, lanes] += jnp.sum(grad_pre.reshape(tile // 8, 8, 128), axis=0)
            if masks is None:
                longer = jnp.concatenate([grad_pre, ext[0, 16 + tile :, lanes]], axis=0)
            for back in range(1, 4):
                if masks is None:
                    ext[back - 1, 16:24, lanes] = grad_pre[0:8]
                    moved = pltpu.roll(longer, tile + 8 - back, 0)[:tile]
                else:
                    ext[back - 1, 16 : 16 + tile, lanes] = grad_pre * masks[back - 1]
                    moved = ext[back - 1, 16 + back : 16 + back + tile, lanes]
                result = result + taps[3 - back : 4 - back, lanes] * moved
                taps_o[8 * (3 - back) : 8 * (4 - back), lanes] += jnp.sum(
                    (moved * source).reshape(tile // 8, 8, 128), axis=0
                )
            high = result.astype(BF)
            in_back_o[:, lanes] = high
            if 128 * slab >= channels:
                in_back_o[:, slice(256 + 128 * slab, 384 + 128 * slab)] = (result - high.astype(F32)).astype(BF)

            @pl.when(step == 0)
            def _():
                tail_o[:, lanes] = result[tile - RIM :]

    @pl.when(plain)
    def _():
        convolve_back(None)

    @pl.when(jnp.logical_not(plain))
    def _():
        convolve_back(docs.tap_masks(first, tile))

    @pl.when(place == 0)
    def _():
        total = jnp.zeros((RIM, width), F32)
        source = edge[...].astype(F32)
        for back in range(1, 4):
            moved = ext[back - 1, back : back + RIM, :]
            total = total + taps[3 - back : 4 - back, :] * moved
            taps_o[8 * (3 - back) : 8 * (4 - back), :] += jnp.sum((moved * source).reshape(RIM // 8, 8, width), axis=0)
        rim_o[...] = total


def part_kernel(
    tile, channels, chained, last, tiles,
    tokens, gate_back, in_back, dt_back, weights, *rest,
):
    if last:
        tail, rim, *rest = rest
    if chained:
        rows_i, *rest = rest
    part_o, rows_o, every = rest[-3:]
    step = pl.program_id(0)
    wide = in_back.shape[1]
    width = wide - 256

    @pl.when(step == 0)
    def _():
        rows_o[...] = rows_i[...] if chained else jnp.zeros_like(rows_o)

    every[:, :channels] = gate_back[...]
    every[:, channels : channels + wide] = in_back[...]
    every[:, channels + wide :] = dt_back[...]
    if last:

        @pl.when(step == tiles - 1)
        def _():
            high, low = halves(tail[...] + rim[...])
            every[tile - RIM :, channels : channels + width] = high
            every[tile - RIM :, channels + width : channels + wide] = low[:, channels:]

    x = tokens[...].astype(F32)
    scale = lax.rsqrt(jnp.mean(x * x, axis=1, keepdims=True) + EPS)
    part = dot_nt(every[...], weights[...])
    part_o[...] = part.astype(BF)
    rows_o[...] += jnp.sum((part * (x * scale)).reshape(tile // 8, 8, x.shape[1]), axis=0)


def weight_kernel(
    tile, channels, chained, tiles,
    normed, in_back, dt_back, tail, rim, *rest,
):
    if chained:
        grads_i, dt_i, *rest = rest
    grads_o, dt_o, every, total, dt_total = rest[-5:]
    step = pl.program_id(0)
    wide = in_back.shape[1]
    width = wide - 256

    @pl.when(step == 0)
    def _():
        total[...] = grads_i[...] if chained else jnp.zeros_like(total)
        dt_total[...] = jnp.zeros_like(dt_total)

    every[...] = in_back[...]

    @pl.when(step == tiles - 1)
    def _():
        high, low = halves(tail[...] + rim[...])
        every[tile - RIM :, :width] = high
        every[tile - RIM :, width:] = low[:, channels:]

    turned = jnp.transpose(normed[...])
    total[:, :channels] += dot(turned, every[:, :channels])
    total[:, channels:] += dot(
        twice(turned, 1), jnp.concatenate([every[:, channels:width], every[:, width:]], axis=0)
    )
    dt_total[...] += dot_nt(jnp.transpose(dt_back[...]), turned)

    @pl.when(step == tiles - 1)
    def _():
        grads_o[...] = total[...].astype(grads_o.dtype)
        dt_o[...] = dt_total[0:8] + dt_i[...] if chained else dt_total[0:8]


def place_kernel(
    token,
    side, mine, other, tokens, *rest,
):
    if token:
        cotangent, table, *rest = rest
    out = rest[-1]
    step = pl.program_id(0)

    def finish(total):
        x = tokens[...].astype(F32)
        total = total.astype(F32)
        if not token:
            return (x + total).astype(BF)
        scale = lax.rsqrt(jnp.mean(x * x, axis=1, keepdims=True) + EPS)
        grad_hat = total * table[GAIN : GAIN + 1, :]
        inner = jnp.mean(grad_hat * x, axis=1, keepdims=True)
        return (cotangent[...].astype(F32) + scale * grad_hat - x * (scale * scale * scale * inner)).astype(BF)

    here = step // (pl.num_programs(0) // 2) == side[0]

    @pl.when(here)
    def _():
        out[...] = finish(mine[...])

    @pl.when(jnp.logical_not(here))
    def _():
        out[...] = finish(other[...])


class Call:
    def __init__(self, kernel, steps, name):
        self.kernel, self.steps, self.name = kernel, steps, name
        self.args, self.in_specs, self.outs, self.out_specs, self.scratch = [], [], [], [], []
        self.aliases = {}

    def whole(self, *arrays):
        for array in arrays:
            self.args.append(array)
            self.in_specs.append(pl.BlockSpec(array.shape, lambda i, *s, rank=array.ndim: (0,) * rank))
        return self

    def scalars(self, array):
        self.args.append(array)
        self.in_specs.append(pl.BlockSpec(memory_space=pltpu.SMEM))
        return self

    def blocks(self, *arrays_specs):
        for array, spec in arrays_specs:
            self.args.append(array)
            self.in_specs.append(spec)
        return self

    def out(self, shape, dtype, spec=None):
        self.outs.append(jax.ShapeDtypeStruct(shape, dtype))
        self.out_specs.append(spec or pl.BlockSpec(shape, lambda i, *s, rank=len(shape): (0,) * rank))
        return self

    def after(self, *arrays):
        for array in arrays:
            self.args.append(array)
            self.in_specs.append(pl.BlockSpec(memory_space=pl.ANY))
        return self

    def alias(self, array):
        self.aliases = {len(self.args): 0}
        return self.after(array)

    def temp(self, shape, dtype):
        self.scratch.append(pltpu.VMEM(shape, dtype))
        return self

    def run(self, micros, scalars=None):
        ahead = () if scalars is None else (scalars,)
        return pl.pallas_call(
            self.kernel,
            grid_spec=pltpu.PrefetchScalarGridSpec(
                num_scalar_prefetch=len(ahead),
                grid=(self.steps,),
                in_specs=self.in_specs,
                out_specs=tuple(self.out_specs),
                scratch_shapes=self.scratch,
            ),
            out_shape=tuple(self.outs),
            input_output_aliases={at + len(ahead): to for at, to in self.aliases.items()},
            compiler_params=pltpu.CompilerParams(
                dimension_semantics=("arbitrary",), vmem_limit_bytes=VMEM_BYTES
            ),
            cost_estimate=pl.CostEstimate(flops=int(micros * SCALE * 1.15e9), bytes_accessed=0, transcendentals=0),
            name=self.name,
        )(*ahead, *self.args)


def swap(value, axis, bits):
    count = lax.axis_size(axis)
    return lax.ppermute(value, axis, [(i, i ^ bits) for i in range(count)])


def from_behind(value, axis, steps):
    count = lax.axis_size(axis)
    sources = range(max(0, -steps), min(count, count - steps))
    return lax.ppermute(value, axis, [(i, i + steps) for i in sources])


def packed(state, decay):
    high, low = halves(jnp.broadcast_to(decay, (8, decay.shape[1])))
    return jnp.concatenate([state.astype(BF), high, low], axis=0)


def unpacked(part):
    if part.dtype == F32:
        return part[:STATES], part[STATES : STATES + 1]
    part = part.astype(F32)
    return part[:STATES], part[STATES : STATES + 1] + part[STATES + 8 : STATES + 9]


def joined(parts):
    state, decay = unpacked(parts[0])
    for part in parts[1:]:
        more, keep = unpacked(part)
        state = state + decay * more
        decay = decay * keep
    return state, decay


def near_parts(leaving, axis, sign):
    return [from_behind(leaving, axis, sign * k) for k in range(1, min(4, lax.axis_size(axis)))]


def far_parts(carry, sent, axis, sign):
    count = lax.axis_size(axis)
    window = 3
    parts = [carry]
    while window < count - 1:
        if len(parts) > 1:
            state, decay = joined(parts)
            sent = packed(state, decay)
            carry = jnp.concatenate([state, jnp.broadcast_to(decay, (8, decay.shape[1]))], axis=0)
        parts = [carry] + [from_behind(sent, axis, sign * k) for k in (window, 2 * window) if k < count]
        window *= 3
    return parts


def sum_rows(parts):
    total = parts[0].astype(F32)
    for part in parts[1:]:
        total = total + part.astype(F32)
    return total


def pair_sum(mine, other):
    return (mine.astype(F32) + swap(other, "head", 1).astype(F32)).astype(BF)


def head_pair(part):
    rows = part.shape[0] // 2
    side = lax.axis_index("head") % 2
    mine = lax.dynamic_slice_in_dim(part, side * rows, rows, 0)
    return pair_sum(mine, lax.dynamic_slice_in_dim(part, (1 - side) * rows, rows, 0))


def head_rest(low):
    bit = 2
    while bit < lax.axis_size("head"):
        low = (low.astype(F32) + swap(low, "head", bit).astype(F32)).astype(BF)
        bit *= 2
    return low


class Reduction:
    def __init__(self, value, axis):
        self.value, self.axis, self.bits, self.out = value, axis, 1, True
        self.count, self.me = lax.axis_size(axis), lax.axis_index(axis)
        self.start()

    def start(self):
        if self.out:
            rows, half = self.value.shape[0] // 2, self.me // self.bits % 2
            sent = lax.dynamic_slice_in_dim(self.value, (1 - half) * rows, rows, 0)
            self.value = lax.dynamic_slice_in_dim(self.value, half * rows, rows, 0)
        else:
            sent = self.value
        self.other = swap(sent, self.axis, self.bits)

    def done(self):
        return not self.out and self.bits == 0

    def step(self, after):
        other, _ = lax.optimization_barrier((self.other, after))
        if self.out:
            self.value = (self.value.astype(F32) + other.astype(F32)).astype(BF)
            self.out = self.bits * 2 < self.count
            self.bits = self.bits * 2 if self.out else self.bits
        else:
            first = self.me // self.bits % 2 == 0
            pieces = [jnp.where(first, self.value, other), jnp.where(first, other, self.value)]
            self.value = jnp.concatenate(pieces, axis=0)
            self.bits //= 2
        if not self.done():
            self.start()


def pair_parts(value, axis):
    rows = value.shape[0] // 2
    half = lax.axis_index(axis) % 2
    mine = lax.dynamic_slice_in_dim(value, half * rows, rows, 0)
    return mine, swap(lax.dynamic_slice_in_dim(value, (1 - half) * rows, rows, 0), axis, 1)


def scatter_parts(value, axis):
    count = lax.axis_size(axis) // 2
    me = lax.axis_index(axis) // 2
    rows = value.shape[0] // count
    parts = [lax.dynamic_slice_in_dim(value, me * rows, rows, 0)]
    for bits in range(1, count):
        piece = lax.dynamic_slice_in_dim(value, jnp.bitwise_xor(me, bits) * rows, rows, 0)
        parts.append(swap(piece, axis, 2 * bits))
    return parts


def gather_half(value, axis):
    count = lax.axis_size(axis) // 2
    me = lax.axis_index(axis) // 2
    rows = value.shape[0]
    result = jnp.zeros((count * rows, value.shape[1]), value.dtype)
    result = lax.dynamic_update_slice_in_dim(result, value, me * rows, 0)
    for bits in range(1, count):
        result = lax.dynamic_update_slice_in_dim(
            result, swap(value, axis, 2 * bits), jnp.bitwise_xor(me, bits) * rows, 0
        )
    return result


def gather_pair(half, axis):
    other = swap(half, axis, 1)
    first = lax.axis_index(axis) % 2 == 0
    return jnp.concatenate([jnp.where(first, half, other), jnp.where(first, other, half)], axis=0)


def add_swaps(value, axis):
    return sum_rows([value] + [swap(value, axis, bits) for bits in range(1, lax.axis_size(axis))])


def all_sum(value, axis):
    bit = 1
    while bit < lax.axis_size(axis):
        value = value + swap(value, axis, bit)
        bit *= 2
    return value


def local(
    tokens,
    doc_starts,
    norm_gain,
    gate_x_weight,
    bc_weight,
    dt_weight,
    conv_x_weight,
    conv_x_bias,
    conv_bc_weight,
    conv_bc_bias,
    dt_bias,
    a_log,
    d_skip,
    gate_gain,
    out_weight,
    cotangent,
):
    micro, length, model = tokens.shape
    channels = gate_x_weight.shape[2]
    heads = dt_weight.shape[1]
    dim = channels // heads
    states = bc_weight.shape[1] // 2
    width = channels + 2 * states
    full = channels * lax.axis_size("head")
    tile, small = min(TILE, length), min(SMALL, length)
    steps = length // tile
    per = tile // Q
    blocks = length // Q

    rim_tokens = from_behind(tokens[:, length - RIM :], "seq", 1)
    weights = jnp.concatenate(
        [gate_x_weight[:, 0], gate_x_weight[:, 1], bc_weight, bc_weight,
         jnp.pad(dt_weight, ((0, 0), (0, 128 - heads)))], axis=1
    )
    decay_rate = -jnp.exp(a_log)

    def table_rows(*parts):
        row = jnp.concatenate(parts, axis=-1)
        row = row if row.ndim == 2 else row[None]
        return jnp.pad(row, ((0, 0), (0, model - row.shape[1])))

    table = jnp.concatenate(
        [
            table_rows(norm_gain),
            table_rows(conv_x_weight, conv_bc_weight),
            table_rows(conv_x_bias, conv_bc_bias),
            table_rows(gate_gain),
            table_rows(jnp.repeat(d_skip, dim)),
            table_rows(decay_rate),
            table_rows(dt_bias, jnp.full((128 - heads,), -200.0, F32)),
            jnp.zeros((TABLE - BIAS - 1, model), F32),
        ],
        axis=0,
    )
    owner = np.arange(channels)[None, :] // dim == np.arange(128)[:, None]
    spread = np.concatenate([owner, owner], axis=0).astype(BF)
    gather = np.concatenate([owner.T, owner.T], axis=0).astype(BF)
    order = np.arange(Q)
    until_here = order[:, None] >= order[None, :]
    below = order[:, None] > order[None, :]
    wedge = np.concatenate([until_here] * 2, axis=1).astype(BF)
    wedge_up = np.concatenate([until_here.T] * 2, axis=1).astype(BF)
    wedge_below = np.concatenate([below] * 2, axis=1).astype(BF)
    anchor = lax.axis_index("seq") * length
    meta = jnp.concatenate(
        [jnp.where(doc_starts >= 1, doc_starts, 2**30), jnp.full((micro, 1), anchor)], axis=1
    ).astype(jnp.int32)

    side = (lax.axis_index("head") % 2).astype(jnp.int32)[None]
    ahead = lambda i: i
    astern = lambda i: steps - 1 - i

    def rows_of(cols, turn, rows=tile):
        return pl.BlockSpec((rows, cols), lambda i, *s: (turn(i), 0))

    def rows_in(m, cols, turn):
        return pl.BlockSpec((None, tile, cols), lambda i, *s: (m, turn(i), 0))

    def chunks_of(turn, rows, cols):
        return pl.BlockSpec((per, rows, cols), lambda i, *s: (turn(i), 0, 0))

    def stat_spec(turn):
        return pl.BlockSpec((8, tile), lambda i, *s: (0, turn(i)))

    def project(m, *waits):
        call = Call(partial(first_kernel, tile, channels, m=m), steps, f"project_{m}")
        call.scalars(meta)
        call.blocks((rim_tokens, pl.BlockSpec((None, RIM, model), lambda i, *s: (m, 0, 0))))
        call.blocks((tokens, rows_in(m, model, ahead)))
        call.whole(weights, table, spread, wedge).after(*waits)
        call.out((length, model), BF, rows_of(model, ahead))
        call.out((length, channels), F32, rows_of(channels, ahead))
        call.out((length, width), BF, rows_of(width, ahead))
        call.out((length, width), BF, rows_of(width, ahead))
        call.out((length, width), BF, rows_of(width, ahead))
        call.out((length, 128), F32, rows_of(128, ahead))
        call.out((blocks, 128, channels), F32, chunks_of(ahead, 128, channels))
        call.out((blocks, 8, 128), F32, chunks_of(ahead, 8, 128))
        call.out((STATES + 16, channels), BF)
        call.out((RIM, width), BF)
        call.temp((tile + 8, width), F32).temp((128, channels), F32).temp((8, 128), F32)
        return call.run(22)

    def inside(m, kept, parts, *waits):
        conv, deltas = kept[4:6]
        call = Call(partial(inside_kernel, tile, channels, m=m, sources=len(parts)), steps, f"inside_{m}")
        call.scalars(meta)
        call.blocks((conv, rows_of(width, ahead)), (deltas, rows_of(128, ahead)))
        call.whole(table, wedge, *parts).after(*waits)
        call.out((length, channels), F32, rows_of(channels, ahead))
        call.out((STATES + 8, channels), F32).out((STATES + 16, channels), BF)
        return call.run(11)

    def mix(m, kept, inner, parts, *waits):
        normed, gate, xbc, pre, conv, deltas, held, sums = kept[:8]
        call = Call(partial(mix_kernel, tile, channels, m=m, sources=len(parts)), steps, f"mix_{m}")
        call.scalars(meta)
        call.blocks(
            (inner, rows_of(channels, ahead)),
            (conv, rows_of(width, ahead)),
            (deltas, rows_of(128, ahead)),
            (gate, rows_of(channels, ahead)),
            (held, chunks_of(ahead, 128, channels)),
            (sums, chunks_of(ahead, 8, 128)),
            (cotangent, rows_in(m, model, ahead)),
        )
        call.whole(out_weight, table, spread, wedge, *parts).after(*waits)
        call.out((length, channels), F32, rows_of(channels, ahead))
        call.out((8, length), F32, stat_spec(ahead))
        call.out((STATES, channels), F32)
        return call.run(12)

    def norm(m, kept, mixed, stats, chain, *waits):
        normed, gate, xbc, pre, conv, deltas = kept[:6]
        final = m + 1 == micro
        call = Call(partial(third_kernel, tile, channels, float(full), bool(chain), final, m=m), steps, f"gate_{m}")
        call.scalars(meta)
        call.blocks(
            (mixed, rows_of(channels, astern)),
            (gate, rows_of(channels, astern)),
            (conv, rows_of(width, astern)),
            (deltas, rows_of(128, astern)),
            (normed, rows_of(model, astern)),
            (cotangent, rows_in(m, model, astern)),
        )
        call.whole(out_weight, table, spread, wedge)
        call.blocks(*[(part, stat_spec(astern)) for part in stats])
        call.whole(*chain).after(*waits)
        half = steps // 2

        def spot(flip):
            return pl.BlockSpec(
                (tile, model),
                lambda i, s: (jnp.clip(astern(i) - (s[0] if flip == 0 else 1 - s[0]) * half, 0, half - 1), 0),
            )

        call.out((length // 2, model), BF, spot(0)).out((length // 2, model), BF, spot(1))
        call.out((length, channels), BF, rows_of(channels, astern))
        call.out((length, channels), BF, rows_of(channels, astern))
        call.out((blocks, 128, channels), F32, chunks_of(astern, 128, channels))
        call.out((blocks, 8, 128), F32, chunks_of(astern, 8, 128))
        call.out((STATES + 16, channels), BF)
        if final:
            call.out((2 * model, channels), BF)
        else:
            call.out((channels, model), F32)
            call.out((model, channels), F32)
        call.out((16, channels), F32)
        call.temp((channels, model), F32).temp((model, channels), F32)
        call.temp((128, channels), F32).temp((8, 128), F32)
        return call.run(17, side)

    def within(m, kept, ssd_back, parts, *waits):
        conv, deltas = kept[4:6]
        call = Call(partial(within_kernel, small, channels, m=m, sources=len(parts)), length // small, f"within_{m}")
        call.scalars(meta)
        call.blocks((conv, rows_of(width, ahead, small)), (deltas, rows_of(128, ahead, small)), (ssd_back, rows_of(channels, ahead, small)))
        call.whole(table, wedge, *parts).after(*waits)
        call.out((length, width), F32, rows_of(width, ahead, small))
        call.out((length, 128), F32, rows_of(128, ahead, small))
        call.out((STATES + 8, channels), F32).out((STATES + 16, channels), BF)
        return call.run(3)

    def across(m, kept, carry, third, inner, parts, chain, *waits):
        normed, gate, xbc, pre, conv, deltas, held, sums, leaving, edge = kept
        call = Call(partial(across_kernel, tile, channels, bool(chain), m=m, sources=len(parts)), steps, f"across_{m}")
        call.scalars(meta)
        call.blocks((conv, rows_of(width, astern)), (pre, rows_of(width, astern)), (xbc, rows_of(width, astern)))
        call.whole(edge)
        call.blocks(
            (deltas, rows_of(128, astern)),
            (third[3], rows_of(channels, astern)),
            (inner[0], rows_of(width, astern)),
            (inner[1], rows_of(128, astern)),
            (held, chunks_of(astern, 128, channels)),
            (sums, chunks_of(astern, 8, 128)),
        )
        call.whole(carry)
        call.blocks((third[4], chunks_of(astern, 128, channels)), (third[5], chunks_of(astern, 8, 128)))
        call.whole(table, spread, gather, wedge, wedge_up, wedge_below, *parts, *chain).after(*waits)
        call.out((length, width + 256), BF, rows_of(width + 256, astern))
        call.out((length, 128), BF, rows_of(128, astern))
        call.out((RIM, width), F32)
        call.out((RIM, width), F32)
        call.out((40, width), F32)
        call.out((16, 128), F32)
        call.temp((3, tile + 24, width), F32).temp((tile, width), F32).temp((STATES, channels), F32)
        return call.run(10)

    def part_of(m, gate_back, fourth, span, rows, rim, chain, earlier, micros, *waits):
        count = span[1] - span[0]
        turn = lambda i: i + span[0]
        put = lambda i: i + span[0] - rows[0]
        call = Call(partial(part_kernel, tile, channels, bool(chain), rim is not None, count), count, f"input_{m}_{span[0]}")
        call.blocks(
            (tokens, rows_in(m, model, turn)),
            (gate_back, rows_of(channels, turn)),
            (fourth[0], rows_of(width + 256, turn)),
            (fourth[1], rows_of(128, turn)),
        )
        call.whole(weights)
        if rim is not None:
            call.whole(fourth[3], rim)
        call.whole(*chain)
        if earlier is not None:
            call.alias(earlier)
        call.after(*waits)
        call.out((rows[1] * tile, model), BF, rows_of(model, put))
        call.out((8, model), F32)
        call.temp((tile, channels + width + 256 + 128), BF)
        return call.run(micros)

    def weight_back(m, kept, fourth, rim, chain, kind, *waits):
        call = Call(partial(weight_kernel, tile, channels, bool(chain), steps), steps, f"weigh_{m}")
        call.blocks(
            (kept[0], rows_of(model, ahead)), (fourth[0], rows_of(width + 256, ahead)), (fourth[1], rows_of(128, ahead))
        )
        call.whole(fourth[3], rim, *chain).after(*waits)
        call.out((model, width), kind)
        call.out((8, model), F32)
        call.temp((tile, width + 256), BF).temp((model, width), F32).temp((128, model), F32)
        return call.run(8)

    def place(m, begin, low, other, token, earlier, *waits):
        big = min(512, low.shape[0])
        half = low.shape[0] // big
        call = Call(partial(place_kernel, token), 2 * half, f"place_{m}_{begin}_{token:d}")

        def source(flip):
            return pl.BlockSpec(
                (big, model), lambda i, s: (jnp.clip(i - (s[0] if flip == 0 else 1 - s[0]) * half, 0, half - 1), 0)
            )

        spot = pl.BlockSpec((None, big, model), lambda i, s: (m, i + begin // big, 0))
        call.blocks((low, source(0)), (other, source(1)), (tokens, spot))
        if token:
            call.blocks((cotangent, spot))
            call.args.append(table)
            call.in_specs.append(pl.BlockSpec(table.shape, lambda i, s: (0, 0)))
        if earlier is not None:
            call.alias(earlier)
        call.after(*waits)
        call.out((micro, length, model), BF, spot)
        return call.run(8, side)[0]

    every = range(micro)
    kept, inner, mixes, thirds, order_by, chain = [], [], [], [], [], ()
    for m in every:
        kept.append(project(m, *order_by))
        order_by = [kept[m][8]]
    for m in every:
        inner.append(inside(m, kept[m], near_parts(kept[m][8], "seq", 1), *order_by))
        order_by = [inner[m][1]]
    for m in every:
        mixes.append(mix(m, kept[m], inner[m][0], far_parts(inner[m][1], inner[m][2], "seq", 1), *order_by))
        order_by = [mixes[m][1]]
    for m in every:
        stats = [mixes[m][1]] + [swap(mixes[m][1], "head", bits) for bits in range(1, lax.axis_size("head"))]
        thirds.append(norm(m, kept[m], mixes[m][0], stats, chain, *order_by))
        chain = thirds[m][7:]
        order_by = [thirds[m][6]]
    packed_grads, gate_rows = chain
    reduction = Reduction(packed_grads, "seq")
    mixed_pair = [pair_sum(thirds[m][0], thirds[m][1]) for m in every]
    mixed_all = [head_rest(mixed_pair[m]) for m in every]
    inner_b, fourths, chain = [], [], ()
    for m in every:
        near = near_parts(thirds[m][6], "seq", -1)
        inner_b.append(within(m, kept[m], thirds[m][3], near, mixed_pair[m], *order_by))
        order_by = [inner_b[m][2]]
        reduction.step(inner_b[m][2])
    far = [far_parts(inner_b[m][2], inner_b[m][3], "seq", -1) for m in every]
    order_by.append(mixed_all[0])
    mixed_other = [swap(mixed_all[m], "head", 1) for m in every]
    token_other = []
    gain_rows, grads, token_all, half_steps = (), (), [], steps // 2
    for m in every:
        final = m + 1 == micro
        fourths.append(across(m, kept[m], mixes[m][2], thirds[m], inner_b[m], far[m], chain, *order_by))
        chain = fourths[m][4:6]
        if not reduction.done():
            reduction.step(fourths[m][4])
        rim = from_behind(fourths[m][2], "seq", -1)
        gate_back = thirds[m][2]
        if not final:
            both = (0, steps)
            first = part_of(m, gate_back, fourths[m], (0, half_steps), both, None, gain_rows, None, 6, mixed_all[m + 1], *far[m + 1])
            second = part_of(m, gate_back, fourths[m], (half_steps, steps), both, rim, first[1:], first[0], 6)
            grads = weight_back(m, kept[m], fourths[m], rim, grads, F32, second[1])
            reduction.step(second[1])
            reduction.step(grads[1])
            pair = head_pair(second[0])
            token_all.append(head_rest(pair))
            token_other.append(swap(token_all[m], "head", 1))
            gain_rows = second[1:]
            order_by = [pair, grads[1]]
        else:
            first = part_of(m, gate_back, fourths[m], (0, half_steps), (0, half_steps), None, gain_rows, None, 6, token_all[-1], *mixed_other)
            pair = head_pair(first[0])
            second = part_of(
                m, gate_back, fourths[m], (half_steps, steps), (half_steps, half_steps), rim, first[1:], None, 6
            )
            grads = weight_back(m, kept[m], fourths[m], rim, grads, BF, second[1], pair, *token_other)
            gain_rows = second[1:]
            last_pair = [pair, head_pair(second[0])]
    tap_rows, head_rows = chain
    grads, dt_rows = grads
    gain_rows = gain_rows[0]

    def folded(rows):
        return jnp.sum(rows.reshape(-1, 8, rows.shape[1]), axis=1)

    by_tap = folded(tap_rows)
    by_row = folded(gate_rows)
    by_head = folded(head_rows)[:, :heads]
    skip_sum = jnp.sum(by_row[1].reshape(heads, dim), axis=1)
    small = jnp.concatenate(
        [by_tap[:, channels:].reshape(-1), jnp.sum(gain_rows, axis=0), dt_rows[:heads].reshape(-1),
         by_tap[:, :channels].reshape(-1), by_row[0], by_head.reshape(-1), skip_sum]
    )
    small = jnp.pad(small, (0, -small.size % 1024)).reshape(-1, 128)
    shared_size = by_tap[:, channels:].size + model
    halved = pair_parts(grads, "seq")
    last_all = [head_rest(last_pair[0])]
    halved, last_pair = lax.optimization_barrier((halved, last_pair))
    last_all.append(head_rest(last_pair[1]))
    halved = sum_rows(halved).astype(BF)
    pieces = scatter_parts(halved, "seq")
    small = all_sum(lax.optimization_barrier((small, halved))[0], "seq")
    mixed_out = place(0, 0, mixed_all[0], mixed_other[0], False, None, halved, last_all[0])
    pieces, mixed_out = lax.optimization_barrier((pieces, mixed_out))
    part = sum_rows(pieces)
    while not reduction.done():
        reduction.step(part)
    packed_grads = reduction.value
    share = 2 * states // lax.axis_size("head")
    bc_parts = [part[:, channels:width]]
    bc_parts += [swap(bc_parts[0], "head", bits) for bits in range(1, lax.axis_size("head"))]
    for m in range(1, micro):
        mixed_out = place(m, 0, mixed_all[m], mixed_other[m], False, mixed_out, part, last_all[1])
    bc_parts, mixed_out = lax.optimization_barrier((bc_parts, mixed_out))
    bc_mine = lax.dynamic_slice_in_dim(sum_rows(bc_parts), lax.axis_index("head") * share, share, 1)
    payload = jnp.concatenate(
        [part[:, :channels], bc_mine, jnp.zeros((part.shape[0], -share % 128), F32)], axis=1
    ).astype(BF)
    gathered = gather_half(payload, "seq")
    token_grad = None
    for m in range(micro - 1):
        token_grad = place(m, 0, token_all[m], token_other[m], True, token_grad, payload)
    gathered, token_grad = lax.optimization_barrier((gathered, token_grad))
    gathered = gather_pair(gathered, "seq")
    grad_x = gathered[:, :channels].astype(F32)
    grad_bc = gathered[:, channels : channels + share].astype(F32)

    token_grad = place(micro - 1, 0, last_all[0], swap(last_all[0], "head", 1), True, token_grad)
    last_other = swap(last_all[1], "head", 1)
    token_grad = place(micro - 1, length // 2, last_all[1], last_other, True, token_grad)

    tap_count = conv_x_weight.shape[0]
    shared, _ = lax.optimization_barrier((small[: shared_size // 128], payload))
    shared = add_swaps(shared, "head").reshape(-1)
    rest = small[shared_size // 128 :].reshape(-1)
    bc_taps = shared[: (tap_count + 1) * 2 * states].reshape(tap_count + 1, 2 * states)
    grad_norm_gain = shared[(tap_count + 1) * 2 * states :]
    grad_dt = rest[: heads * model].reshape(heads, model).T
    rest = rest[heads * model :]
    cut = (tap_count + 1) * channels
    x_taps = rest[:cut].reshape(tap_count + 1, channels)
    grad_gate_gain = rest[cut : cut + channels]
    tails = rest[cut + channels : cut + channels + 3 * heads].reshape(3, heads)
    grad_gate = packed_grads[:model].astype(F32)
    grad_out = jnp.concatenate(
        [packed_grads[row : row + channels] for row in range(model, 2 * model, channels)], axis=1
    ).astype(F32)
    return (
        mixed_out,
        token_grad,
        grad_norm_gain,
        jnp.stack([grad_gate, grad_x], axis=1),
        grad_bc,
        grad_dt,
        x_taps[:tap_count],
        x_taps[tap_count],
        bc_taps[:tap_count],
        bc_taps[tap_count],
        tails[0],
        tails[1] * decay_rate,
        tails[2],
        grad_gate_gain,
        grad_out,
    )


def solution(mesh):
    in_specs = (
        P(None, "seq", None),
        P(),
        P(),
        P(None, None, "head"),
        P(),
        P(None, "head"),
        P(None, "head"),
        P("head"),
        P(),
        P(),
        P("head"),
        P("head"),
        P("head"),
        P("head"),
        P("head", None),
        P(None, "seq", None),
    )
    out_specs = (
        P(None, "seq", None),
        P(None, "seq", None),
        P(),
        P(None, None, "head"),
        P(None, "head"),
        P(None, "head"),
        P(None, "head"),
        P("head"),
        P(),
        P(),
        P("head"),
        P("head"),
        P("head"),
        P("head"),
        P("head", None),
    )
    return jax.shard_map(local, mesh=mesh, in_specs=in_specs, out_specs=out_specs, check_vma=False)
```
